32 devices in a mesh: rows: 2 (over core), blk: 16 (over z, y, x).
Axes of the slice: x: 2, y: 2, z: 4, core: 2. Of those that a mesh axis runs over, the one named last changes fastest.
Arguments:
- inputs: bfloat16 [2, 2, 2048, 768], P(None, 'rows', 'blk'), may hold values from -6 to 6
- doc_lengths: int32 [2, 2, 6], P(None, 'rows'), may hold values from 1 to 2043, as said below
- attn_gain: bfloat16 [768], P(('rows', 'blk')), may hold values from 0.25 to 1.75
- w_query: bfloat16 [768, 768], P(('rows', 'blk')), may hold values from -0.0546875 to 0.0546875
- w_key: bfloat16 [768, 768], P(('rows', 'blk')), may hold values from -0.21875 to 0.21875
- w_value: bfloat16 [768, 768], P(('rows', 'blk')), may hold values from -0.21875 to 0.21875
- w_out: bfloat16 [768, 768], P(None, ('rows', 'blk')), may hold values from -1.25 to 1.25
- ff_gain: bfloat16 [768], P(('rows', 'blk')), may hold values from 0.25 to 1.75
- w_gate: bfloat16 [768, 2048], P(('rows', 'blk')), may hold values from -0.21875 to 0.21875
- w_up: bfloat16 [768, 2048], P(('rows', 'blk')), may hold values from -0.21875 to 0.21875
- w_down: bfloat16 [2048, 768], P(None, ('rows', 'blk')), may hold values from -0.125 to 0.125
- rel_table: bfloat16 [32, 12], replicated, may hold values from -4 to 4
- cotangent: bfloat16 [2, 2, 2048, 768], P(None, 'rows', 'blk'), may hold values from -6 to 6
Outputs:
- output: bfloat16 [2, 2, 2048, 768], P(None, 'rows', 'blk')
- input_grad: float32 [2, 2, 2048, 768], P(None, 'rows', 'blk')
- attn_gain_grad: float32 [768], P(('rows', 'blk'))
- query_grad: float32 [768, 768], P(('rows', 'blk'))
- key_grad: float32 [768, 768], P(('rows', 'blk'))
- value_grad: float32 [768, 768], P(('rows', 'blk'))
- out_grad: float32 [768, 768], P(None, ('rows', 'blk'))
- ff_gain_grad: float32 [768], P(('rows', 'blk'))
- gate_grad: float32 [768, 2048], P(('rows', 'blk'))
- up_grad: float32 [768, 2048], P(('rows', 'blk'))
- down_grad: float32 [2048, 768], P(None, ('rows', 'blk'))
- table_grad: float32 [32, 12], replicated
The draws below stay inside these ranges and needn't reach their ends.
Inputs may be any that keep to these rules, and one draw needn't show every extreme that they name: `doc_lengths`: in every row the 6 pieces sum to 2048. The last piece is padding. One of the other pieces, drawn for each row, starts within the row's first 128 positions and ends within its last 128; every other piece is at most 21 long.
All inputs are finite; a program needn't handle non-finite values.
Results may differ from the reference program's by a relative error of at most 0.02.
Values may be sent and summed in bfloat16 or wider, within the bound.
No kernel may reach another device: no remote copies, remote signals or barrier semaphores. Data moves between devices by JAX's collectives and lax.ppermute only.
A program may use at most 256 MiB of HBM per device.

```python
import jax
import jax.numpy as jnp
from jax import lax

D = 768
HEADS = 12
HEAD_DIM = 64
FF = 2048
BUCKETS = 32
TOK_DEV = 128
MB = 2
DOCS = 6
ROWS = 2
SEQ = 2048
HD = 768


def draw_doc_lengths(key, part):
    key = jax.random.fold_in(key, 11)
    short_most = max(1, TOK_DEV // DOCS)
    key_short, key_long = jax.random.split(key)
    long_index = jax.random.randint(key_long, (MB, ROWS, 1), 0, DOCS - 1)
    which = lax.broadcasted_iota(jnp.int32, (MB, ROWS, DOCS), 2) == long_index
    pieces = jax.random.randint(key_short, (MB, ROWS, DOCS), 1, short_most + 1)
    first_row = (lax.broadcasted_iota(jnp.int32, (MB, ROWS, DOCS), 0) == 0) & (lax.broadcasted_iota(jnp.int32, (MB, ROWS, DOCS), 1) == 0)
    pieces = jnp.where(first_row, 1, pieces)
    smallest = jnp.min(jnp.where(which, short_most + 1, pieces), axis=-1, keepdims=True)
    pieces = pieces - (smallest - 1)
    others = jnp.sum(jnp.where(which, 0, pieces), axis=-1, keepdims=True)
    return jnp.where(which, SEQ - others, pieces).astype(jnp.int32)


def block_scale(own_key, shape, cuts, least, high):
    level, own = 1.0, jax.random.fold_in(own_key, 6)
    for dim, parts in cuts:
        steps = jnp.exp(jax.random.uniform(jax.random.fold_in(own, dim), (parts,), jnp.float32, least / len(cuts), high / len(cuts)))
        level = level * jnp.repeat(steps, shape[dim] // parts).reshape([-1 if axis == dim else 1 for axis in range(len(shape))])
    return level


def gaussian(own_key, extent, width, reach, shards=(), kind=jnp.bfloat16):
    level = block_scale(own_key, extent, shards, -0.22, 0.18) if shards else 1.0
    entries = jax.random.normal(own_key, extent, jnp.float32) * width * level
    return jnp.minimum(jnp.maximum(entries, -reach), reach).astype(kind)


def setup_inputs(seed: int = 0) -> dict:
    key_of = jax.random.split(jax.random.key(seed), 14)
    inputs = gaussian(key_of[0], (MB, ROWS, SEQ, D), 1.0, 6.0, ((1, 2), (2, 16)))
    doc_lengths = draw_doc_lengths(jax.random.fold_in(key_of[13], 71), 0)
    attn_gain = jnp.clip(1.0 + 0.15 * jax.random.normal(key_of[2], (D,), jnp.float32), 0.25, 1.75).astype(jnp.bfloat16)
    w_query = gaussian(key_of[3], (D, HD), (D * HEAD_DIM // 4) ** -0.5, 0.0546875, ((0, 32),))
    w_key = gaussian(key_of[4], (D, HD), D ** -0.5, 0.21875, ((0, 32),))
    w_value = gaussian(key_of[5], (D, HD), D ** -0.5, 0.21875, ((0, 32),))
    w_out = gaussian(key_of[6], (HD, D), (max(1, 64 * D // SEQ)) ** -0.5, 1.25, ((1, 32),))
    ff_gain = jnp.clip(1.0 + 0.15 * jax.random.normal(key_of[7], (D,), jnp.float32), 0.25, 1.75).astype(jnp.bfloat16)
    w_gate = gaussian(key_of[8], (D, FF), D ** -0.5, 0.21875, ((0, 32),))
    w_up = gaussian(key_of[9], (D, FF), D ** -0.5, 0.21875, ((0, 32),))
    w_down = gaussian(key_of[10], (FF, D), FF ** -0.5, 0.125, ((1, 32),))
    rel_table = gaussian(key_of[11], (BUCKETS, HEADS), 1.0, 4.0)
    cotangent = gaussian(key_of[12], (MB, ROWS, SEQ, D), 1.0, 6.0, ((1, 2), (2, 16)))
    return dict(inputs=inputs, doc_lengths=doc_lengths, attn_gain=attn_gain, w_query=w_query, w_key=w_key, w_value=w_value, w_out=w_out, ff_gain=ff_gain, w_gate=w_gate, w_up=w_up, w_down=w_down, rel_table=rel_table, cotangent=cotangent)


@jax.custom_vjp
def low(v):
    return lax.optimization_barrier(v.astype(jnp.bfloat16)).astype(jnp.float32)

@jax.custom_vjp
def low_back(v):
    return v

def low_keep(v):
    return (low(v), None)

def low_pass(kept, grad):
    return (grad,)

def back_keep(v):
    return (v, None)

def back_low(kept, grad):
    return (low(grad),)
low.defvjp(low_keep, low_pass)
low_back.defvjp(back_keep, back_low)
bucket_edges = (12, 16, 23, 32, 46, 64, 91)
norm_eps = 1e-06
masked_score = -1e+30

def bucket_of(relative, total_buckets):
    half = total_buckets // 2
    exact = half // 2
    distance = jnp.abs(relative)
    far_bucket = exact + sum(((distance >= edge).astype(jnp.int32) for edge in bucket_edges))
    return (jnp.where(relative > 0, half, 0) + jnp.where(distance < exact, distance, far_bucket)).astype(jnp.int32)

def segments_at(lengths_row, positions):
    bounds = jnp.cumsum(lengths_row).astype(jnp.int32)
    return lax.optimization_barrier(jnp.sum((positions[:, None] >= bounds[None, :]).astype(jnp.int32), axis=1))

def rms_norm(hidden, gain):
    return hidden * lax.rsqrt(lax.optimization_barrier(jnp.mean(hidden * hidden, axis=-1, keepdims=True)) + norm_eps) * gain

def reference(inputs, doc_lengths, attn_gain, w_query, w_key, w_value, w_out, ff_gain, w_gate, w_up, w_down, rel_table, cotangent):
    highest = lax.Precision.HIGHEST
    rows_all = MB * ROWS
    flat_inputs = inputs.reshape(rows_all, SEQ, D).astype(jnp.float32)
    flat_cot = cotangent.reshape(rows_all, SEQ, D).astype(jnp.float32)
    positions = jnp.arange(SEQ, dtype=jnp.int32)
    segments = jax.vmap(lambda lengths_row: segments_at(lengths_row, positions))(doc_lengths.reshape(rows_all, DOCS))
    params = tuple((weight.astype(jnp.float32) for weight in (attn_gain, w_query, w_key, w_value, w_out, ff_gain, w_gate, w_up, w_down, rel_table)))
    block = 512 if SEQ % 512 == 0 else SEQ

    def matmul(left, right):
        return jnp.dot(left, right, precision=highest, preferred_element_type=jnp.float32)

    def forward(flat, gain_attn, weight_query, weight_key, weight_value, weight_out, gain_ff, weight_gate, weight_up, weight_down, table):

        def one_row(item):
            row, seg = item
            normed = low(rms_norm(row, gain_attn))
            queries = low_back(low(matmul(normed, weight_query))).reshape(SEQ, HEADS, HEAD_DIM)
            keys = low_back(low(matmul(normed, weight_key))).reshape(SEQ, HEADS, HEAD_DIM)
            values = low_back(low(matmul(normed, weight_value))).reshape(SEQ, HEADS, HEAD_DIM)

            def one_block(index):
                start = index * block
                query_blk = lax.dynamic_slice_in_dim(queries, start, block, 0)
                query_pos = start + jnp.arange(block, dtype=jnp.int32)
                query_seg = lax.dynamic_slice_in_dim(seg, start, block, 0)
                raw = jnp.einsum('ihd,jhd->ihj', query_blk, keys, precision=highest)
                bucket = bucket_of(positions[None, :] - query_pos[:, None], BUCKETS)
                bias = jnp.transpose(table[bucket], (0, 2, 1))
                scores = low_back(raw + bias)
                allowed = (query_seg[:, None] == seg[None, :])[:, None, :]
                scores = jnp.where(allowed, scores, masked_score)
                top = lax.optimization_barrier(jnp.max(scores, axis=-1, keepdims=True))
                expo = jnp.exp(scores - top)
                probs = expo / lax.optimization_barrier(jnp.sum(expo, axis=-1, keepdims=True))
                return jnp.einsum('ihj,jhd->ihd', low(probs), values, precision=highest)
            context = lax.map(jax.checkpoint(one_block), jnp.arange(SEQ // block, dtype=jnp.int32))
            context = low_back(low(context.reshape(SEQ, HEADS * HEAD_DIM)))
            mid = row + low_back(matmul(context, weight_out))
            normed_ff = low(rms_norm(mid, gain_ff))
            gate = low_back(matmul(normed_ff, weight_gate))
            up = low_back(matmul(normed_ff, weight_up))
            inner = low(jax.nn.gelu(gate, approximate=True) * up)
            return mid + low_back(matmul(inner, weight_down))
        return lax.map(jax.checkpoint(one_row), (flat, segments))
    result, pullback = jax.vjp(forward, flat_inputs, *params)
    grads = pullback(flat_cot)
    output = result.astype(jnp.bfloat16).reshape(MB, ROWS, SEQ, D)
    input_grad = grads[0].reshape(MB, ROWS, SEQ, D)
    return (output, input_grad, grads[1], grads[2], grads[3], grads[4], grads[5], grads[6], grads[7], grads[8], grads[9], grads[10])
```

```python
import functools

import jax
import jax.numpy as jnp
from jax import lax
from jax.experimental import pallas as pl
from jax.experimental.pallas import tpu as pltpu
from jax.sharding import PartitionSpec as P

bucket_edges = (12, 16, 23, 32, 46, 64, 91)
norm_eps = 1e-06
masked_score = -1e30
f32 = jnp.float32
bf16 = jnp.bfloat16
both = ("rows", "blk")
chunk = 256
vmem_bytes = 56 * 1024 * 1024


def bucket_of(relative, total_buckets):
    half = total_buckets // 2
    exact = half // 2
    distance = jnp.abs(relative)
    far_bucket = exact + sum(((distance >= edge).astype(jnp.int32) for edge in bucket_edges))
    return jnp.where(relative > 0, half, 0) + jnp.where(distance < exact, distance, far_bucket)


def rms_norm(hidden, gain):
    return hidden * lax.rsqrt(jnp.mean(hidden * hidden, axis=-1, keepdims=True) + norm_eps) * gain


def gated(gate, up):
    return jax.nn.gelu(gate, approximate=True) * up


def dot_on(left, right, left_dim, right_dim):
    return lax.dot_general(
        left, right, (((left_dim,), (right_dim,)), ((), ())), preferred_element_type=f32
    )


def flip(array, axis, bit):
    count = lax.axis_size(axis)
    return lax.ppermute(array, axis, [(i, i ^ bit) for i in range(count)])


def bits_of(count):
    return [1 << k for k in range(count.bit_length() - 1)]


def segments_at(bounds, positions):
    total = jnp.zeros(positions.shape, jnp.int32)
    for bound in bounds:
        total = total + (positions >= bound).astype(jnp.int32)
    return total


def gather_steps(shard, order):
    blocks = lax.axis_size("blk")
    bits = bits_of(blocks)
    spots = len(bits)
    me = lax.axis_index("blk")
    held = shard.reshape((1,) * spots + shard.shape)
    for bit in order:
        dim = spots - 1 - bits.index(bit)
        other = flip(held, "blk", bit)
        high = (me & bit) != 0
        held = jnp.where(
            high, jnp.concatenate([other, held], dim), jnp.concatenate([held, other], dim)
        )
    held = held.reshape((1, blocks) + shard.shape)
    rows = lax.axis_size("rows")
    mine = lax.axis_index("rows")
    held = held.reshape((1,) * len(bits_of(rows)) + (blocks,) + shard.shape)
    for k, bit in enumerate(bits_of(rows)):
        dim = len(bits_of(rows)) - 1 - k
        other = flip(held, "rows", bit)
        high = (mine & bit) != 0
        held = jnp.where(
            high, jnp.concatenate([other, held], dim), jnp.concatenate([held, other], dim)
        )
    return held.reshape((rows * blocks * shard.shape[0],) + shard.shape[1:])


def scatter_steps(total, order):
    blocks = lax.axis_size("blk")
    rows = lax.axis_size("rows")
    bits = bits_of(blocks)
    spots = len(bits)
    row_bits = bits_of(rows)
    share = total.shape[0] // (rows * blocks)
    held = total.reshape((2,) * (len(row_bits) + spots) + (share,) + total.shape[1:])

    def halve(held, axis, bit, dim):
        high = (lax.axis_index(axis) & bit) != 0
        low_half = lax.slice_in_dim(held, 0, 1, axis=dim)
        high_half = lax.slice_in_dim(held, 1, 2, axis=dim)
        keep = jnp.where(high, high_half, low_half)
        send = jnp.where(high, low_half, high_half)
        return keep + flip(send, axis, bit)

    for k, bit in enumerate(row_bits):
        held = halve(held, "rows", bit, len(row_bits) - 1 - k)
    for bit in order:
        held = halve(held, "blk", bit, len(row_bits) + spots - 1 - bits.index(bit))
    return held.reshape((share,) + total.shape[1:])


def gather_orders(blocks):
    bits = bits_of(blocks)
    high = bits[2:]
    return (high + [bits[0], bits[1]], high + [bits[1], bits[0]])


def tile_rows(ref, index, start, stop):
    return jnp.concatenate(
        [ref[2 * index, start:stop, :], ref[2 * index + 1, start:stop, :]], axis=1
    )


def attend_kernel(
    size, blocks, docs, bounds_ref, table_ref, taken_ref, band_ref,
    sent_ref, context_ref, expo_ref, scale_ref, keys_ref, query_ref, score_ref,
):
    micro_index, block = pl.program_id(0), pl.program_id(1)
    chunks = blocks // 2
    tok = chunk // 2
    bounds = [bounds_ref[micro_index, d] for d in range(docs)]

    @pl.when(block == 0)
    def _():
        for s in range(blocks):
            position = s * tok + lax.broadcasted_iota(jnp.int32, (1, tok), 1)
            segment = segments_at(bounds, position)
            row = lax.broadcasted_iota(jnp.int32, (16, tok), 0)
            own = jnp.where(row == segment, 1.0, 0.0)
            part = jnp.where(row == s // 2, 1.0, 0.0)
            tall = jnp.concatenate(
                [
                    taken_ref[s, size : 2 * size, :].astype(f32),
                    own,
                    part,
                    jnp.zeros((2 * size - size - 32, tok), f32),
                ],
                axis=0,
            )
            keys_ref[s * tok : (s + 1) * tok, :] = tall.T.astype(bf16)
        query_ref[size:, :] = jnp.zeros((size, chunk), bf16)

    position = block * chunk + lax.broadcasted_iota(jnp.int32, (1, chunk), 1)
    segment = segments_at(bounds, position)
    row = lax.broadcasted_iota(jnp.int32, (16, chunk), 0)
    query_ref[:size, :] = tile_rows(taken_ref, block, 0, size)
    query_ref[size : size + 16, :] = jnp.where(row == segment, 0.0, masked_score).astype(bf16)
    far = jnp.where(
        row <= block - 2, table_ref[0], jnp.where(row >= block + 2, table_ref[1], 0.0)
    )
    query_ref[size + 16 : size + 32, :] = far.astype(bf16)
    query = query_ref[...]
    top = jnp.full((8, chunk), masked_score, f32)
    for c in range(chunks):
        scores = jnp.dot(
            keys_ref[c * chunk : (c + 1) * chunk, :], query, preferred_element_type=f32
        )
        score_ref[c * chunk : (c + 1) * chunk, :] = scores
        top = jnp.maximum(top, jnp.max(scores.reshape(chunk // 8, 8, chunk), axis=0))
    for j in (-1, 0, 1):

        @pl.when((block + j >= 0) & (block + j < chunks))
        def _():
            spot = pl.ds(pl.multiple_of((block + j) * chunk, chunk), chunk)
            score_ref[spot, :] = score_ref[spot, :] + band_ref[j + 1]

    top = jnp.max(top, axis=0, keepdims=True) + table_ref[2]
    total = jnp.zeros((8, chunk), f32)
    context = jnp.zeros((size, chunk), f32)
    for c in range(chunks):
        expo = jnp.exp(score_ref[c * chunk : (c + 1) * chunk, :] - top)
        total = total + jnp.sum(expo.reshape(chunk // 8, 8, chunk), axis=0)
        low = expo.astype(bf16)
        expo_ref[c * chunk : (c + 1) * chunk, :] = low
        context = context + jnp.dot(
            tile_rows(taken_ref, c, 2 * size, 3 * size), low, preferred_element_type=f32
        )
    scale = 1.0 / jnp.sum(total, axis=0, keepdims=True)
    context = context * scale
    context_ref[...] = context
    scale_ref[...] = scale
    sent_ref[0] = context[:, :tok].astype(bf16)
    sent_ref[1] = context[:, tok:].astype(bf16)


def attend(taken, bounds, scalars, band, blocks, micro, size):
    length = blocks * taken.shape[2] // micro
    tok = length // blocks
    smem = pl.BlockSpec(memory_space=pltpu.SMEM)
    return pl.pallas_call(
        functools.partial(attend_kernel, size, blocks, bounds.shape[1]),
        grid=(micro, blocks // 2),
        in_specs=[
            smem,
            smem,
            pl.BlockSpec((blocks, 3 * size, tok), lambda m, q: (0, 0, m)),
            pl.BlockSpec((3, chunk, chunk), lambda m, q: (0, 0, 0)),
        ],
        out_specs=[
            pl.BlockSpec((2, size, tok), lambda m, q: (q, 0, m)),
            pl.BlockSpec((None, size, chunk), lambda m, q: (m, 0, q)),
            pl.BlockSpec((None, length, chunk), lambda m, q: (m, 0, q)),
            pl.BlockSpec((None, 1, chunk), lambda m, q: (m, 0, q)),
        ],
        out_shape=[
            jax.ShapeDtypeStruct((blocks, size, micro * tok), bf16),
            jax.ShapeDtypeStruct((micro, size, length), f32),
            jax.ShapeDtypeStruct((micro, length, length), bf16),
            jax.ShapeDtypeStruct((micro, 1, length), f32),
        ],
        scratch_shapes=[
            pltpu.VMEM((length, 2 * size), bf16),
            pltpu.VMEM((2 * size, chunk), bf16),
            pltpu.VMEM((length, chunk), f32),
        ],
        compiler_params=pltpu.CompilerParams(vmem_limit_bytes=vmem_bytes),
        name="attend",
    )(bounds, scalars, taken, band)


def attend_back_kernel(
    size, blocks, taken_ref, grad_ref, context_ref, expo_ref, scale_ref,
    sent_ref, band_ref, far_ref,
    queries_ref, tall_ref, wide_ref, delta_ref, grad_queries_ref, grad_scores_ref,
):
    micro_index, c = pl.program_id(0), pl.program_id(1)
    chunks = blocks // 2
    tok = chunk // 2
    length = blocks * tok

    @pl.when(c == 0)
    def _():
        for s in range(blocks):
            spot = slice(s * tok, (s + 1) * tok)
            scaled = grad_ref[s].astype(f32) * scale_ref[:, spot]
            wide_ref[:, spot] = scaled.astype(bf16)
            tall_ref[spot, :] = scaled.T.astype(bf16)
            delta_ref[:, spot] = jnp.sum(scaled * context_ref[:, spot], axis=0, keepdims=True)
            queries_ref[spot, :] = taken_ref[s, :size, :].astype(f32).T.astype(bf16)
        grad_queries_ref[...] = jnp.zeros_like(grad_queries_ref)

    @pl.when((c == 0) & (micro_index == 0))
    def _():
        band_ref[...] = jnp.zeros_like(band_ref)
        far_ref[...] = jnp.zeros_like(far_ref)

    values = tile_rows(taken_ref, c, 2 * size, 3 * size).astype(f32).T.astype(bf16)
    for q in range(chunks):
        spot = slice(q * chunk, (q + 1) * chunk)
        grad_weights = jnp.dot(values, wide_ref[:, spot], preferred_element_type=f32)
        weights = expo_ref[:, spot].astype(f32)
        grad_scores_ref[:, spot] = (weights * (grad_weights - delta_ref[:, spot])).astype(bf16)
    grad_values = jnp.dot(expo_ref[...], tall_ref[...], preferred_element_type=f32).T.astype(bf16)
    grad_keys = jnp.dot(
        grad_scores_ref[...], queries_ref[...], preferred_element_type=f32
    ).T.astype(bf16)
    for t in range(2):
        sent_ref[2 * c + t, size : 2 * size, :] = grad_keys[:, t * tok : (t + 1) * tok]
        sent_ref[2 * c + t, 2 * size :, :] = grad_values[:, t * tok : (t + 1) * tok]
    keys = jnp.concatenate(
        [tile_rows(taken_ref, c, size, 2 * size), jnp.ones((16, chunk), bf16)], axis=0
    )
    for q in range(chunks):
        spot = slice(q * chunk, (q + 1) * chunk)
        part = jnp.dot(keys, grad_scores_ref[:, spot], preferred_element_type=f32)
        grad_queries_ref[:, spot] = grad_queries_ref[:, spot] + part[:size]
        sums = part[size : size + 8]
        far_ref[0, :, spot] = far_ref[0, :, spot] + jnp.where(c <= q - 2, sums, 0.0)
        far_ref[1, :, spot] = far_ref[1, :, spot] + jnp.where(c >= q + 2, sums, 0.0)
    for j in (-1, 0, 1):

        @pl.when((c - j >= 0) & (c - j < chunks))
        def _():
            spot = pl.ds(pl.multiple_of((c - j) * chunk, chunk), chunk)
            band_ref[j + 1] = band_ref[j + 1] + grad_scores_ref[:, spot].astype(f32)

    @pl.when(c == chunks - 1)
    def _():
        for s in range(blocks):
            sent_ref[s, :size, :] = grad_queries_ref[:, s * tok : (s + 1) * tok].astype(bf16)


def attend_back(taken, grads, context, expo, scale, blocks, micro, size):
    length = expo.shape[1]
    tok = length // blocks
    return pl.pallas_call(
        functools.partial(attend_back_kernel, size, blocks),
        grid=(micro, blocks // 2),
        in_specs=[
            pl.BlockSpec((blocks, 3 * size, tok), lambda m, c: (0, 0, m)),
            pl.BlockSpec((blocks, size, tok), lambda m, c: (0, 0, m)),
            pl.BlockSpec((None, size, length), lambda m, c: (m, 0, 0)),
            pl.BlockSpec((None, chunk, length), lambda m, c: (m, c, 0)),
            pl.BlockSpec((None, 1, length), lambda m, c: (m, 0, 0)),
        ],
        out_specs=[
            pl.BlockSpec((blocks, 3 * size, tok), lambda m, c: (0, 0, m)),
            pl.BlockSpec((3, chunk, chunk), lambda m, c: (0, 0, 0)),
            pl.BlockSpec((2, 8, length), lambda m, c: (0, 0, 0)),
        ],
        out_shape=[
            jax.ShapeDtypeStruct((blocks, 3 * size, micro * tok), bf16),
            jax.ShapeDtypeStruct((3, chunk, chunk), f32),
            jax.ShapeDtypeStruct((2, 8, length), f32),
        ],
        scratch_shapes=[
            pltpu.VMEM((length, size), bf16),
            pltpu.VMEM((length, size), bf16),
            pltpu.VMEM((size, length), bf16),
            pltpu.VMEM((1, length), f32),
            pltpu.VMEM((size, length), f32),
            pltpu.VMEM((chunk, length), bf16),
        ],
        compiler_params=pltpu.CompilerParams(vmem_limit_bytes=vmem_bytes),
        name="attend_back",
    )(taken, grads, context, expo, scale)


def body(
    inputs, doc_lengths, attn_gain, w_query, w_key, w_value, w_out, ff_gain,
    w_gate, w_up, w_down, rel_table, cotangent,
):
    micro, _, tok, width = inputs.shape
    inner_width = w_query.shape[1]
    hidden_units = w_gate.shape[1]
    buckets, heads = rel_table.shape
    size = inner_width // heads
    blocks = lax.axis_size("blk")
    rows = lax.axis_size("rows")
    me = lax.axis_index("blk")
    share = w_query.shape[0]
    here = micro * tok
    orders = gather_orders(blocks)

    with jax.named_scope("weights"):
        grouped = jnp.concatenate(
            [w.reshape(share, heads, size) for w in (w_query, w_key, w_value)], axis=2
        ).reshape(share, 3 * inner_width)
        front = jnp.concatenate(
            [
                grouped,
                attn_gain[:, None],
                ff_gain[:, None],
                jnp.zeros((share, 254), bf16),
            ],
            axis=1,
        )
        half = front.shape[1] // 2
        front_full = jnp.concatenate(
            [gather_steps(front[:, :half], orders[0]), gather_steps(front[:, half:], orders[1])],
            axis=1,
        )
        back = jnp.concatenate([w_out.T, w_gate, w_up, w_down.T], axis=1)
        back_full = lax.all_gather(back, both, axis=0, tiled=True)
        qkv_full = front_full[:, : 3 * inner_width]
        gain_a = front_full[:, 3 * inner_width].astype(f32)
        gain_f = front_full[:, 3 * inner_width + 1].astype(f32)
        out_t = back_full[:, :inner_width]
        gate_full = back_full[:, inner_width : inner_width + hidden_units]
        up_full = back_full[:, inner_width + hidden_units : inner_width + 2 * hidden_units]
        down_t = back_full[:, inner_width + 2 * hidden_units :]

    with jax.named_scope("bias"):
        head = jnp.minimum(me, heads - 1)
        column = lax.dynamic_slice_in_dim(rel_table, head, 1, axis=1)[:, 0].astype(f32)
        shape = (3, chunk, chunk)
        relative = (
            lax.broadcasted_iota(jnp.int32, shape, 1)
            - lax.broadcasted_iota(jnp.int32, shape, 2)
            + (lax.broadcasted_iota(jnp.int32, shape, 0) - 1) * chunk
        )
        bucket = bucket_of(relative, buckets)
        band = jnp.zeros(shape, f32)
        for b in range(buckets):
            band = jnp.where(bucket == b, column[b], band)
        scalars = jnp.stack(
            [column[buckets // 2 - 1], column[buckets - 1], jnp.maximum(jnp.max(column), 0.0)]
        )
        bounds = jnp.cumsum(doc_lengths[:, 0], axis=1).astype(jnp.int32)

    with jax.named_scope("project"):
        hidden = inputs.reshape(here, width).astype(f32)
        normed_a = rms_norm(hidden, gain_a).astype(bf16)
        qkv = dot_on(qkv_full, normed_a, 0, 1).astype(bf16)
        qkv = jnp.pad(qkv, ((0, (blocks - heads) * 3 * size), (0, 0)))
        qkv = qkv.reshape(blocks, 3 * size, here)
        taken = lax.all_to_all(qkv, "blk", 0, 0, tiled=True)

    sent, context, expo, scale = attend(taken, bounds, scalars, band, blocks, micro, size)
    with jax.named_scope("context"):
        context_t = lax.all_to_all(sent, "blk", 0, 0, tiled=True)
        context_t = context_t.reshape(blocks * size, here)[:inner_width]

    with jax.named_scope("forward"):
        mid = hidden + dot_on(context_t, out_t, 0, 1)
        normed_f = rms_norm(mid, gain_f).astype(bf16)
        gate = jnp.dot(normed_f, gate_full, preferred_element_type=f32)
        up = jnp.dot(normed_f, up_full, preferred_element_type=f32)
        inner = gated(gate, up).astype(bf16)
        result = (mid + dot_on(inner, down_t, 1, 1)).astype(bf16)

    with jax.named_scope("backward"):
        grad_out_b = cotangent.reshape(here, width)
        grad_out = grad_out_b.astype(f32)
        down_grad = dot_on(grad_out_b, inner, 0, 0)
        grad_inner = jnp.dot(grad_out_b, down_t, preferred_element_type=f32)
        _, gated_pullback = jax.vjp(gated, gate, up)
        grad_gate, grad_up = gated_pullback(grad_inner)
        grad_gate_b = grad_gate.astype(bf16)
        grad_up_b = grad_up.astype(bf16)
        gate_grad = dot_on(normed_f, grad_gate_b, 0, 0)
        up_grad = dot_on(normed_f, grad_up_b, 0, 0)
        grad_normed_f = dot_on(grad_gate_b, gate_full, 1, 1) + dot_on(grad_up_b, up_full, 1, 1)
        _, norm_pullback = jax.vjp(rms_norm, mid, gain_f)
        grad_mid_norm, grad_gain_f = norm_pullback(grad_normed_f)
        grad_mid = grad_out + grad_mid_norm
        grad_branch = grad_mid.astype(bf16)
        out_grad = dot_on(grad_branch, context_t, 0, 1)
        grad_context = dot_on(out_t, grad_branch, 0, 1).astype(bf16)
        grad_context = jnp.pad(grad_context, ((0, (blocks - heads) * size), (0, 0)))
        grad_context = grad_context.reshape(blocks, size, here)
        grads = lax.all_to_all(grad_context, "blk", 0, 0, tiled=True)

    with jax.named_scope("back_grads"):
        back_sum = jnp.concatenate([out_grad, gate_grad, up_grad, down_grad], axis=1).astype(bf16)
        back_grad = lax.psum_scatter(back_sum, both, scatter_dimension=0, tiled=True).astype(f32)

    returned, band_grad, far_grad = attend_back(
        taken, grads, context, expo, scale, blocks, micro, size
    )
    with jax.named_scope("table"):
        sums = [jnp.sum(jnp.where(bucket == b, band_grad, 0.0)) for b in range(buckets)]
        sums[buckets // 2 - 1] = sums[buckets // 2 - 1] + jnp.sum(far_grad[0, 0])
        sums[buckets - 1] = sums[buckets - 1] + jnp.sum(far_grad[1, 0])
        mine = lax.broadcasted_iota(jnp.int32, (buckets, heads), 1) == me
        table_grad = lax.psum(jnp.where(mine, jnp.stack(sums)[:, None], 0.0), both)

    with jax.named_scope("input"):
        grad_qkv = lax.all_to_all(returned, "blk", 0, 0, tiled=True)
        grad_qkv = grad_qkv.reshape(blocks * 3 * size, here)[: 3 * inner_width]
        front_sum = dot_on(normed_a, grad_qkv, 0, 1)
        grad_normed_a = dot_on(grad_qkv, qkv_full, 0, 1)
        _, first_pullback = jax.vjp(rms_norm, hidden, gain_a)
        grad_hidden_norm, grad_gain_a = first_pullback(grad_normed_a)
        input_grad = grad_mid + grad_hidden_norm

    with jax.named_scope("front_grads"):
        front_sum = jnp.concatenate(
            [
                front_sum,
                grad_gain_a[:, None],
                grad_gain_f[:, None],
                jnp.zeros((width, 254), f32),
            ],
            axis=1,
        ).astype(bf16)
        half = front_sum.shape[1] // 2
        front_grad = jnp.concatenate(
            [
                scatter_steps(front_sum[:, :half], orders[0][::-1]),
                scatter_steps(front_sum[:, half:], orders[1][::-1]),
            ],
            axis=1,
        ).astype(f32)
        parts = front_grad[:, : 3 * inner_width].reshape(share, heads, 3, size)
        query_grad, key_grad, value_grad = (
            parts[:, :, k].reshape(share, inner_width) for k in range(3)
        )
        cut = inner_width + hidden_units

    return (
        result.reshape(micro, 1, tok, width),
        input_grad.reshape(micro, 1, tok, width),
        front_grad[:, 3 * inner_width],
        query_grad,
        key_grad,
        value_grad,
        back_grad[:, :inner_width].T,
        front_grad[:, 3 * inner_width + 1],
        back_grad[:, inner_width:cut],
        back_grad[:, cut : cut + hidden_units],
        back_grad[:, cut + hidden_units :].T,
        table_grad,
    )


def solution(mesh):
    weight_rows = P(both, None)
    weight_columns = P(None, both)
    tokens = P(None, "rows", "blk", None)
    in_specs = (
        tokens, P(None, "rows", None), P(both), weight_rows, weight_rows, weight_rows,
        weight_columns, P(both), weight_rows, weight_rows, weight_columns, P(), tokens,
    )
    out_specs = (
        tokens, tokens, P(both), weight_rows, weight_rows, weight_rows,
        weight_columns, P(both), weight_rows, weight_rows, weight_columns, P(),
    )
    return jax.shard_map(body, mesh=mesh, in_specs=in_specs, out_specs=out_specs, check_vma=False)
```

```python
import functools

import jax
import jax.numpy as jnp
import numpy as np
from jax import lax
from jax.experimental import pallas as pl
from jax.experimental.pallas import tpu as pltpu
from jax.sharding import PartitionSpec as P

bucket_edges = (12, 16, 23, 32, 46, 64, 91)
norm_eps = 1e-06
masked_score = -1e30
f32 = jnp.float32
bf16 = jnp.bfloat16
both = ("rows", "blk")
chunk = 256
vmem_bytes = 56 * 1024 * 1024


def bucket_of(relative, total_buckets):
    half = total_buckets // 2
    exact = half // 2
    distance = jnp.abs(relative)
    far_bucket = exact + sum(((distance >= edge).astype(jnp.int32) for edge in bucket_edges))
    return jnp.where(relative > 0, half, 0) + jnp.where(distance < exact, distance, far_bucket)


def rms_norm(hidden, gain):
    return hidden * lax.rsqrt(jnp.mean(hidden * hidden, axis=-1, keepdims=True) + norm_eps) * gain


def gated(gate, up):
    return jax.nn.gelu(gate, approximate=True) * up


def dot_on(left, right, left_dim, right_dim):
    return lax.dot_general(
        left, right, (((left_dim,), (right_dim,)), ((), ())), preferred_element_type=f32
    )


def flip(array, axis, bit):
    count = lax.axis_size(axis)
    return lax.ppermute(array, axis, [(i, i ^ bit) for i in range(count)])


def bits_of(count):
    return [1 << k for k in range(count.bit_length() - 1)]


def segments_at(bounds, positions):
    total = jnp.zeros(positions.shape, jnp.int32)
    for bound in bounds:
        total = total + (positions >= bound).astype(jnp.int32)
    return total


def groups_of(blocks):
    near = 4
    far = blocks // near
    across = [[f * near + n for f in range(far)] for n in range(near)]
    within = [[f * near + n for n in range(near)] for f in range(far)]
    return far, near, across, within


def staged(rows, blocks, share):
    return rows == 2 and blocks % 4 == 0 and share % 8 == 0


def stage_matrix(rows, blocks, share):
    place = np.arange(rows * blocks * share)
    taken = place
    if staged(rows, blocks, share):
        far, near, _, _ = groups_of(blocks)
        slab = place // share
        half, inner = slab // blocks, slab % blocks
        taken = (half * blocks + inner % far * near + inner // far) * share + place % share
    return jnp.asarray((place[:, None] == taken[None, :]).astype(np.float32), bf16)


def tie_kernel(*refs):
    pass


def tie(value, *after):
    space = pl.BlockSpec(memory_space=pl.ANY)
    return pl.pallas_call(
        tie_kernel,
        in_specs=[space] * (1 + len(after)),
        out_specs=space,
        out_shape=jax.ShapeDtypeStruct(value.shape, value.dtype),
        input_output_aliases={0: 0},
        name="tie",
    )(value, *after)


def exchange(array, groups):
    return lax.all_to_all(array, "blk", 0, 0, tiled=True, axis_index_groups=groups)


def halves_of_whole(whole):
    half = whole.shape[0] // 2
    return whole[:half], whole[half:]


def pack_kernel(query_ref, key_ref, value_ref, gain_a_ref, gain_f_ref, out_ref):
    share = query_ref.shape[0]
    spread = lax.broadcasted_iota(jnp.int32, (share, share), 0) == lax.broadcasted_iota(
        jnp.int32, (share, share), 1
    )
    lane = lax.broadcasted_iota(jnp.int32, (share, 128), 1)
    gains = jnp.zeros((share, 128), f32)
    for k, ref in enumerate((gain_a_ref, gain_f_ref)):
        column = jnp.where(spread, ref[...].astype(f32), 0.0)
        gains = jnp.where(lane == k, jnp.sum(column, axis=1, keepdims=True), gains)
    parts = [query_ref[...], key_ref[...], value_ref[...], gains.astype(bf16)]
    packed = jnp.concatenate(parts, axis=1)
    for copy in range(out_ref.shape[0]):
        out_ref[copy] = packed


def pack(query, key, value, gain_a, gain_f, copies):
    shape = (copies, query.shape[0], 3 * query.shape[1] + 128)
    return pl.pallas_call(
        pack_kernel,
        out_shape=jax.ShapeDtypeStruct(shape, bf16),
        compiler_params=pltpu.CompilerParams(vmem_limit_bytes=vmem_bytes),
        name="pack",
    )(query, key, value, gain_a[None, :], gain_f[None, :])


def gather_front(*parts):
    blocks, rows = lax.axis_size("blk"), lax.axis_size("rows")
    if not staged(rows, blocks, parts[0].shape[0]):
        shard = pack(*parts, 1)[0]
        return halves_of_whole(lax.all_gather(shard, both, axis=0, tiled=True))
    far, near, across, within = groups_of(blocks)
    packed = pack(*parts, far)
    first = exchange(packed.reshape(-1, packed.shape[2]), across)
    own = exchange(jnp.tile(first, (near, 1)), within)
    return own, flip(own, "rows", 1)


def gather_back(shard, after):
    blocks, rows = lax.axis_size("blk"), lax.axis_size("rows")
    if not staged(rows, blocks, shard.shape[0]):
        return lax.all_gather(shard, both, axis=0, tiled=True)
    far, near, across, within = groups_of(blocks)
    own = lax.all_gather(shard, "blk", axis=0, tiled=True, axis_index_groups=across)
    own = tie(own, after)
    return lax.all_gather(own, "blk", axis=0, tiled=True, axis_index_groups=within)


def gather_other(own, after):
    blocks, rows = lax.axis_size("blk"), lax.axis_size("rows")
    if not staged(rows, blocks, own.shape[0] // blocks):
        return halves_of_whole(own)
    own = tie(own, after)
    return own, flip(own, "rows", 1)


def scatter_front(own, share):
    far, near, _, within = groups_of(lax.axis_size("blk"))
    held = exchange(own, within).reshape(near, far * share, own.shape[1])
    return jnp.sum(held.astype(f32), axis=0).astype(bf16)


def scatter_front_end(held, share, *after):
    far, _, across, _ = groups_of(lax.axis_size("blk"))
    return exchange(tie(held, *after), across).reshape(far, share, held.shape[1])


def scatter_back(own):
    _, _, _, within = groups_of(lax.axis_size("blk"))
    return lax.psum_scatter(
        own, "blk", scatter_dimension=0, axis_index_groups=within, tiled=True
    )


def scatter_back_end(part, after):
    _, _, across, _ = groups_of(lax.axis_size("blk"))
    return lax.psum_scatter(
        tie(part, after), "blk", scatter_dimension=0, axis_index_groups=across, tiled=True
    )


def scatter_whole(own, other):
    whole = jnp.concatenate([own, other], axis=0)
    return lax.psum_scatter(whole, both, scatter_dimension=0, tiled=True)


def side(flipped, half):
    return (
        pl.ds(pl.multiple_of(flipped * half, half), half),
        pl.ds(pl.multiple_of((1 - flipped) * half, half), half),
    )


def cost(micros):
    return pl.CostEstimate(flops=int(micros * 1e9), bytes_accessed=0, transcendentals=0)


def tile_rows(ref, index, start, stop):
    return jnp.concatenate(
        [ref[2 * index, start:stop, :], ref[2 * index + 1, start:stop, :]], axis=1
    )


def steps_of(buckets):
    half = buckets // 2
    exact = half // 2
    lows = list(range(1, exact)) + [exact] + list(bucket_edges)
    places = [(1 - low, k) for k, low in reversed(list(enumerate(lows)))]
    return half - 1, places + [(low, half + 1 + k) for k, low in enumerate(lows)]


def relative_tile(j):
    shape = (chunk, chunk)
    return (
        lax.broadcasted_iota(jnp.int32, shape, 0)
        - lax.broadcasted_iota(jnp.int32, shape, 1)
        + j * chunk
    )


def bias_kernel(buckets, heads, head_ref, table_ref, band_ref):
    first, places = steps_of(buckets)
    value = lambda bucket: table_ref[bucket * heads + head_ref[0]]
    for j in (-1, 0, 1):
        relative = relative_tile(j)
        tile = jnp.full((chunk, chunk), value(first), f32)
        for place, bucket in places:
            tile = jnp.where(relative >= place, value(bucket), tile)
        band_ref[j + 1] = tile


def bias_tiles(head, table, buckets):
    smem = pl.BlockSpec(memory_space=pltpu.SMEM)
    return pl.pallas_call(
        functools.partial(bias_kernel, buckets, table.shape[0] // buckets),
        in_specs=[smem, smem],
        out_shape=jax.ShapeDtypeStruct((3, chunk, chunk), f32),
        compiler_params=pltpu.CompilerParams(vmem_limit_bytes=vmem_bytes),
        cost_estimate=cost(2),
        name="bias_tiles",
    )(head, table)


def table_pieces(buckets, band_ref, far_ref, sums_ref):
    first, places = steps_of(buckets)
    edge = chunk // 2
    reach = -(-bucket_edges[-1] // 8) * 8
    sums_ref[...] = jnp.zeros_like(sums_ref)
    relative = [relative_tile(j) for j in (-1, 0, 1)]

    def fold(tile):
        return jnp.sum(tile.reshape(-1, 8, tile.shape[1]), axis=0)

    above = fold(band_ref[0]) + fold(band_ref[1]) + fold(band_ref[2])
    for q in range(far_ref.shape[2] // chunk):
        spot = slice(q * chunk, (q + 1) * chunk)
        above = above + far_ref[0, :, spot] * 0.125 + far_ref[1, :, spot] * 0.125
    right = fold(band_ref[2])
    for q in range(far_ref.shape[2] // chunk):
        right = right + far_ref[1, :, q * chunk : (q + 1) * chunk] * 0.125
    corner = band_ref[2, :reach, edge:]
    corner_relative = relative[2][:reach, edge:]
    left_corner = band_ref[0, chunk - reach :, :edge]
    left_relative = relative[0][chunk - reach :, :edge]
    bucket = first
    for place, following in places:
        if place > 0:
            after = right[:, :edge] + right[:, edge:]
            after = after - fold(jnp.where(corner_relative < place, corner, 0.0))
        else:
            after = right[:, :edge] + right[:, edge:]
            after = after + fold(jnp.where(left_relative >= place, left_corner, 0.0))
        part = fold(jnp.where(relative[1] >= place, band_ref[1], 0.0))
        after = after + part[:, :edge] + part[:, edge:]
        if above.shape[1] == chunk:
            above = above[:, :edge] + above[:, edge:]
        sums_ref[bucket : bucket + 1, :] = jnp.sum(above - after, axis=0, keepdims=True)
        above, bucket = after, following
    sums_ref[bucket : bucket + 1, :] = jnp.sum(above, axis=0, keepdims=True)
    found = jnp.sum(sums_ref[...], axis=1, keepdims=True)
    shape = (buckets, edge)
    spread = lax.broadcasted_iota(jnp.int32, shape, 0) == lax.broadcasted_iota(jnp.int32, shape, 1)
    found = jnp.sum(jnp.where(spread, found, 0.0), axis=0, keepdims=True)
    high = found.astype(bf16).astype(f32)
    middle = (found - high).astype(bf16).astype(f32)
    pieces = [high, middle, found - high - middle, jnp.zeros((13, edge), f32)]
    return jnp.concatenate(pieces, axis=0).astype(bf16)


def attend_kernel(
    size, blocks, docs, buckets, bounds_ref, head_ref, table_ref, taken_ref, band_ref, *refs
):
    sent_ref, context_ref, expo_ref, scale_ref, keys_ref, query_ref, score_ref = refs[-7:]
    block = pl.program_id(0)
    chunks = blocks // 2
    tok = chunk // 2
    bounds = [bounds_ref[0]]
    for d in range(1, docs):
        bounds.append(bounds[-1] + bounds_ref[d])
    heads = table_ref.shape[0] // buckets
    entry = lambda bucket: table_ref[bucket * heads + head_ref[0]]
    highest = jnp.float32(0.0)
    for bucket in range(buckets):
        highest = jnp.maximum(highest, entry(bucket))

    @pl.when(block == 0)
    def _():
        for s in range(blocks):
            position = s * tok + lax.broadcasted_iota(jnp.int32, (1, tok), 1)
            segment = segments_at(bounds, position)
            row = lax.broadcasted_iota(jnp.int32, (16, tok), 0)
            own = jnp.where(row == segment, 1.0, 0.0)
            part = jnp.where(row == s // 2, 1.0, 0.0)
            tall = jnp.concatenate(
                [
                    taken_ref[s, size : 2 * size, :].astype(f32),
                    own,
                    part,
                    jnp.zeros((size - 32, tok), f32),
                ],
                axis=0,
            )
            keys_ref[s * tok : (s + 1) * tok, :] = tall.T.astype(bf16)
        query_ref[size:, :] = jnp.zeros((size, chunk), bf16)

    position = block * chunk + lax.broadcasted_iota(jnp.int32, (1, chunk), 1)
    segment = segments_at(bounds, position)
    row = lax.broadcasted_iota(jnp.int32, (16, chunk), 0)
    query_ref[:size, :] = tile_rows(taken_ref, block, 0, size)
    query_ref[size : size + 16, :] = jnp.where(row == segment, 0.0, masked_score).astype(bf16)
    far = jnp.where(
        row <= block - 2,
        entry(buckets // 2 - 1),
        jnp.where(row >= block + 2, entry(buckets - 1), 0.0),
    )
    query_ref[size + 16 : size + 32, :] = far.astype(bf16)
    query = query_ref[...]
    top = jnp.full((8, chunk), masked_score, f32)
    for c in range(chunks):
        scores = jnp.dot(
            keys_ref[c * chunk : (c + 1) * chunk, :], query, preferred_element_type=f32
        )
        score_ref[c * chunk : (c + 1) * chunk, :] = scores
        top = jnp.maximum(top, jnp.max(scores.reshape(chunk // 8, 8, chunk), axis=0))
    for j in (-1, 0, 1):

        @pl.when((block + j >= 0) & (block + j < chunks))
        def _():
            spot = pl.ds(pl.multiple_of((block + j) * chunk, chunk), chunk)
            score_ref[spot, :] = score_ref[spot, :] + band_ref[j + 1]

    top = jnp.max(top, axis=0, keepdims=True) + highest
    total = jnp.zeros((8, chunk), f32)
    context = jnp.zeros((size, chunk), f32)
    for c in range(chunks):
        expo = jnp.exp(score_ref[c * chunk : (c + 1) * chunk, :] - top)
        total = total + jnp.sum(expo.reshape(chunk // 8, 8, chunk), axis=0)
        low = expo.astype(bf16)
        expo_ref[c * chunk : (c + 1) * chunk, :] = low
        context = context + jnp.dot(
            tile_rows(taken_ref, c, 2 * size, 3 * size), low, preferred_element_type=f32
        )
    scale = 1.0 / jnp.sum(total, axis=0, keepdims=True)
    context = context * scale
    context_ref[...] = context
    scale_ref[...] = scale
    sent_ref[0] = context[:, :tok].astype(bf16)
    sent_ref[1] = context[:, tok:].astype(bf16)


def attend(taken, lengths, head, table, band, buckets, *after):
    blocks, size, tok = taken.shape
    size = size // 3
    length = blocks * tok
    smem = pl.BlockSpec(memory_space=pltpu.SMEM)
    return pl.pallas_call(
        functools.partial(attend_kernel, size, blocks, lengths.shape[0], buckets),
        grid=(blocks // 2,),
        in_specs=[
            smem,
            smem,
            smem,
            pl.BlockSpec((blocks, 3 * size, tok), lambda q: (0, 0, 0)),
            pl.BlockSpec((3, chunk, chunk), lambda q: (0, 0, 0)),
        ]
        + [pl.BlockSpec(memory_space=pl.ANY)] * len(after),
        out_specs=[
            pl.BlockSpec((2, size, tok), lambda q: (q, 0, 0)),
            pl.BlockSpec((size, chunk), lambda q: (0, q)),
            pl.BlockSpec((length, chunk), lambda q: (0, q)),
            pl.BlockSpec((1, chunk), lambda q: (0, q)),
        ],
        out_shape=[
            jax.ShapeDtypeStruct((blocks, size, tok), bf16),
            jax.ShapeDtypeStruct((size, length), f32),
            jax.ShapeDtypeStruct((length, length), bf16),
            jax.ShapeDtypeStruct((1, length), f32),
        ],
        scratch_shapes=[
            pltpu.VMEM((length, 2 * size), bf16),
            pltpu.VMEM((2 * size, chunk), bf16),
            pltpu.VMEM((length, chunk), f32),
        ],
        compiler_params=pltpu.CompilerParams(vmem_limit_bytes=vmem_bytes),
        cost_estimate=cost(11),
        name="attend",
    )(lengths, head, table, taken, band, *after)


def attend_back_kernel(
    size, blocks, buckets, after, taken_ref, grad_ref, context_ref, expo_ref, scale_ref, *refs
):
    sent_ref, band_ref, far_ref, sums_ref, *refs = refs[after:]
    attend_back_steps(
        size, blocks, buckets, taken_ref, grad_ref, context_ref, expo_ref, scale_ref,
        sent_ref, band_ref, far_ref, sums_ref, *refs,
    )


def attend_back_steps(
    size, blocks, buckets, taken_ref, grad_ref, context_ref, expo_ref, scale_ref,
    sent_ref, band_ref, far_ref, sums_ref,
    queries_ref, tall_ref, wide_ref, delta_ref, grad_queries_ref, grad_scores_ref,
):
    c = pl.program_id(0)
    chunks = blocks // 2
    tok = chunk // 2

    @pl.when(c == 0)
    def _():
        for s in range(blocks):
            spot = slice(s * tok, (s + 1) * tok)
            scaled = grad_ref[s].astype(f32) * scale_ref[:, spot]
            wide_ref[:, spot] = scaled.astype(bf16)
            tall_ref[spot, :] = scaled.T.astype(bf16)
            delta_ref[:, spot] = jnp.sum(scaled * context_ref[:, spot], axis=0, keepdims=True)
            queries_ref[spot, :] = taken_ref[s, :size, :].astype(f32).T.astype(bf16)
        grad_queries_ref[...] = jnp.zeros_like(grad_queries_ref)
        band_ref[...] = jnp.zeros_like(band_ref)
        far_ref[...] = jnp.zeros_like(far_ref)

    values = tile_rows(taken_ref, c, 2 * size, 3 * size).astype(f32).T.astype(bf16)
    for q in range(chunks):
        spot = slice(q * chunk, (q + 1) * chunk)
        grad_weights = jnp.dot(values, wide_ref[:, spot], preferred_element_type=f32)
        weights = expo_ref[:, spot].astype(f32)
        grad_scores_ref[:, spot] = (weights * (grad_weights - delta_ref[:, spot])).astype(bf16)
    grad_values = jnp.dot(expo_ref[...], tall_ref[...], preferred_element_type=f32).T.astype(bf16)
    grad_keys = jnp.dot(
        grad_scores_ref[...], queries_ref[...], preferred_element_type=f32
    ).T.astype(bf16)
    for t in range(2):
        sent_ref[2 * c + t, size : 2 * size, :] = grad_keys[:, t * tok : (t + 1) * tok]
        sent_ref[2 * c + t, 2 * size : 3 * size, :] = grad_values[:, t * tok : (t + 1) * tok]
    keys = jnp.concatenate(
        [tile_rows(taken_ref, c, size, 2 * size), jnp.ones((16, chunk), bf16)], axis=0
    )
    for q in range(chunks):
        spot = slice(q * chunk, (q + 1) * chunk)
        part = jnp.dot(keys, grad_scores_ref[:, spot], preferred_element_type=f32)
        grad_queries_ref[:, spot] = grad_queries_ref[:, spot] + part[:size]
        sums = part[size : size + 8]
        far_ref[0, :, spot] = far_ref[0, :, spot] + jnp.where(c <= q - 2, sums, 0.0)
        far_ref[1, :, spot] = far_ref[1, :, spot] + jnp.where(c >= q + 2, sums, 0.0)
    for j in (-1, 0, 1):

        @pl.when((c - j >= 0) & (c - j < chunks))
        def _():
            spot = pl.ds(pl.multiple_of((c - j) * chunk, chunk), chunk)
            band_ref[j + 1] = band_ref[j + 1] + grad_scores_ref[:, spot].astype(f32)

    @pl.when(c == chunks - 1)
    def _():
        for s in range(blocks):
            sent_ref[s, :size, :] = grad_queries_ref[:, s * tok : (s + 1) * tok].astype(bf16)
        pieces = table_pieces(buckets, band_ref, far_ref, sums_ref)
        for s in range(blocks):
            sent_ref[s, 3 * size :, :] = pieces


def attend_back(taken, grads, context, expo, scale, buckets, *after):
    blocks, size, tok = grads.shape
    length = expo.shape[0]
    return pl.pallas_call(
        functools.partial(attend_back_kernel, size, blocks, buckets, len(after)),
        grid=(blocks // 2,),
        in_specs=[
            pl.BlockSpec((blocks, 3 * size, tok), lambda c: (0, 0, 0)),
            pl.BlockSpec((blocks, size, tok), lambda c: (0, 0, 0)),
            pl.BlockSpec((size, length), lambda c: (0, 0)),
            pl.BlockSpec((chunk, length), lambda c: (c, 0)),
            pl.BlockSpec((1, length), lambda c: (0, 0)),
        ]
        + [pl.BlockSpec(memory_space=pl.ANY)] * len(after),
        out_specs=pl.BlockSpec((blocks, 3 * size + 16, tok), lambda c: (0, 0, 0)),
        out_shape=jax.ShapeDtypeStruct((blocks, 3 * size + 16, tok), bf16),
        scratch_shapes=[
            pltpu.VMEM((3, chunk, chunk), f32),
            pltpu.VMEM((2, 8, length), f32),
            pltpu.VMEM((buckets, chunk // 2), f32),
            pltpu.VMEM((length, size), bf16),
            pltpu.VMEM((length, size), bf16),
            pltpu.VMEM((size, length), bf16),
            pltpu.VMEM((1, length), f32),
            pltpu.VMEM((size, length), f32),
            pltpu.VMEM((chunk, length), bf16),
        ],
        compiler_params=pltpu.CompilerParams(vmem_limit_bytes=vmem_bytes),
        cost_estimate=cost(13),
        name="attend_back",
    )(taken, grads, context, expo, scale, *after)


def feed_kernel(
    heads, steps, flipped_ref, matrix_ref, hidden_ref, context_ref, given_ref, gain_ref, *refs
):
    outs, gates, ups, downs = (refs[2 * k : 2 * k + 2] for k in range(4))
    (
        result_ref, grad_mid_ref, grad_context_ref, packet_ref, left_ref,
        normed_ref, branch_ref, cot_ref, mid_ref, total_ref, grad_ref,
    ) = refs[-11:]
    units = steps * chunk
    lead = packet_ref.shape[1] - 3 * units - context_ref.shape[0] * context_ref.shape[1]
    j = pl.program_id(0)
    size, tok = context_ref.shape[1:]
    sides = side(flipped_ref[0], hidden_ref.shape[1] // 2)

    @pl.when(j == 0)
    def _():
        cot_ref[...] = jnp.dot(
            given_ref[...], matrix_ref[...], preferred_element_type=f32
        ).astype(bf16)
        context = context_ref[...].reshape(-1, tok)
        context = context.astype(f32).T.astype(bf16)
        packet_ref[:, packet_ref.shape[1] - context.shape[1] :] = context
        context = context[:, : heads * size]
        for lanes, ref in zip(sides, outs):
            mid_ref[:, lanes] = dot_on(context, ref[...], 1, 1)
        mid = hidden_ref[...].astype(f32) + mid_ref[...]
        mid_ref[...] = mid
        total_ref[...] = mid
        normed_ref[...] = rms_norm(mid, gain_ref[...]).astype(bf16)
        grad_ref[...] = jnp.zeros_like(grad_ref)

    def over_width(left_ref, rights):
        own, other = (
            jnp.dot(left_ref[:, lanes], ref[...], preferred_element_type=f32)
            for lanes, ref in zip(sides, rights)
        )
        return own + other

    gate = over_width(normed_ref, gates)
    up = over_width(normed_ref, ups)
    grad_inner = over_width(cot_ref, downs)
    slope = 0.7978845608028654
    square = gate * gate
    bent = jnp.tanh(slope * (gate + 0.044715 * (square * gate)))
    half = 0.5 * (1.0 + bent)
    gelu = gate * half
    gelu_grad = half + (0.5 * gate) * (1.0 - bent * bent) * (
        slope * (1.0 + (3 * 0.044715) * square)
    )
    inner = (gelu * up).astype(bf16)
    grad_gate = (grad_inner * up * gelu_grad).astype(bf16)
    grad_up = (grad_inner * gelu).astype(bf16)
    for k, part in enumerate((grad_gate, grad_up, inner)):
        packet_ref[:, pl.ds(pl.multiple_of(lead + k * units + j * chunk, chunk), chunk)] = part
    for k, lanes in enumerate(sides):
        total_ref[:, lanes] = total_ref[:, lanes] + dot_on(inner, downs[k][...], 1, 1)
        grad_ref[:, lanes] = (
            grad_ref[:, lanes]
            + dot_on(grad_gate, gates[k][...], 1, 1)
            + dot_on(grad_up, ups[k][...], 1, 1)
        )

    @pl.when(j == steps - 1)
    def _():
        result_ref[...] = dot_on(total_ref[...].astype(bf16), matrix_ref[...], 1, 1).astype(bf16)
        mid = mid_ref[...]
        scale = lax.rsqrt(jnp.mean(mid * mid, axis=-1, keepdims=True) + norm_eps)
        grad_normed = grad_ref[...]
        gained = grad_normed * gain_ref[...]
        inward = jnp.mean(gained * mid, axis=-1, keepdims=True)
        grad_mid = cot_ref[...].astype(f32) + scale * gained - mid * (scale * scale * scale * inward)
        grad_mid_ref[...] = grad_mid
        branch_ref[...] = grad_mid.astype(bf16)
        grad_context = over_width(branch_ref, outs).T.astype(bf16)
        grad_context_ref[...] = jnp.zeros_like(grad_context_ref)
        for h in range(heads):
            grad_context_ref[h] = grad_context[h * size : (h + 1) * size, :]
        own, other = sides
        half = hidden_ref.shape[1] // 2
        for k, ref in enumerate((normed_ref, cot_ref, branch_ref)):
            left_ref[:, k * half : (k + 1) * half] = ref[:, own]
            packet_ref[:, k * half : (k + 1) * half] = ref[:, other]
        packet_ref[:, 3 * half : lead] = jnp.zeros((tok, lead - 3 * half), bf16)


def feed(flipped, matrix, hidden, context, cot, gain, weights, heads, *after):
    tok, width = hidden.shape
    blocks, size, _ = context.shape
    inner_width = heads * size
    units = (weights[0].shape[1] - inner_width) // 3
    steps = units // chunk
    first = inner_width // chunk
    whole = lambda *shape: pl.BlockSpec(shape, lambda j: (0,) * len(shape))
    column = lambda offset: pl.BlockSpec((width // 2, chunk), lambda j: (0, offset + j))
    lead = -(-3 * (width // 2) // (2 * chunk)) * 2 * chunk
    packet = lead + 3 * units + blocks * size
    weight_specs = [whole(width // 2, inner_width)] * 2
    for k in range(3):
        weight_specs += [column(first + k * steps)] * 2
    return pl.pallas_call(
        functools.partial(feed_kernel, heads, steps),
        grid=(steps,),
        in_specs=[
            pl.BlockSpec(memory_space=pltpu.SMEM),
            whole(width, width),
            whole(tok, width),
            whole(blocks, size, tok),
            whole(tok, width),
            whole(1, width),
            *weight_specs,
        ]
        + [pl.BlockSpec(memory_space=pl.ANY)] * len(after),
        out_specs=[
            whole(tok, width),
            whole(tok, width),
            whole(blocks, size, tok),
            whole(tok, packet),
            whole(tok, 3 * (width // 2)),
        ],
        out_shape=[
            jax.ShapeDtypeStruct((tok, width), bf16),
            jax.ShapeDtypeStruct((tok, width), f32),
            jax.ShapeDtypeStruct((blocks, size, tok), bf16),
            jax.ShapeDtypeStruct((tok, packet), bf16),
            jax.ShapeDtypeStruct((tok, 3 * (width // 2)), bf16),
        ],
        scratch_shapes=[pltpu.VMEM((tok, width), bf16)] * 3 + [pltpu.VMEM((tok, width), f32)] * 3,
        compiler_params=pltpu.CompilerParams(vmem_limit_bytes=vmem_bytes),
        cost_estimate=cost(8),
        name="feed",
    )(flipped, matrix, hidden, context, cot, gain, *weights * 4, *after)


def store_tall(ref, parts):
    for m, part in enumerate(parts):
        tok = part.shape[0]
        ref[:, m * tok : (m + 1) * tok] = part.astype(f32).T.astype(bf16)


def weight_grad_kernel(counts, parts, half, *refs):
    j = pl.program_id(0)
    out_ref, tall_ref = refs[-2:]
    lefts, rights = refs[:parts], refs[parts : 2 * parts]
    start = 0
    for k, count in counts:

        @pl.when(j == start)
        def _(k=k):
            store_tall(tall_ref, [ref[:, k * half : (k + 1) * half] for ref in lefts])

        start += count
    right = jnp.concatenate([ref[...] for ref in rights], axis=0)
    out_ref[...] = jnp.dot(tall_ref[...], right, preferred_element_type=f32).astype(bf16)


def weight_grads(lefts, rights, half, units, inner_width, *after):
    tok, block = lefts[0].shape[0], 2 * chunk
    steps = units // block
    counts = [(0, 2 * steps), (1, steps), (2, inner_width // block)]
    total = 3 * steps + inner_width // block
    lead = rights[0].shape[1] - total * block
    anywhere = pl.BlockSpec(memory_space=pl.ANY)
    return pl.pallas_call(
        functools.partial(weight_grad_kernel, counts, len(lefts), half),
        grid=(total,),
        in_specs=[
            pl.BlockSpec((tok, min(left.shape[1], lead)), lambda j: (0, 0)) for left in lefts
        ]
        + [pl.BlockSpec((tok, block), lambda j: (0, lead // block + j))] * len(rights)
        + [anywhere] * len(after),
        out_specs=pl.BlockSpec((half, block), lambda j: (0, j)),
        out_shape=jax.ShapeDtypeStruct((half, total * block), bf16),
        scratch_shapes=[pltpu.VMEM((half, len(lefts) * tok), bf16)],
        compiler_params=pltpu.CompilerParams(vmem_limit_bytes=vmem_bytes),
        cost_estimate=cost(10),
        name="weight_grads",
    )(*lefts, *rights, *after)


def project_kernel(
    heads, flipped_ref, matrix_ref, inputs_ref, own_ref, other_ref, after_ref, *refs
):
    micro, tok, width = inputs_ref.shape
    sent, (tokens_ref, normed_ref, gain_a_ref, gain_f_ref, gains_ref) = refs[:micro], refs[micro:]
    inner_width = (own_ref.shape[1] - 128) // 3
    size = inner_width // heads
    sides = side(flipped_ref[0], width // 2)
    for lanes, ref in zip(sides, (own_ref, other_ref)):
        gains_ref[:, lanes] = ref[:, 3 * inner_width :].astype(f32).T[:8]
    gain_a_ref[...] = gains_ref[:1]
    gain_f_ref[...] = gains_ref[1:2]
    hidden = jnp.dot(
        inputs_ref[...].reshape(micro * tok, width), matrix_ref[...], preferred_element_type=f32
    )
    tokens_ref[...] = hidden.astype(bf16).reshape(micro, tok, width)
    normed_ref[...] = rms_norm(hidden, gains_ref[:1]).astype(bf16)
    for ref in sent:
        ref[heads:] = jnp.zeros((ref.shape[0] - heads,) + ref.shape[1:], bf16)
    for k in range(3):
        for half in range(2):
            start = k * inner_width + half * (inner_width // 2)
            own, other = (
                jnp.dot(
                    normed_ref[:, lanes],
                    ref[:, start : start + inner_width // 2],
                    preferred_element_type=f32,
                )
                for lanes, ref in zip(sides, (own_ref, other_ref))
            )
            part = (own + other).T.astype(bf16)
            for h in range(heads // 2):
                for m, ref in enumerate(sent):
                    ref[half * (heads // 2) + h, k * size : (k + 1) * size, :] = part[
                        h * size : (h + 1) * size, m * tok : (m + 1) * tok
                    ]


def project(flipped, matrix, inputs, weights, heads, blocks, after):
    micro, tok, width = inputs.shape
    size = (weights[0].shape[1] - 128) // 3 // heads
    vmem = pl.BlockSpec(memory_space=pltpu.VMEM)
    outs = pl.pallas_call(
        functools.partial(project_kernel, heads),
        in_specs=[
            pl.BlockSpec(memory_space=pltpu.SMEM),
            vmem,
            vmem,
            vmem,
            vmem,
            pl.BlockSpec(memory_space=pl.ANY),
        ],
        out_shape=[jax.ShapeDtypeStruct((blocks, 3 * size, tok), bf16)] * micro
        + [
            jax.ShapeDtypeStruct((micro, tok, width), bf16),
            jax.ShapeDtypeStruct((micro * tok, width), bf16),
            jax.ShapeDtypeStruct((1, width), f32),
            jax.ShapeDtypeStruct((1, width), f32),
        ],
        scratch_shapes=[pltpu.VMEM((8, width), f32)],
        compiler_params=pltpu.CompilerParams(vmem_limit_bytes=vmem_bytes),
        cost_estimate=cost(3),
        name="project",
    )(flipped, matrix, inputs, *weights, after)
    return outs[:micro], *outs[micro:]


def lined(refs, heads, size, lined_ref):
    tok = refs[0].shape[2]
    for m, ref in enumerate(refs):
        for k in range(3):
            for h in range(heads):
                start = (k * heads + h) * size
                lined_ref[start : start + size, m * tok : (m + 1) * tok] = ref[
                    h, k * size : (k + 1) * size, :
                ]


def input_grad_kernel(heads, micro, *refs):
    flipped_ref, matrix_ref, inputs_ref, own_weights, other_weights, gains_ref = refs[:6]
    grads, mids = (refs[6 + k * micro : 6 + (k + 1) * micro] for k in range(2))
    input_grad_ref, wide_ref, lined_ref = refs[-3:]
    tok, width = inputs_ref.shape[1:]
    inner_width = (own_weights.shape[1] - 128) // 3
    sides = side(flipped_ref[0], width // 2)
    lined(grads, heads, inner_width // heads, lined_ref)
    for ref, rows in zip((own_weights, other_weights), sides):
        wide_ref[rows, :] = jnp.dot(
            ref[:, : 3 * inner_width], lined_ref[...], preferred_element_type=f32
        )
    gain = gains_ref[...]
    for m in range(micro):
        grad = wide_ref[:, m * tok : (m + 1) * tok].T
        hidden = inputs_ref[m].astype(f32)
        scale = lax.rsqrt(jnp.mean(hidden * hidden, axis=-1, keepdims=True) + norm_eps)
        gained = grad * gain
        inward = jnp.mean(gained * hidden, axis=-1, keepdims=True)
        found = mids[m][...] + scale * gained - hidden * (scale * scale * scale * inward)
        high = found.astype(bf16)
        rest = found - high.astype(f32)
        middle = rest.astype(bf16)
        low = (rest - middle.astype(f32)).astype(bf16)
        input_grad_ref[m] = sum(
            dot_on(part, matrix_ref[...], 1, 1) for part in (low, middle, high)
        )


def input_grads(flipped, matrix, inputs, weights, gains, grads, mids, heads, *after):
    micro, tok, width = inputs.shape
    inner_width = (weights[0].shape[1] - 128) // 3
    vmem = pl.BlockSpec(memory_space=pltpu.VMEM)
    return pl.pallas_call(
        functools.partial(input_grad_kernel, heads, micro),
        in_specs=[pl.BlockSpec(memory_space=pltpu.SMEM)]
        + [vmem] * (5 + 2 * micro)
        + [pl.BlockSpec(memory_space=pl.ANY)] * len(after),
        out_shape=jax.ShapeDtypeStruct((micro, tok, width), f32),
        scratch_shapes=[
            pltpu.VMEM((width, micro * tok), f32),
            pltpu.VMEM((3 * inner_width, micro * tok), bf16),
        ],
        compiler_params=pltpu.CompilerParams(vmem_limit_bytes=vmem_bytes),
        cost_estimate=cost(6),
        name="input_grads",
    )(flipped, matrix, inputs, *weights, gains, *grads, *mids, *after)


def front_grad_kernel(heads, parts, half, which, *refs):
    flipped_ref = refs[0]
    lefts, grads = refs[1 : 1 + parts], refs[1 + parts : 1 + 2 * parts]
    out_ref, tall_ref, lined_ref = refs[-3:]
    tok = grads[0].shape[2]
    inner_width = out_ref.shape[1] // 3
    lined(grads, heads, inner_width // heads, lined_ref)
    lanes = side(flipped_ref[0], half)[which]
    for p, ref in enumerate(lefts):
        tall = ref[:, lanes].astype(f32).T.astype(bf16)
        tall_ref[:, p * tok : (p + 1) * tok] = tall
    for k in range(3):
        spot = slice(k * inner_width, (k + 1) * inner_width)
        out_ref[:, spot] = dot_on(tall_ref[...], lined_ref[spot, :], 1, 1).astype(bf16)


def front_grads(flipped, lefts, grads, inner_width, heads, which):
    tok, width = lefts[0].shape
    parts = len(lefts)
    vmem = pl.BlockSpec(memory_space=pltpu.VMEM)
    return pl.pallas_call(
        functools.partial(front_grad_kernel, heads, parts, width // 2, which),
        in_specs=[pl.BlockSpec(memory_space=pltpu.SMEM)] + [vmem] * (2 * parts),
        out_shape=jax.ShapeDtypeStruct((width // 2, 3 * inner_width), bf16),
        scratch_shapes=[
            pltpu.VMEM((width // 2, parts * tok), bf16),
            pltpu.VMEM((3 * inner_width, parts * tok), bf16),
        ],
        compiler_params=pltpu.CompilerParams(vmem_limit_bytes=vmem_bytes),
        cost_estimate=cost(5),
        name="front_grads",
    )(flipped, *lefts, *grads)


def row_of(column):
    share = column.shape[0]
    shape = (share, share)
    spread = lax.broadcasted_iota(jnp.int32, shape, 0) == lax.broadcasted_iota(jnp.int32, shape, 1)
    return jnp.sum(jnp.where(spread, column, 0.0), axis=0, keepdims=True)


def gain_grad_of(weights, grads, gain_ref):
    total = sum(
        jnp.sum(weight[...].astype(f32) * grad[...], axis=1, keepdims=True)
        for weight, grad in zip(weights, grads)
    )
    return row_of(total) / gain_ref[...].astype(f32)


def unpack_back_kernel(sums_ref, gate_ref, up_ref, gain_ref, *refs):
    gate_grad_ref, up_grad_ref, down_grad_ref, out_grad_ref, gain_grad_ref = refs
    units = gate_ref.shape[1]
    for k, ref in enumerate((gate_grad_ref, up_grad_ref, down_grad_ref, out_grad_ref)):
        ref[...] = sums_ref[:, k * units : k * units + ref.shape[1]].astype(f32)
    gain_grad_ref[...] = gain_grad_of((gate_ref, up_ref), (gate_grad_ref, up_grad_ref), gain_ref)


def unpack_back(sums, w_gate, w_up, gain, inner_width):
    share, units = w_gate.shape
    shapes = [(share, units)] * 3 + [(share, inner_width), (1, share)]
    gate, up, down, out, gain_grad = pl.pallas_call(
        unpack_back_kernel,
        out_shape=[jax.ShapeDtypeStruct(shape, f32) for shape in shapes],
        compiler_params=pltpu.CompilerParams(vmem_limit_bytes=vmem_bytes),
        name="unpack_back",
    )(sums, w_gate, w_up, gain[None, :])
    return gate, up, down.T, out.T, gain_grad[0]


def unpack_front_kernel(parts_ref, query_ref, key_ref, value_ref, gain_ref, after_ref, *refs):
    grads, gain_grad_ref = refs[:3], refs[3]
    width = query_ref.shape[1]
    for k, ref in enumerate(grads):
        part = parts_ref[:, :, k * width : (k + 1) * width].astype(f32)
        ref[...] = jnp.sum(part, axis=0)
    gain_grad_ref[...] = gain_grad_of((query_ref, key_ref, value_ref), grads, gain_ref)


def unpack_front(parts, w_query, w_key, w_value, gain, after):
    share, width = w_query.shape
    vmem = pl.BlockSpec(memory_space=pltpu.VMEM)
    shapes = [(share, width)] * 3 + [(1, share)]
    query, key, value, gain_grad = pl.pallas_call(
        unpack_front_kernel,
        in_specs=[vmem] * 5 + [pl.BlockSpec(memory_space=pl.ANY)],
        out_shape=[jax.ShapeDtypeStruct(shape, f32) for shape in shapes],
        compiler_params=pltpu.CompilerParams(vmem_limit_bytes=vmem_bytes),
        name="unpack_front",
    )(parts, w_query, w_key, w_value, gain[None, :], after)
    return query, key, value, gain_grad[0]


def body(
    inputs, doc_lengths, attn_gain, w_query, w_key, w_value, w_out, ff_gain,
    w_gate, w_up, w_down, rel_table, cotangent,
):
    micro, _, tok, width = inputs.shape
    inner_width = w_query.shape[1]
    hidden_units = w_gate.shape[1]
    buckets, heads = rel_table.shape
    size = inner_width // heads
    blocks = lax.axis_size("blk")
    rows = lax.axis_size("rows")
    me = lax.axis_index("blk")
    share = w_query.shape[0]
    micros = range(micro)

    flipped = lax.axis_index("rows") if staged(rows, blocks, share) else 0
    flipped = jnp.full((1,), flipped, jnp.int32)
    matrix = stage_matrix(rows, blocks, share)
    head = jnp.minimum(me, heads - 1).astype(jnp.int32).reshape(1)
    table = rel_table.astype(f32).reshape(-1)

    with jax.named_scope("weights"):
        front_full = gather_front(w_query, w_key, w_value, attn_gain, ff_gain)
        back_own = gather_back(jnp.concatenate([w_out.T, w_gate, w_up, w_down.T], axis=1), front_full[0])

    band = bias_tiles(head, table, buckets)
    sent, tokens, normed_a, gain_a, gain_f = project(
        flipped, matrix, inputs[:, 0], front_full, heads, blocks, band
    )
    taken = []
    for m in micros:
        with jax.named_scope("project"):
            part = tie(sent[m], taken[-1]) if m else sent[m]
            taken.append(lax.all_to_all(part, "blk", 0, 0, tiled=True))

    kept, contexts = [], []
    for m in micros:
        part, *rest = attend(
            taken[m], doc_lengths[m, 0], head, table, band, buckets, *[k[0] for k in kept]
        )
        kept.append(rest)
        with jax.named_scope("context"):
            contexts.append(lax.all_to_all(part, "blk", 0, 0, tiled=True))
    with jax.named_scope("weights"):
        back_full = gather_other(back_own, part)

    fed, grads, packets = [], [], []
    fits = staged(rows, blocks, share)
    for m in micros:
        outs = list(
            feed(
                flipped, matrix, tokens[m], contexts[m], cotangent[m, 0], gain_f, back_full, heads,
            )
        )
        with jax.named_scope("grad_context"):
            part = tie(outs[2], *grads) if m else outs[2]
            grads.append(lax.all_to_all(part, "blk", 0, 0, tiled=True))
        if fits:
            with jax.named_scope("packet"):
                outs[3] = tie(outs[3], grads[0]) if m else outs[3]
                packets.append(flip(outs[3], "rows", 1))
        fed.append(outs)
    result, grad_mid, _, mine, left = zip(*fed)

    wide = blocks * size
    with jax.named_scope("back_grads"):
        sizes = width // 2, hidden_units, wide
        if fits:
            own = weight_grads([*left, *packets], [*mine, *packets], *sizes)
            back_grad = scatter_back(own)
        else:
            own, other = (weight_grads(lefts, mine, *sizes) for lefts in (left, mine))
            back_grad = scatter_whole(own, other)
    grad_qkv = []
    for m in micros:
        returned = attend_back(taken[m], grads[m], *kept[m], buckets, own)
        with jax.named_scope("grad_qkv"):
            returned = tie(returned, *grad_qkv) if m else returned
            grad_qkv.append(lax.all_to_all(returned, "blk", 0, 0, tiled=True))

    with jax.named_scope("table"):
        sums = sum(
            jnp.sum(g[:heads, 3 * size : 3 * size + 3, :buckets].astype(f32), axis=1)
            for g in grad_qkv
        )
        table_grad = sums.T
        for bit in bits_of(rows):
            table_grad = table_grad + flip(table_grad, "rows", bit)

    with jax.named_scope("front_grads"):
        normed = [normed_a[m * tok : (m + 1) * tok] for m in micros]
        if fits:
            near_grads = [flip(g, "rows", 1) for g in grad_qkv]
            near_normed = [flip(n, "rows", 1) for n in normed]
            own = front_grads(
                flipped, normed + near_normed, grad_qkv + near_grads, inner_width, heads, 0
            )
            back_grad = scatter_back_end(back_grad, own)
            front_parts = scatter_front(own, share)
        else:
            own, other = (
                front_grads(flipped, normed, grad_qkv, inner_width, heads, which)
                for which in (0, 1)
            )
            front_parts = scatter_whole(own, other)[None]
    input_grad = input_grads(
        flipped, matrix, tokens, front_full, gain_a, grad_qkv, grad_mid, heads, own
    )
    if fits:
        with jax.named_scope("front_grads"):
            front_parts = scatter_front_end(front_parts, share, input_grad)
    gate_grad, up_grad, down_grad, out_grad, ff_gain_grad = unpack_back(
        back_grad, w_gate, w_up, ff_gain, inner_width
    )
    query_grad, key_grad, value_grad, attn_gain_grad = unpack_front(
        front_parts, w_query, w_key, w_value, attn_gain, gate_grad
    )

    return (
        jnp.stack(result).reshape(micro, 1, tok, width),
        input_grad[:, None],
        attn_gain_grad,
        query_grad,
        key_grad,
        value_grad,
        out_grad,
        ff_gain_grad,
        gate_grad,
        up_grad,
        down_grad,
        table_grad,
    )


def solution(mesh):
    weight_rows = P(both, None)
    weight_columns = P(None, both)
    tokens = P(None, "rows", "blk", None)
    in_specs = (
        tokens, P(None, "rows", None), P(both), weight_rows, weight_rows, weight_rows,
        weight_columns, P(both), weight_rows, weight_rows, weight_columns, P(), tokens,
    )
    out_specs = (
        tokens, tokens, P(both), weight_rows, weight_rows, weight_rows,
        weight_columns, P(both), weight_rows, weight_rows, weight_columns, P(),
    )
    return jax.shard_map(body, mesh=mesh, in_specs=in_specs, out_specs=out_specs, check_vma=False)
```

```python
import functools

import jax
import jax.numpy as jnp
import numpy as np
from jax import lax
from jax.experimental import pallas as pl
from jax.experimental.pallas import tpu as pltpu
from jax.sharding import PartitionSpec as P

bucket_edges = (12, 16, 23, 32, 46, 64, 91)
norm_eps = 1e-06
masked_score = -1e30
f32 = jnp.float32
bf16 = jnp.bfloat16
both = ("rows", "blk")
chunk = 256
feed_chunk = 512
grad_chunk = 1024
subs = 2
vmem_bytes = 56 * 1024 * 1024
few_bytes = 24 * 1024 * 1024


def bucket_of(relative, total_buckets):
    half = total_buckets // 2
    exact = half // 2
    distance = jnp.abs(relative)
    far_bucket = exact + sum(((distance >= edge).astype(jnp.int32) for edge in bucket_edges))
    return jnp.where(relative > 0, half, 0) + jnp.where(distance < exact, distance, far_bucket)


def rms_norm(hidden, gain):
    return hidden * lax.rsqrt(jnp.mean(hidden * hidden, axis=-1, keepdims=True) + norm_eps) * gain


def gated(gate, up):
    return jax.nn.gelu(gate, approximate=True) * up


def dot_on(left, right, left_dim, right_dim):
    return lax.dot_general(
        left, right, (((left_dim,), (right_dim,)), ((), ())), preferred_element_type=f32
    )


def flip(array, axis, bit):
    count = lax.axis_size(axis)
    return lax.ppermute(array, axis, [(i, i ^ bit) for i in range(count)])


def bits_of(count):
    return [1 << k for k in range(count.bit_length() - 1)]


def segments_at(bounds, positions):
    total = jnp.zeros(positions.shape, jnp.int32)
    for bound in bounds:
        total = total + (positions >= bound).astype(jnp.int32)
    return total


def groups_of(blocks):
    near = 4
    far = blocks // near
    across = [[f * near + n for f in range(far)] for n in range(near)]
    within = [[f * near + n for n in range(near)] for f in range(far)]
    return far, near, across, within


def staged(rows, blocks, share):
    return rows == 2 and blocks % 4 == 0 and share % 8 == 0


def stage_matrix(rows, blocks, share):
    place = np.arange(rows * blocks * share)
    taken = place
    if staged(rows, blocks, share):
        far, near, _, _ = groups_of(blocks)
        slab = place // share
        half, inner = slab // blocks, slab % blocks
        taken = (half * blocks + inner % far * near + inner // far) * share + place % share
    return jnp.asarray((place[:, None] == taken[None, :]).astype(np.float32), bf16)


def tie_kernel(*refs):
    pass


def tie(value, *after):
    space = pl.BlockSpec(memory_space=pl.ANY)
    return pl.pallas_call(
        tie_kernel,
        in_specs=[space] * (1 + len(after)),
        out_specs=space,
        out_shape=jax.ShapeDtypeStruct(value.shape, value.dtype),
        input_output_aliases={0: 0},
        name="tie",
    )(value, *after)


def exchange(array, groups):
    return lax.all_to_all(array, "blk", 0, 0, tiled=True, axis_index_groups=groups)


def halves_of_whole(whole):
    half = whole.shape[0] // 2
    return whole[:half], whole[half:]


def pack_kernel(query_ref, key_ref, value_ref, gain_a_ref, gain_f_ref, out_ref):
    share = query_ref.shape[0]
    spread = lax.broadcasted_iota(jnp.int32, (share, share), 0) == lax.broadcasted_iota(
        jnp.int32, (share, share), 1
    )
    lane = lax.broadcasted_iota(jnp.int32, (share, 128), 1)
    gains = jnp.zeros((share, 128), f32)
    for k, ref in enumerate((gain_a_ref, gain_f_ref)):
        column = jnp.where(spread, ref[...].astype(f32), 0.0)
        gains = jnp.where(lane == k, jnp.sum(column, axis=1, keepdims=True), gains)
    parts = [query_ref[...], key_ref[...], value_ref[...], gains.astype(bf16)]
    packed = jnp.concatenate(parts, axis=1)
    for copy in range(out_ref.shape[0]):
        out_ref[copy] = packed


def pack(query, key, value, gain_a, gain_f, copies):
    shape = (copies, query.shape[0], 3 * query.shape[1] + 128)
    return pl.pallas_call(
        pack_kernel,
        out_shape=jax.ShapeDtypeStruct(shape, bf16),
        compiler_params=pltpu.CompilerParams(vmem_limit_bytes=vmem_bytes),
        name="pack",
    )(query, key, value, gain_a[None, :], gain_f[None, :])


def gather_front(*parts):
    blocks, rows = lax.axis_size("blk"), lax.axis_size("rows")
    if not staged(rows, blocks, parts[0].shape[0]):
        shard = pack(*parts, 1)[0]
        return halves_of_whole(lax.all_gather(shard, both, axis=0, tiled=True))
    far, near, across, within = groups_of(blocks)
    packed = pack(*parts, far)
    first = exchange(packed.reshape(-1, packed.shape[2]), across)
    own = exchange(jnp.tile(first, (near, 1)), within)
    return own, flip(own, "rows", 1)


def gather_back(shard, after):
    blocks, rows = lax.axis_size("blk"), lax.axis_size("rows")
    if not staged(rows, blocks, shard.shape[0]):
        return lax.all_gather(shard, both, axis=0, tiled=True)
    far, near, across, within = groups_of(blocks)
    own = lax.all_gather(shard, "blk", axis=0, tiled=True, axis_index_groups=across)
    own = tie(own, after)
    return lax.all_gather(own, "blk", axis=0, tiled=True, axis_index_groups=within)


def gather_other(own, after):
    blocks, rows = lax.axis_size("blk"), lax.axis_size("rows")
    if not staged(rows, blocks, own.shape[0] // blocks):
        return halves_of_whole(own)
    own = tie(own, after)
    return own, flip(own, "rows", 1)


def scatter_front(own, share):
    far, near, _, within = groups_of(lax.axis_size("blk"))
    held = exchange(own, within).reshape(near, far * share, own.shape[1])
    return jnp.sum(held.astype(f32), axis=0).astype(bf16)


def scatter_front_end(held, share, *after):
    far, _, across, _ = groups_of(lax.axis_size("blk"))
    return exchange(tie(held, *after), across).reshape(far, share, held.shape[1])


def scatter_back(own):
    _, _, _, within = groups_of(lax.axis_size("blk"))
    return lax.psum_scatter(
        own, "blk", scatter_dimension=0, axis_index_groups=within, tiled=True
    )


def scatter_back_end(part, after):
    _, _, across, _ = groups_of(lax.axis_size("blk"))
    return lax.psum_scatter(
        tie(part, after), "blk", scatter_dimension=0, axis_index_groups=across, tiled=True
    )


def scatter_whole(own, other):
    whole = jnp.concatenate([own, other], axis=0)
    return lax.psum_scatter(whole, both, scatter_dimension=0, tiled=True)


def side(flipped, half):
    return (
        pl.ds(pl.multiple_of(flipped * half, half), half),
        pl.ds(pl.multiple_of((1 - flipped) * half, half), half),
    )


def cost(micros):
    return pl.CostEstimate(flops=int(micros * 1e9), bytes_accessed=0, transcendentals=0)


def tile_rows(ref, index, start, stop):
    return jnp.concatenate(
        [ref[2 * index, start:stop, :], ref[2 * index + 1, start:stop, :]], axis=1
    )


def steps_of(buckets):
    half = buckets // 2
    exact = half // 2
    lows = list(range(1, exact)) + [exact] + list(bucket_edges)
    places = [(1 - low, k) for k, low in reversed(list(enumerate(lows)))]
    return half - 1, places + [(low, half + 1 + k) for k, low in enumerate(lows)]


def relative_tile(j):
    shape = (chunk, chunk)
    return (
        lax.broadcasted_iota(jnp.int32, shape, 0)
        - lax.broadcasted_iota(jnp.int32, shape, 1)
        + j * chunk
    )


def bias_kernel(buckets, heads, head_ref, table_ref, band_ref):
    first, places = steps_of(buckets)
    value = lambda bucket: table_ref[bucket * heads + head_ref[0]]
    for j in (-1, 0, 1):
        relative = relative_tile(j)
        tile = jnp.full((chunk, chunk), value(first), f32)
        for place, bucket in places:
            tile = jnp.where(relative >= place, value(bucket), tile)
        band_ref[j + 1] = tile


def bias_tiles(head, table, buckets):
    smem = pl.BlockSpec(memory_space=pltpu.SMEM)
    return pl.pallas_call(
        functools.partial(bias_kernel, buckets, table.shape[0] // buckets),
        in_specs=[smem, smem],
        out_shape=jax.ShapeDtypeStruct((3, chunk, chunk), f32),
        compiler_params=pltpu.CompilerParams(vmem_limit_bytes=vmem_bytes),
        cost_estimate=cost(2),
        name="bias_tiles",
    )(head, table)


def table_sums(buckets, band_ref, far_ref, sums_ref):
    first, places = steps_of(buckets)
    edge = chunk // 2
    reach = -(-bucket_edges[-1] // 8) * 8
    sums_ref[...] = jnp.zeros_like(sums_ref)
    relative = [relative_tile(j) for j in (-1, 0, 1)]

    def fold(tile):
        return jnp.sum(tile.reshape(-1, 8, tile.shape[1]), axis=0)

    above = fold(band_ref[0]) + fold(band_ref[1]) + fold(band_ref[2])
    for q in range(far_ref.shape[2] // chunk):
        spot = slice(q * chunk, (q + 1) * chunk)
        above = above + far_ref[0, :, spot] * 0.125 + far_ref[1, :, spot] * 0.125
    right = fold(band_ref[2])
    for q in range(far_ref.shape[2] // chunk):
        right = right + far_ref[1, :, q * chunk : (q + 1) * chunk] * 0.125
    corner = band_ref[2, :reach, edge:]
    corner_relative = relative[2][:reach, edge:]
    left_corner = band_ref[0, chunk - reach :, :edge]
    left_relative = relative[0][chunk - reach :, :edge]
    bucket = first
    for place, following in places:
        if place > 0:
            after = right[:, :edge] + right[:, edge:]
            after = after - fold(jnp.where(corner_relative < place, corner, 0.0))
        else:
            after = right[:, :edge] + right[:, edge:]
            after = after + fold(jnp.where(left_relative >= place, left_corner, 0.0))
        part = fold(jnp.where(relative[1] >= place, band_ref[1], 0.0))
        after = after + part[:, :edge] + part[:, edge:]
        if above.shape[1] == chunk:
            above = above[:, :edge] + above[:, edge:]
        sums_ref[bucket : bucket + 1, :] = jnp.sum(above - after, axis=0, keepdims=True)
        above, bucket = after, following
    sums_ref[bucket : bucket + 1, :] = jnp.sum(above, axis=0, keepdims=True)
    found = jnp.sum(sums_ref[...], axis=1, keepdims=True)
    shape = (buckets, edge)
    spread = lax.broadcasted_iota(jnp.int32, shape, 0) == lax.broadcasted_iota(jnp.int32, shape, 1)
    return jnp.sum(jnp.where(spread, found, 0.0), axis=0, keepdims=True)


def table_pieces(found):
    high = found.astype(bf16).astype(f32)
    middle = (found - high).astype(bf16).astype(f32)
    pieces = [high, middle, found - high - middle, jnp.zeros((13, found.shape[1]), f32)]
    return jnp.concatenate(pieces, axis=0).astype(bf16)


def attend_kernel(
    size, blocks, docs, buckets, first, bounds_ref, head_ref, table_ref, taken_ref, band_ref, *refs
):
    sent_ref, context_ref, expo_ref, scale_ref, keys_ref, *scratch = refs[-5 - 2 * subs :]
    step = pl.program_id(0) + first
    chunks = blocks // 2
    tok = chunk // 2
    bounds = [bounds_ref[0]]
    for d in range(1, docs):
        bounds.append(bounds[-1] + bounds_ref[d])
    heads = table_ref.shape[0] // buckets
    entry = lambda bucket: table_ref[bucket * heads + head_ref[0]]

    @pl.when(step == first)
    def _():
        for s in range(blocks):
            position = s * tok + lax.broadcasted_iota(jnp.int32, (1, tok), 1)
            segment = segments_at(bounds, position)
            row = lax.broadcasted_iota(jnp.int32, (16, tok), 0)
            own = jnp.where(row == segment, 1.0, 0.0)
            part = jnp.where(row == s // 2, 1.0, 0.0)
            tall = jnp.concatenate(
                [
                    taken_ref[s, size : 2 * size, :].astype(f32),
                    own,
                    part,
                    jnp.zeros((size - 32, tok), f32),
                ],
                axis=0,
            )
            keys_ref[s * tok : (s + 1) * tok, :] = tall.T.astype(bf16)
        for query_ref in scratch[::2]:
            query_ref[size:, :] = jnp.zeros((size, chunk), bf16)

    def turned(block, d):
        c = block + d
        return jnp.where(c >= chunks, c - chunks, c)

    blocks_here = [step * subs + k for k in range(subs)]
    tops = []
    for k, block in enumerate(blocks_here):
        query_ref, score_ref = scratch[2 * k : 2 * k + 2]
        position = block * chunk + lax.broadcasted_iota(jnp.int32, (1, chunk), 1)
        segment = segments_at(bounds, position)
        row = lax.broadcasted_iota(jnp.int32, (16, chunk), 0)
        query_ref[:size, :] = tile_rows(taken_ref, block, 0, size)
        query_ref[size : size + 16, :] = jnp.where(row == segment, 0.0, masked_score).astype(bf16)
        far = jnp.where(
            row <= block - 2,
            entry(buckets // 2 - 1),
            jnp.where(row >= block + 2, entry(buckets - 1), 0.0),
        )
        query_ref[size + 16 : size + 32, :] = far.astype(bf16)
        query = query_ref[...]
        top = jnp.full((8, chunk), masked_score, f32)
        for d in range(chunks):
            spot = pl.ds(pl.multiple_of(turned(block, d) * chunk, chunk), chunk)
            scores = jnp.dot(keys_ref[spot, :], query, preferred_element_type=f32)
            if d == 0:
                scores = scores + band_ref[1]
            elif d == 1:
                scores = scores + jnp.where(block + 1 < chunks, 1.0, 0.0) * band_ref[2]
            elif d == chunks - 1:
                scores = scores + jnp.where(block >= 1, 1.0, 0.0) * band_ref[0]
            score_ref[d * chunk : (d + 1) * chunk, :] = scores
            top = jnp.maximum(top, jnp.max(scores.reshape(chunk // 8, 8, chunk), axis=0))
        tops.append(jnp.max(top, axis=0, keepdims=True))
    for k, block in enumerate(blocks_here):
        score_ref = scratch[2 * k + 1]
        lanes = slice(k * chunk, (k + 1) * chunk)
        total = jnp.zeros((8, chunk), f32)
        context = jnp.zeros((size, chunk), f32)
        for d in range(chunks):
            c = turned(block, d)
            expo = jnp.exp(score_ref[d * chunk : (d + 1) * chunk, :] - tops[k])
            total = total + jnp.sum(expo.reshape(chunk // 8, 8, chunk), axis=0)
            low = expo.astype(bf16)
            expo_ref[pl.ds(pl.multiple_of(c * chunk, chunk), chunk), lanes] = low
            context = context + jnp.dot(
                tile_rows(taken_ref, c, 2 * size, 3 * size), low, preferred_element_type=f32
            )
        scale = 1.0 / jnp.sum(total, axis=0, keepdims=True)
        context = context * scale
        context_ref[:, lanes] = context
        scale_ref[:, lanes] = scale
        sent_ref[2 * k] = context[:, :tok].astype(bf16)
        sent_ref[2 * k + 1] = context[:, tok:].astype(bf16)


def attend(taken, lengths, head, table, band, buckets, first, stop, given, *after):
    blocks, size, tok = taken.shape
    size = size // 3
    length = blocks * tok
    smem = pl.BlockSpec(memory_space=pltpu.SMEM)
    return pl.pallas_call(
        functools.partial(attend_kernel, size, blocks, lengths.shape[0], buckets, first),
        grid=((stop or blocks // 2 // subs) - first,),
        in_specs=[
            smem,
            smem,
            smem,
            pl.BlockSpec((blocks, 3 * size, tok), lambda q: (0, 0, 0)),
            pl.BlockSpec((3, chunk, chunk), lambda q: (0, 0, 0)),
        ]
        + [pl.BlockSpec(memory_space=pl.ANY)] * (len(given) + len(after)),
        out_specs=[
            pl.BlockSpec((2 * subs, size, tok), lambda q: (first + q, 0, 0)),
            pl.BlockSpec((size, subs * chunk), lambda q: (0, first + q)),
            pl.BlockSpec((length, subs * chunk), lambda q: (0, first + q)),
            pl.BlockSpec((1, subs * chunk), lambda q: (0, first + q)),
        ],
        out_shape=[
            jax.ShapeDtypeStruct((blocks, size, tok), bf16),
            jax.ShapeDtypeStruct((size, length), f32),
            jax.ShapeDtypeStruct((length, length), bf16),
            jax.ShapeDtypeStruct((1, length), f32),
        ],
        scratch_shapes=[
            pltpu.VMEM((length, 2 * size), bf16),
        ]
        + [
            pltpu.VMEM((2 * size, chunk), bf16),
            pltpu.VMEM((length, chunk), f32),
        ]
        * subs,
        compiler_params=pltpu.CompilerParams(vmem_limit_bytes=vmem_bytes),
        input_output_aliases={5 + k: k for k in range(len(given))},
        cost_estimate=cost(6),
        name="attend",
    )(lengths, head, table, taken, band, *given, *after)


def attend_back_kernel(
    size, blocks, buckets, last, after, taken_ref, grad_ref, context_ref, expo_ref, scale_ref,
    *refs,
):
    before_ref, *refs = refs
    (
        sent_ref, found_ref, band_ref, far_ref, sums_ref,
        queries_ref, wide_ref, delta_ref, grad_queries_ref, grad_scores_ref,
    ) = refs[after:]
    step = pl.program_id(0)
    chunks = blocks // 2
    tok = chunk // 2

    @pl.when(step == 0)
    def _():
        for s in range(blocks):
            spot = slice(s * tok, (s + 1) * tok)
            scaled = grad_ref[s].astype(f32) * scale_ref[:, spot]
            wide_ref[:, spot] = scaled.astype(bf16)
            delta_ref[:, spot] = jnp.sum(scaled * context_ref[:, spot], axis=0, keepdims=True)
            queries_ref[:, spot] = taken_ref[s, :size, :]
        grad_queries_ref[...] = jnp.zeros_like(grad_queries_ref)
        band_ref[...] = jnp.zeros_like(band_ref)
        far_ref[...] = jnp.zeros_like(far_ref)
        for k in range(subs):
            grad_scores_ref[k, :, :chunk] = jnp.zeros((chunk, chunk), bf16)
            grad_scores_ref[k, :, (chunks + 1) * chunk :] = jnp.zeros((chunk, chunk), bf16)

    keys = []
    for k in range(subs):
        c = step * subs + k
        rows = slice(k * chunk, (k + 1) * chunk)
        values = tile_rows(taken_ref, c, 2 * size, 3 * size).astype(f32).T.astype(bf16)
        for q in range(chunks):
            spot = slice(q * chunk, (q + 1) * chunk)
            grad_weights = jnp.dot(values, wide_ref[:, spot], preferred_element_type=f32)
            weights = expo_ref[rows, spot].astype(f32)
            grad_scores = (weights * (grad_weights - delta_ref[:, spot])).astype(bf16)
            grad_scores_ref[k, :, (q + 1) * chunk : (q + 2) * chunk] = grad_scores
        grad_values = dot_on(wide_ref[...], expo_ref[rows, :], 1, 1).astype(bf16)
        grad_keys = dot_on(
            queries_ref[...], grad_scores_ref[k, :, chunk : (chunks + 1) * chunk], 1, 1
        ).astype(bf16)
        for t in range(2):
            sent_ref[2 * c + t, size : 2 * size, :] = grad_keys[:, t * tok : (t + 1) * tok]
            sent_ref[2 * c + t, 2 * size : 3 * size, :] = grad_values[:, t * tok : (t + 1) * tok]
        keys.append(
            jnp.concatenate(
                [tile_rows(taken_ref, c, size, 2 * size), jnp.ones((16, chunk), bf16)], axis=0
            )
        )
    for q in range(chunks):
        spot = slice(q * chunk, (q + 1) * chunk)
        total = grad_queries_ref[:, spot]
        for k in range(subs):
            c = step * subs + k
            part = jnp.dot(
                keys[k],
                grad_scores_ref[k, :, (q + 1) * chunk : (q + 2) * chunk],
                preferred_element_type=f32,
            )
            total = total + part[:size]
            sums = part[size : size + 8]
            far_ref[0, :, spot] = far_ref[0, :, spot] + jnp.where(c <= q - 2, sums, 0.0)
            far_ref[1, :, spot] = far_ref[1, :, spot] + jnp.where(c >= q + 2, sums, 0.0)
        grad_queries_ref[:, spot] = total
    for k in range(subs):
        c = step * subs + k
        for j in (-1, 0, 1):
            spot = pl.ds(pl.multiple_of((c - j + 1) * chunk, chunk), chunk)
            band_ref[j + 1] = band_ref[j + 1] + grad_scores_ref[k, :, spot].astype(f32)

    @pl.when(step == chunks // subs - 1)
    def _():
        for s in range(blocks):
            sent_ref[s, :size, :] = grad_queries_ref[:, s * tok : (s + 1) * tok].astype(bf16)
        found = before_ref[...] + table_sums(buckets, band_ref, far_ref, sums_ref)
        found_ref[...] = found
        if last:
            pieces = table_pieces(found)
            for s in range(blocks):
                sent_ref[s, 3 * size :, :] = pieces


def attend_back(taken, grads, context, expo, scale, buckets, m, last, before, *after):
    blocks, size, _ = grads.shape
    tok = taken.shape[2]
    length = expo.shape[0]
    height = 3 * size + 16 if last else 3 * size
    return pl.pallas_call(
        functools.partial(attend_back_kernel, size, blocks, buckets, last, len(after)),
        grid=(blocks // 2 // subs,),
        in_specs=[
            pl.BlockSpec((blocks, 3 * size, tok), lambda c: (0, 0, 0)),
            pl.BlockSpec((blocks, size, tok), lambda c: (0, 0, m)),
            pl.BlockSpec((size, length), lambda c: (0, 0)),
            pl.BlockSpec((subs * chunk, length), lambda c: (c, 0)),
            pl.BlockSpec((1, length), lambda c: (0, 0)),
            pl.BlockSpec((1, chunk // 2), lambda c: (0, 0)),
        ]
        + [pl.BlockSpec(memory_space=pl.ANY)] * len(after),
        out_specs=[
            pl.BlockSpec((blocks, height, tok), lambda c: (0, 0, 0)),
            pl.BlockSpec((1, chunk // 2), lambda c: (0, 0)),
        ],
        out_shape=[
            jax.ShapeDtypeStruct((blocks, height, tok), bf16),
            jax.ShapeDtypeStruct((1, chunk // 2), f32),
        ],
        scratch_shapes=[
            pltpu.VMEM((3, chunk, chunk), f32),
            pltpu.VMEM((2, 8, length), f32),
            pltpu.VMEM((buckets, chunk // 2), f32),
            pltpu.VMEM((size, length), bf16),
            pltpu.VMEM((size, length), bf16),
            pltpu.VMEM((1, length), f32),
            pltpu.VMEM((size, length), f32),
            pltpu.VMEM((subs, chunk, length + 2 * chunk), bf16),
        ],
        compiler_params=pltpu.CompilerParams(vmem_limit_bytes=vmem_bytes),
        cost_estimate=cost(13),
        name="attend_back",
    )(taken, grads, context, expo, scale, before, *after)


def feed_kernel(
    heads, steps, micro, flipped_ref, matrix_ref, hidden_ref, given_ref, gain_ref, *refs
):
    contexts, refs = refs[:micro], refs[micro:]
    outs, gates, ups, downs = (refs[2 * k : 2 * k + 2] for k in range(4))
    (
        result_ref, grad_mid_ref, grad_context_ref, packet_ref, left_ref, other_left_ref,
        normed_ref, branch_ref, cot_ref, mid_ref, total_ref, grad_ref,
    ) = refs[-12:]
    units = steps * feed_chunk
    j = pl.program_id(0)
    size = contexts[0].shape[1]
    sides = side(flipped_ref[0], hidden_ref.shape[1] // 2)

    @pl.when(j == 0)
    def _():
        cot_ref[...] = jnp.dot(
            given_ref[...], matrix_ref[...], preferred_element_type=f32
        ).astype(bf16)
        context = jnp.concatenate(
            [ref[...].reshape(-1, ref.shape[2]).astype(f32).T for ref in contexts], axis=0
        ).astype(bf16)
        packet_ref[:, 3 * units :] = context
        context = context[:, : heads * size]
        for lanes, ref in zip(sides, outs):
            mid_ref[:, lanes] = dot_on(context, ref[...], 1, 1)
        mid = hidden_ref[...].astype(f32) + mid_ref[...]
        mid_ref[...] = mid
        total_ref[...] = mid
        normed_ref[...] = rms_norm(mid, gain_ref[...]).astype(bf16)
        grad_ref[...] = jnp.zeros_like(grad_ref)

    def over_width(left_ref, rights):
        own, other = (
            jnp.dot(left_ref[:, lanes], ref[...], preferred_element_type=f32)
            for lanes, ref in zip(sides, rights)
        )
        return own + other

    gate = over_width(normed_ref, gates)
    up = over_width(normed_ref, ups)
    grad_inner = over_width(cot_ref, downs)
    slope = 0.7978845608028654
    square = gate * gate
    bent = jnp.tanh(slope * (gate + 0.044715 * (square * gate)))
    half = 0.5 * (1.0 + bent)
    gelu = gate * half
    gelu_grad = half + (0.5 * gate) * (1.0 - bent * bent) * (
        slope * (1.0 + (3 * 0.044715) * square)
    )
    inner = (gelu * up).astype(bf16)
    grad_gate = (grad_inner * up * gelu_grad).astype(bf16)
    grad_up = (grad_inner * gelu).astype(bf16)
    for k, part in enumerate((grad_gate, grad_up, inner)):
        packet_ref[
            :, pl.ds(pl.multiple_of(k * units + j * feed_chunk, feed_chunk), feed_chunk)
        ] = part
    for k, lanes in enumerate(sides):
        total_ref[:, lanes] = total_ref[:, lanes] + dot_on(inner, downs[k][...], 1, 1)
        grad_ref[:, lanes] = (
            grad_ref[:, lanes]
            + dot_on(grad_gate, gates[k][...], 1, 1)
            + dot_on(grad_up, ups[k][...], 1, 1)
        )

    @pl.when(j == steps - 1)
    def _():
        result_ref[...] = dot_on(total_ref[...].astype(bf16), matrix_ref[...], 1, 1).astype(bf16)
        mid = mid_ref[...]
        scale = lax.rsqrt(jnp.mean(mid * mid, axis=-1, keepdims=True) + norm_eps)
        grad_normed = grad_ref[...]
        gained = grad_normed * gain_ref[...]
        inward = jnp.mean(gained * mid, axis=-1, keepdims=True)
        grad_mid = cot_ref[...].astype(f32) + scale * gained - mid * (scale * scale * scale * inward)
        grad_mid_ref[...] = grad_mid
        branch_ref[...] = grad_mid.astype(bf16)
        grad_context = over_width(branch_ref, outs).T.astype(bf16)
        grad_context_ref[...] = jnp.zeros_like(grad_context_ref)
        for h in range(heads):
            grad_context_ref[h] = grad_context[h * size : (h + 1) * size, :]
        own, other = sides
        half = hidden_ref.shape[1] // 2
        for k, ref in enumerate((normed_ref, cot_ref, branch_ref)):
            left_ref[:, k * half : (k + 1) * half] = ref[:, own]
            other_left_ref[:, k * half : (k + 1) * half] = ref[:, other]


def feed(flipped, matrix, hidden, contexts, cot, gain, weights, heads, *after):
    tok, width = hidden.shape
    blocks, size, _ = contexts[0].shape
    micro = len(contexts)
    inner_width = heads * size
    units = (weights[0].shape[1] - inner_width) // 3
    steps = units // feed_chunk
    assert 3 * units % inner_width == 0
    whole = lambda *shape: pl.BlockSpec(shape, lambda j: (0,) * len(shape))
    column = lambda offset: pl.BlockSpec((width // 2, feed_chunk), lambda j: (0, offset + j))
    packet = 3 * units + blocks * size
    spot = 3 * units // inner_width
    weight_specs = [pl.BlockSpec((width // 2, inner_width), lambda j: (0, spot))] * 2
    for k in range(3):
        weight_specs += [column(k * steps)] * 2
    return pl.pallas_call(
        functools.partial(feed_kernel, heads, steps, micro),
        grid=(steps,),
        in_specs=[
            pl.BlockSpec(memory_space=pltpu.SMEM),
            whole(width, width),
            whole(tok, width),
            whole(tok, width),
            whole(1, width),
            *[whole(*context.shape) for context in contexts],
            *weight_specs,
        ]
        + [pl.BlockSpec(memory_space=pl.ANY)] * len(after),
        out_specs=[
            whole(tok, width),
            whole(tok, width),
            whole(blocks, size, tok),
            whole(tok, packet),
            whole(tok, 3 * (width // 2)),
            whole(tok, 3 * (width // 2)),
        ],
        out_shape=[
            jax.ShapeDtypeStruct((tok, width), bf16),
            jax.ShapeDtypeStruct((tok, width), f32),
            jax.ShapeDtypeStruct((blocks, size, tok), bf16),
            jax.ShapeDtypeStruct((tok, packet), bf16),
            jax.ShapeDtypeStruct((tok, 3 * (width // 2)), bf16),
            jax.ShapeDtypeStruct((tok, 3 * (width // 2)), bf16),
        ],
        scratch_shapes=[pltpu.VMEM((tok, width), bf16)] * 3 + [pltpu.VMEM((tok, width), f32)] * 3,
        compiler_params=pltpu.CompilerParams(vmem_limit_bytes=vmem_bytes),
        cost_estimate=cost(8),
        name="feed",
    )(flipped, matrix, hidden, cot, gain, *contexts, *weights * 4, *after)


def store_tall(ref, parts):
    for m, part in enumerate(parts):
        tok = part.shape[0]
        ref[:, m * tok : (m + 1) * tok] = part.astype(f32).T.astype(bf16)


def weight_grad_kernel(counts, parts, half, *refs):
    j = pl.program_id(0)
    out_ref, tall_ref = refs[-2:]
    lefts, rights = refs[:parts], refs[parts : 2 * parts]
    start = 0
    for k, count in counts:

        @pl.when(j == start)
        def _(k=k):
            store_tall(tall_ref, [ref[:, k * half : (k + 1) * half] for ref in lefts])

        start += count
    right = jnp.concatenate([ref[...] for ref in rights], axis=0)
    out_ref[...] = jnp.dot(tall_ref[...], right, preferred_element_type=f32).astype(bf16)


def weight_grads(lefts, rights, half, units, inner_width, *after):
    tok, block = lefts[0].shape[0], grad_chunk
    steps = units // block
    counts = [(0, 2 * steps), (1, steps), (2, inner_width // block)]
    total = 3 * steps + inner_width // block
    anywhere = pl.BlockSpec(memory_space=pl.ANY)
    return pl.pallas_call(
        functools.partial(weight_grad_kernel, counts, len(lefts), half),
        grid=(total,),
        in_specs=[pl.BlockSpec((tok, 3 * half), lambda j: (0, 0))] * len(lefts)
        + [pl.BlockSpec((tok, block), lambda j: (0, j))] * len(rights)
        + [anywhere] * len(after),
        out_specs=pl.BlockSpec((half, block), lambda j: (0, j)),
        out_shape=jax.ShapeDtypeStruct((half, total * block), bf16),
        scratch_shapes=[pltpu.VMEM((half, len(lefts) * tok), bf16)],
        compiler_params=pltpu.CompilerParams(vmem_limit_bytes=vmem_bytes),
        cost_estimate=cost(10),
        name="weight_grads",
    )(*lefts, *rights, *after)


def project_kernel(
    heads, flipped_ref, matrix_ref, inputs_ref, own_ref, other_ref, after_ref, *refs
):
    micro, tok, width = inputs_ref.shape
    sent, (tokens_ref, normed_ref, gain_a_ref, gain_f_ref, gains_ref) = refs[:micro], refs[micro:]
    inner_width = (own_ref.shape[1] - 128) // 3
    size = inner_width // heads
    sides = side(flipped_ref[0], width // 2)
    for lanes, ref in zip(sides, (own_ref, other_ref)):
        gains_ref[:, lanes] = ref[:, 3 * inner_width :].astype(f32).T[:8]
    gain_a_ref[...] = gains_ref[:1]
    gain_f_ref[...] = gains_ref[1:2]
    hidden = jnp.dot(
        inputs_ref[...].reshape(micro * tok, width), matrix_ref[...], preferred_element_type=f32
    )
    tokens_ref[...] = hidden.astype(bf16).reshape(micro, tok, width)
    normed_ref[...] = rms_norm(hidden, gains_ref[:1]).astype(bf16)
    for ref in sent:
        ref[heads:] = jnp.zeros((ref.shape[0] - heads,) + ref.shape[1:], bf16)
    for k in range(3):
        for half in range(2):
            start = k * inner_width + half * (inner_width // 2)
            own, other = (
                jnp.dot(
                    normed_ref[:, lanes],
                    ref[:, start : start + inner_width // 2],
                    preferred_element_type=f32,
                )
                for lanes, ref in zip(sides, (own_ref, other_ref))
            )
            part = (own + other).T.astype(bf16)
            for h in range(heads // 2):
                for m, ref in enumerate(sent):
                    ref[half * (heads // 2) + h, k * size : (k + 1) * size, :] = part[
                        h * size : (h + 1) * size, m * tok : (m + 1) * tok
                    ]


def project(flipped, matrix, inputs, weights, heads, blocks, after):
    micro, tok, width = inputs.shape
    size = (weights[0].shape[1] - 128) // 3 // heads
    vmem = pl.BlockSpec(memory_space=pltpu.VMEM)
    outs = pl.pallas_call(
        functools.partial(project_kernel, heads),
        in_specs=[
            pl.BlockSpec(memory_space=pltpu.SMEM),
            vmem,
            vmem,
            vmem,
            vmem,
            pl.BlockSpec(memory_space=pl.ANY),
        ],
        out_shape=[jax.ShapeDtypeStruct((blocks, 3 * size, tok), bf16)] * micro
        + [
            jax.ShapeDtypeStruct((micro, tok, width), bf16),
            jax.ShapeDtypeStruct((micro * tok, width), bf16),
            jax.ShapeDtypeStruct((1, width), f32),
            jax.ShapeDtypeStruct((1, width), f32),
        ],
        scratch_shapes=[pltpu.VMEM((8, width), f32)],
        compiler_params=pltpu.CompilerParams(vmem_limit_bytes=few_bytes),
        cost_estimate=cost(3),
        name="project",
    )(flipped, matrix, inputs, *weights, after)
    return outs[:micro], *outs[micro:]


def lined(refs, heads, size, lined_ref):
    tok = refs[0].shape[2]
    for m, ref in enumerate(refs):
        for k in range(3):
            for h in range(heads):
                start = (k * heads + h) * size
                lined_ref[start : start + size, m * tok : (m + 1) * tok] = ref[
                    h, k * size : (k + 1) * size, :
                ]


def input_grad_kernel(heads, micro, *refs):
    flipped_ref, matrix_ref, inputs_ref, own_weights, other_weights, gains_ref = refs[:6]
    mid_ref, *grads = refs[6 : 7 + micro]
    input_grad_ref, wide_ref, lined_ref = refs[-3:]
    tok, width = inputs_ref.shape[1:]
    inner_width = (own_weights.shape[1] - 128) // 3
    sides = side(flipped_ref[0], width // 2)
    lined(grads, heads, inner_width // heads, lined_ref)
    for ref, rows in zip((own_weights, other_weights), sides):
        wide_ref[rows, :] = jnp.dot(
            ref[:, : 3 * inner_width], lined_ref[...], preferred_element_type=f32
        )
    gain = gains_ref[...]
    for m in range(micro):
        grad = wide_ref[:, m * tok : (m + 1) * tok].T
        hidden = inputs_ref[m].astype(f32)
        scale = lax.rsqrt(jnp.mean(hidden * hidden, axis=-1, keepdims=True) + norm_eps)
        gained = grad * gain
        inward = jnp.mean(gained * hidden, axis=-1, keepdims=True)
        found = mid_ref[m * tok : (m + 1) * tok, :] + scale * gained - hidden * (scale * scale * scale * inward)
        high = found.astype(bf16)
        rest = found - high.astype(f32)
        middle = rest.astype(bf16)
        low = (rest - middle.astype(f32)).astype(bf16)
        input_grad_ref[m] = sum(
            dot_on(part, matrix_ref[...], 1, 1) for part in (low, middle, high)
        )


def input_grads(flipped, matrix, inputs, weights, gains, grads, mid, heads, *after):
    micro, tok, width = inputs.shape
    inner_width = (weights[0].shape[1] - 128) // 3
    vmem = pl.BlockSpec(memory_space=pltpu.VMEM)
    return pl.pallas_call(
        functools.partial(input_grad_kernel, heads, micro),
        in_specs=[pl.BlockSpec(memory_space=pltpu.SMEM)]
        + [vmem] * (6 + micro)
        + [pl.BlockSpec(memory_space=pl.ANY)] * len(after),
        out_shape=jax.ShapeDtypeStruct((micro, tok, width), f32),
        scratch_shapes=[
            pltpu.VMEM((width, micro * tok), f32),
            pltpu.VMEM((3 * inner_width, micro * tok), bf16),
        ],
        compiler_params=pltpu.CompilerParams(vmem_limit_bytes=few_bytes),
        cost_estimate=cost(6),
        name="input_grads",
    )(flipped, matrix, inputs, *weights, gains, mid, *grads, *after)


def front_grad_kernel(heads, parts, half, which, *refs):
    flipped_ref = refs[0]
    lefts, grads = refs[1 : 1 + parts], refs[1 + parts : 1 + 2 * parts]
    out_ref, tall_ref, lined_ref = refs[-3:]
    _, size, tok = grads[0].shape

    @pl.when(pl.program_id(0) == 0)
    def _():
        lanes = side(flipped_ref[0], half)[which]
        for p, ref in enumerate(lefts):
            tall = ref[:, lanes].astype(f32).T.astype(bf16)
            tall_ref[:, p * tok : (p + 1) * tok] = tall

    for p, ref in enumerate(grads):
        lined_ref[:, p * tok : (p + 1) * tok] = ref[:heads].reshape(heads * size, tok)
    out_ref[...] = dot_on(tall_ref[...], lined_ref[...], 1, 1).astype(bf16)


def front_grads(flipped, lefts, grads, inner_width, heads, which):
    tok, width = lefts[0].shape
    parts = len(lefts)
    part = pl.BlockSpec((grads[0].shape[0], inner_width // heads, tok), lambda k: (0, k, 0))
    return pl.pallas_call(
        functools.partial(front_grad_kernel, heads, parts, width // 2, which),
        grid=(3,),
        in_specs=[pl.BlockSpec(memory_space=pltpu.SMEM)]
        + [pl.BlockSpec((tok, width), lambda k: (0, 0))] * parts
        + [part] * parts,
        out_specs=pl.BlockSpec((width // 2, inner_width), lambda k: (0, k)),
        out_shape=jax.ShapeDtypeStruct((width // 2, 3 * inner_width), bf16),
        scratch_shapes=[
            pltpu.VMEM((width // 2, parts * tok), bf16),
            pltpu.VMEM((inner_width, parts * tok), bf16),
        ],
        compiler_params=pltpu.CompilerParams(vmem_limit_bytes=few_bytes),
        cost_estimate=cost(5),
        name="front_grads",
    )(flipped, *lefts, *grads)


def row_of(column):
    share = column.shape[0]
    shape = (share, share)
    spread = lax.broadcasted_iota(jnp.int32, shape, 0) == lax.broadcasted_iota(jnp.int32, shape, 1)
    return jnp.sum(jnp.where(spread, column, 0.0), axis=0, keepdims=True)


def gain_grad_of(weights, grads, gain_ref):
    total = sum(
        jnp.sum(weight[...].astype(f32) * grad[...], axis=1, keepdims=True)
        for weight, grad in zip(weights, grads)
    )
    return row_of(total) / gain_ref[...].astype(f32)


def unpack_back_kernel(sums_ref, gate_ref, up_ref, gain_ref, *refs):
    gate_grad_ref, up_grad_ref, down_grad_ref, out_grad_ref, gain_grad_ref = refs
    units = gate_ref.shape[1]
    for k, ref in enumerate((gate_grad_ref, up_grad_ref, down_grad_ref, out_grad_ref)):
        ref[...] = sums_ref[:, k * units : k * units + ref.shape[1]].astype(f32)
    gain_grad_ref[...] = gain_grad_of((gate_ref, up_ref), (gate_grad_ref, up_grad_ref), gain_ref)


def unpack_back(sums, w_gate, w_up, gain, inner_width):
    share, units = w_gate.shape
    shapes = [(share, units)] * 3 + [(share, inner_width), (1, share)]
    gate, up, down, out, gain_grad = pl.pallas_call(
        unpack_back_kernel,
        out_shape=[jax.ShapeDtypeStruct(shape, f32) for shape in shapes],
        compiler_params=pltpu.CompilerParams(vmem_limit_bytes=few_bytes),
        name="unpack_back",
    )(sums, w_gate, w_up, gain[None, :])
    return gate, up, down.T, out.T, gain_grad[0]


def unpack_front_kernel(parts_ref, query_ref, key_ref, value_ref, gain_ref, after_ref, *refs):
    grads, gain_grad_ref = refs[:3], refs[3]
    width = query_ref.shape[1]
    for k, ref in enumerate(grads):
        part = parts_ref[:, :, k * width : (k + 1) * width].astype(f32)
        ref[...] = jnp.sum(part, axis=0)
    gain_grad_ref[...] = gain_grad_of((query_ref, key_ref, value_ref), grads, gain_ref)


def unpack_front(parts, w_query, w_key, w_value, gain, after):
    share, width = w_query.shape
    vmem = pl.BlockSpec(memory_space=pltpu.VMEM)
    shapes = [(share, width)] * 3 + [(1, share)]
    query, key, value, gain_grad = pl.pallas_call(
        unpack_front_kernel,
        in_specs=[vmem] * 5 + [pl.BlockSpec(memory_space=pl.ANY)],
        out_shape=[jax.ShapeDtypeStruct(shape, f32) for shape in shapes],
        compiler_params=pltpu.CompilerParams(vmem_limit_bytes=few_bytes),
        name="unpack_front",
    )(parts, w_query, w_key, w_value, gain[None, :], after)
    return query, key, value, gain_grad[0]


def body(
    inputs, doc_lengths, attn_gain, w_query, w_key, w_value, w_out, ff_gain,
    w_gate, w_up, w_down, rel_table, cotangent,
):
    micro, _, tok, width = inputs.shape
    inner_width = w_query.shape[1]
    hidden_units = w_gate.shape[1]
    buckets, heads = rel_table.shape
    size = inner_width // heads
    blocks = lax.axis_size("blk")
    rows = lax.axis_size("rows")
    me = lax.axis_index("blk")
    share = w_query.shape[0]
    micros = range(micro)

    flipped = lax.axis_index("rows") if staged(rows, blocks, share) else 0
    flipped = jnp.full((1,), flipped, jnp.int32)
    matrix = stage_matrix(rows, blocks, share)
    head = jnp.minimum(me, heads - 1).astype(jnp.int32).reshape(1)
    table = rel_table.astype(f32).reshape(-1)

    with jax.named_scope("weights"):
        front_full = gather_front(w_query, w_key, w_value, attn_gain, ff_gain)
        back_own = gather_back(jnp.concatenate([w_gate, w_up, w_down.T, w_out.T], axis=1), front_full[0])

    band = bias_tiles(head, table, buckets)
    sent, tokens, normed_a, gain_a, gain_f = project(
        flipped, matrix, inputs[:, 0], front_full, heads, blocks, band
    )
    taken = []
    for m in micros:
        with jax.named_scope("project"):
            part = tie(sent[m], taken[-1]) if m else sent[m]
            taken.append(lax.all_to_all(part, "blk", 0, 0, tiled=True))

    kept, contexts, half = [], [], blocks // 4 // subs
    for m in micros:
        given = taken[m], doc_lengths[m, 0], head, table, band, buckets
        outs = [k[0] for k in kept]
        if m:
            outs = attend(*given, 0, half, [], *outs)
            outs = attend(*given, half, None, outs, *contexts)
        else:
            outs = attend(*given, 0, None, [])
        kept.append(outs[1:])
        with jax.named_scope("context"):
            contexts.append(lax.all_to_all(outs[0], "blk", 0, 0, tiled=True))
    with jax.named_scope("weights"):
        back_full = gather_other(back_own, outs[0])

    fits = staged(rows, blocks, share)
    here = micro * tok
    result, grad_mid, grad_context, mine, left, left_other = feed(
        flipped, matrix, tokens.reshape(here, width), contexts,
        cotangent[:, 0].reshape(here, width), gain_f, back_full, heads,
    )
    with jax.named_scope("grad_context"):
        grads = lax.all_to_all(grad_context, "blk", 0, 0, tiled=True)
    if fits:
        with jax.named_scope("packet"):
            packet, near_left = flip(mine, "rows", 1), flip(left_other, "rows", 1)

    wide = blocks * size
    with jax.named_scope("back_grads"):
        sizes = width // 2, hidden_units, wide
        if fits:
            parts = [left, near_left], [mine, packet]
            own = tie(weight_grads(*parts, *sizes), grads)
            back_grad = scatter_back(own)
        else:
            own, other = (weight_grads([lefts], [mine], *sizes) for lefts in (left, left_other))
            back_grad = scatter_whole(own, other)
    grad_qkv, found = [], jnp.zeros((1, chunk // 2), f32)
    for m in micros:
        returned, found = attend_back(
            taken[m], grads, *kept[m], buckets, m, m == micro - 1, found, own
        )
        with jax.named_scope("grad_qkv"):
            returned = tie(returned, *grad_qkv) if m else returned
            grad_qkv.append(lax.all_to_all(returned, "blk", 0, 0, tiled=True))

    with jax.named_scope("table"):
        pieces = grad_qkv[-1][:heads, 3 * size : 3 * size + 3, :buckets]
        table_grad = jnp.sum(pieces.astype(f32), axis=1).T
        for bit in bits_of(rows):
            table_grad = table_grad + flip(table_grad, "rows", bit)

    with jax.named_scope("front_grads"):
        normed = [normed_a[m * tok : (m + 1) * tok] for m in micros]
        if fits:
            near_grads = [flip(g, "rows", 1) for g in grad_qkv]
            near_normed = [flip(n, "rows", 1) for n in normed]
            own = front_grads(
                flipped, normed + near_normed, grad_qkv + near_grads, inner_width, heads, 0
            )
            back_grad = scatter_back_end(back_grad, own)
            front_parts = scatter_front(own, share)
        else:
            own, other = (
                front_grads(flipped, normed, grad_qkv, inner_width, heads, which)
                for which in (0, 1)
            )
            front_parts = scatter_whole(own, other)[None]
    input_grad = input_grads(
        flipped, matrix, tokens, front_full, gain_a, grad_qkv, grad_mid, heads, own
    )
    if fits:
        with jax.named_scope("front_grads"):
            front_parts = scatter_front_end(front_parts, share, input_grad)
    gate_grad, up_grad, down_grad, out_grad, ff_gain_grad = unpack_back(
        back_grad, w_gate, w_up, ff_gain, inner_width
    )
    query_grad, key_grad, value_grad, attn_gain_grad = unpack_front(
        front_parts, w_query, w_key, w_value, attn_gain, gate_grad
    )

    return (
        result.reshape(micro, 1, tok, width),
        input_grad[:, None],
        attn_gain_grad,
        query_grad,
        key_grad,
        value_grad,
        out_grad,
        ff_gain_grad,
        gate_grad,
        up_grad,
        down_grad,
        table_grad,
    )


def solution(mesh):
    weight_rows = P(both, None)
    weight_columns = P(None, both)
    tokens = P(None, "rows", "blk", None)
    in_specs = (
        tokens, P(None, "rows", None), P(both), weight_rows, weight_rows, weight_rows,
        weight_columns, P(both), weight_rows, weight_rows, weight_columns, P(), tokens,
    )
    out_specs = (
        tokens, tokens, P(both), weight_rows, weight_rows, weight_rows,
        weight_columns, P(both), weight_rows, weight_rows, weight_columns, P(),
    )
    return jax.shard_map(body, mesh=mesh, in_specs=in_specs, out_specs=out_specs, check_vma=False)
```

```python
import functools

import jax
import jax.numpy as jnp
import numpy as np
from jax import lax
from jax.experimental import pallas as pl
from jax.experimental.pallas import tpu as pltpu
from jax.sharding import PartitionSpec as P

bucket_edges = (12, 16, 23, 32, 46, 64, 91)
norm_eps = 1e-06
masked_score = -1e30
f32 = jnp.float32
bf16 = jnp.bfloat16
both = ("rows", "blk")
chunk = 256
feed_chunk = 512
grad_chunk = 1024
subs = 2
vmem_bytes = 56 * 1024 * 1024
few_bytes = 24 * 1024 * 1024


def bucket_of(relative, total_buckets):
    half = total_buckets // 2
    exact = half // 2
    distance = jnp.abs(relative)
    far_bucket = exact + sum(((distance >= edge).astype(jnp.int32) for edge in bucket_edges))
    return jnp.where(relative > 0, half, 0) + jnp.where(distance < exact, distance, far_bucket)


def rms_norm(hidden, gain):
    return hidden * lax.rsqrt(jnp.mean(hidden * hidden, axis=-1, keepdims=True) + norm_eps) * gain


def gated(gate, up):
    return jax.nn.gelu(gate, approximate=True) * up


def dot_on(left, right, left_dim, right_dim):
    return lax.dot_general(
        left, right, (((left_dim,), (right_dim,)), ((), ())), preferred_element_type=f32
    )


def flip(array, axis, bit):
    count = lax.axis_size(axis)
    return lax.ppermute(array, axis, [(i, i ^ bit) for i in range(count)])


def bits_of(count):
    return [1 << k for k in range(count.bit_length() - 1)]


def segments_at(bounds, positions):
    total = jnp.zeros(positions.shape, jnp.int32)
    for bound in bounds:
        total = total + (positions >= bound).astype(jnp.int32)
    return total


def groups_of(blocks):
    near = 4
    far = blocks // near
    across = [[f * near + n for f in range(far)] for n in range(near)]
    within = [[f * near + n for n in range(near)] for f in range(far)]
    return far, near, across, within


def staged(rows, blocks, share):
    return rows == 2 and blocks % 4 == 0 and share % 8 == 0


def stage_matrix(rows, blocks, share):
    place = np.arange(rows * blocks * share)
    taken = place
    if staged(rows, blocks, share):
        far, near, _, _ = groups_of(blocks)
        slab = place // share
        half, inner = slab // blocks, slab % blocks
        taken = (half * blocks + inner % far * near + inner // far) * share + place % share
    return jnp.asarray((place[:, None] == taken[None, :]).astype(np.float32), bf16)


def tie_kernel(*refs):
    pass


def tie(value, *after):
    space = pl.BlockSpec(memory_space=pl.ANY)
    return pl.pallas_call(
        tie_kernel,
        in_specs=[space] * (1 + len(after)),
        out_specs=space,
        out_shape=jax.ShapeDtypeStruct(value.shape, value.dtype),
        input_output_aliases={0: 0},
        name="tie",
    )(value, *after)


def exchange(array, groups):
    return lax.all_to_all(array, "blk", 0, 0, tiled=True, axis_index_groups=groups)


def halves_of_whole(whole):
    half = whole.shape[0] // 2
    return whole[:half], whole[half:]


def pack_kernel(query_ref, key_ref, value_ref, gain_a_ref, gain_f_ref, out_ref):
    share = query_ref.shape[0]
    spread = lax.broadcasted_iota(jnp.int32, (share, share), 0) == lax.broadcasted_iota(
        jnp.int32, (share, share), 1
    )
    lane = lax.broadcasted_iota(jnp.int32, (share, 128), 1)
    gains = jnp.zeros((share, 128), f32)
    for k, ref in enumerate((gain_a_ref, gain_f_ref)):
        column = jnp.where(spread, ref[...].astype(f32), 0.0)
        gains = jnp.where(lane == k, jnp.sum(column, axis=1, keepdims=True), gains)
    parts = [query_ref[...], key_ref[...], value_ref[...], gains.astype(bf16)]
    packed = jnp.concatenate(parts, axis=1)
    for copy in range(out_ref.shape[0]):
        out_ref[copy] = packed


def pack(query, key, value, gain_a, gain_f, copies):
    shape = (copies, query.shape[0], 3 * query.shape[1] + 128)
    return pl.pallas_call(
        pack_kernel,
        out_shape=jax.ShapeDtypeStruct(shape, bf16),
        compiler_params=pltpu.CompilerParams(vmem_limit_bytes=vmem_bytes),
        name="pack",
    )(query, key, value, gain_a[None, :], gain_f[None, :])


def gather_front(*parts):
    blocks, rows = lax.axis_size("blk"), lax.axis_size("rows")
    if not staged(rows, blocks, parts[0].shape[0]):
        shard = pack(*parts, 1)[0]
        return halves_of_whole(lax.all_gather(shard, both, axis=0, tiled=True))
    far, near, across, within = groups_of(blocks)
    packed = pack(*parts, far)
    first = exchange(packed.reshape(-1, packed.shape[2]), across)
    own = exchange(jnp.tile(first, (near, 1)), within)
    return own, flip(own, "rows", 1)


def gather_back(shard, after):
    blocks, rows = lax.axis_size("blk"), lax.axis_size("rows")
    if not staged(rows, blocks, shard.shape[0]):
        return lax.all_gather(shard, both, axis=0, tiled=True)
    far, near, across, within = groups_of(blocks)
    own = lax.all_gather(shard, "blk", axis=0, tiled=True, axis_index_groups=across)
    own = tie(own, after)
    return lax.all_gather(own, "blk", axis=0, tiled=True, axis_index_groups=within)


def gather_other(own, after):
    blocks, rows = lax.axis_size("blk"), lax.axis_size("rows")
    if not staged(rows, blocks, own.shape[0] // blocks):
        return halves_of_whole(own)
    own = tie(own, after)
    return own, flip(own, "rows", 1)


def scatter_front(own, share):
    far, near, _, within = groups_of(lax.axis_size("blk"))
    held = exchange(own, within).reshape(near, far * share, own.shape[1])
    return jnp.sum(held.astype(f32), axis=0).astype(bf16)


def scatter_front_end(held, share, *after):
    far, _, across, _ = groups_of(lax.axis_size("blk"))
    return exchange(tie(held, *after), across).reshape(far, share, held.shape[1])


def scatter_back(own):
    _, _, _, within = groups_of(lax.axis_size("blk"))
    return lax.psum_scatter(
        own, "blk", scatter_dimension=0, axis_index_groups=within, tiled=True
    )


def scatter_back_end(part, after):
    _, _, across, _ = groups_of(lax.axis_size("blk"))
    return lax.psum_scatter(
        tie(part, after), "blk", scatter_dimension=0, axis_index_groups=across, tiled=True
    )


def scatter_whole(own, other):
    whole = jnp.concatenate([own, other], axis=0)
    return lax.psum_scatter(whole, both, scatter_dimension=0, tiled=True)


def side(flipped, half):
    return (
        pl.ds(pl.multiple_of(flipped * half, half), half),
        pl.ds(pl.multiple_of((1 - flipped) * half, half), half),
    )


def cost(micros):
    return pl.CostEstimate(flops=int(micros * 1e9), bytes_accessed=0, transcendentals=0)


def tile_rows(ref, index, start, stop):
    return jnp.concatenate(
        [ref[2 * index, start:stop, :], ref[2 * index + 1, start:stop, :]], axis=1
    )


def steps_of(buckets):
    half = buckets // 2
    exact = half // 2
    lows = list(range(1, exact)) + [exact] + list(bucket_edges)
    places = [(1 - low, k) for k, low in reversed(list(enumerate(lows)))]
    return half - 1, places + [(low, half + 1 + k) for k, low in enumerate(lows)]


def relative_tile(j):
    shape = (chunk, chunk)
    return (
        lax.broadcasted_iota(jnp.int32, shape, 0)
        - lax.broadcasted_iota(jnp.int32, shape, 1)
        + j * chunk
    )


def bias_kernel(buckets, heads, head_ref, table_ref, band_ref):
    first, places = steps_of(buckets)
    value = lambda bucket: table_ref[bucket * heads + head_ref[0]]
    for j in (-1, 0, 1):
        relative = relative_tile(j)
        tile = jnp.full((chunk, chunk), value(first), f32)
        for place, bucket in places:
            tile = jnp.where(relative >= place, value(bucket), tile)
        band_ref[j + 1] = tile


def bias_tiles(head, table, buckets):
    smem = pl.BlockSpec(memory_space=pltpu.SMEM)
    return pl.pallas_call(
        functools.partial(bias_kernel, buckets, table.shape[0] // buckets),
        in_specs=[smem, smem],
        out_shape=jax.ShapeDtypeStruct((3, chunk, chunk), f32),
        compiler_params=pltpu.CompilerParams(vmem_limit_bytes=vmem_bytes),
        cost_estimate=cost(2),
        name="bias_tiles",
    )(head, table)


def table_sums(buckets, band_ref, far_ref, sums_ref):
    first, places = steps_of(buckets)
    edge = chunk // 2
    reach = -(-bucket_edges[-1] // 8) * 8
    sums_ref[...] = jnp.zeros_like(sums_ref)
    relative = [relative_tile(j) for j in (-1, 0, 1)]

    def fold(tile):
        return jnp.sum(tile.reshape(-1, 8, tile.shape[1]), axis=0)

    above = fold(band_ref[0]) + fold(band_ref[1]) + fold(band_ref[2])
    for q in range(far_ref.shape[2] // chunk):
        spot = slice(q * chunk, (q + 1) * chunk)
        above = above + far_ref[0, :, spot] * 0.125 + far_ref[1, :, spot] * 0.125
    right = fold(band_ref[2])
    for q in range(far_ref.shape[2] // chunk):
        right = right + far_ref[1, :, q * chunk : (q + 1) * chunk] * 0.125
    corner = band_ref[2, :reach, edge:]
    corner_relative = relative[2][:reach, edge:]
    left_corner = band_ref[0, chunk - reach :, :edge]
    left_relative = relative[0][chunk - reach :, :edge]
    bucket = first
    for place, following in places:
        if place > 0:
            after = right[:, :edge] + right[:, edge:]
            after = after - fold(jnp.where(corner_relative < place, corner, 0.0))
        else:
            after = right[:, :edge] + right[:, edge:]
            after = after + fold(jnp.where(left_relative >= place, left_corner, 0.0))
        part = fold(jnp.where(relative[1] >= place, band_ref[1], 0.0))
        after = after + part[:, :edge] + part[:, edge:]
        if above.shape[1] == chunk:
            above = above[:, :edge] + above[:, edge:]
        sums_ref[bucket : bucket + 1, :] = jnp.sum(above - after, axis=0, keepdims=True)
        above, bucket = after, following
    sums_ref[bucket : bucket + 1, :] = jnp.sum(above, axis=0, keepdims=True)
    found = jnp.sum(sums_ref[...], axis=1, keepdims=True)
    shape = (buckets, edge)
    spread = lax.broadcasted_iota(jnp.int32, shape, 0) == lax.broadcasted_iota(jnp.int32, shape, 1)
    return jnp.sum(jnp.where(spread, found, 0.0), axis=0, keepdims=True)


def table_pieces(found):
    high = found.astype(bf16).astype(f32)
    middle = (found - high).astype(bf16).astype(f32)
    pieces = [high, middle, found - high - middle, jnp.zeros((13, found.shape[1]), f32)]
    return jnp.concatenate(pieces, axis=0).astype(bf16)


def attend_kernel(
    size, blocks, docs, buckets, first, bounds_ref, head_ref, table_ref, taken_ref, band_ref, *refs
):
    sent_ref, context_ref, expo_ref, scale_ref, keys_ref, *scratch = refs[-5 - 2 * subs :]
    step = pl.program_id(0) + first
    chunks = blocks // 2
    tok = chunk // 2
    bounds = [bounds_ref[0]]
    for d in range(1, docs):
        bounds.append(bounds[-1] + bounds_ref[d])
    heads = table_ref.shape[0] // buckets
    entry = lambda bucket: table_ref[bucket * heads + head_ref[0]]

    @pl.when(step == first)
    def _():
        for s in range(blocks):
            position = s * tok + lax.broadcasted_iota(jnp.int32, (1, tok), 1)
            segment = segments_at(bounds, position)
            row = lax.broadcasted_iota(jnp.int32, (16, tok), 0)
            own = jnp.where(row == segment, 1.0, 0.0)
            part = jnp.where(row == s // 2, 1.0, 0.0)
            tall = jnp.concatenate(
                [
                    taken_ref[s, size : 2 * size, :].astype(f32),
                    own,
                    part,
                    jnp.zeros((size - 32, tok), f32),
                ],
                axis=0,
            )
            keys_ref[s * tok : (s + 1) * tok, :] = tall.T.astype(bf16)
        for query_ref in scratch[::2]:
            query_ref[size:, :] = jnp.zeros((size, chunk), bf16)

    def turned(block, d):
        c = block + d
        return jnp.where(c >= chunks, c - chunks, c)

    blocks_here = [step * subs + k for k in range(subs)]
    tops = []
    for k, block in enumerate(blocks_here):
        query_ref, score_ref = scratch[2 * k : 2 * k + 2]
        position = block * chunk + lax.broadcasted_iota(jnp.int32, (1, chunk), 1)
        segment = segments_at(bounds, position)
        row = lax.broadcasted_iota(jnp.int32, (16, chunk), 0)
        query_ref[:size, :] = tile_rows(taken_ref, block, 0, size)
        query_ref[size : size + 16, :] = jnp.where(row == segment, 0.0, masked_score).astype(bf16)
        far = jnp.where(
            row <= block - 2,
            entry(buckets // 2 - 1),
            jnp.where(row >= block + 2, entry(buckets - 1), 0.0),
        )
        query_ref[size + 16 : size + 32, :] = far.astype(bf16)
        query = query_ref[...]
        top = jnp.full((8, chunk), masked_score, f32)
        for d in range(chunks):
            spot = pl.ds(pl.multiple_of(turned(block, d) * chunk, chunk), chunk)
            scores = jnp.dot(keys_ref[spot, :], query, preferred_element_type=f32)
            if d == 0:
                scores = scores + band_ref[1]
            elif d == 1:
                scores = scores + jnp.where(block + 1 < chunks, 1.0, 0.0) * band_ref[2]
            elif d == chunks - 1:
                scores = scores + jnp.where(block >= 1, 1.0, 0.0) * band_ref[0]
            score_ref[d * chunk : (d + 1) * chunk, :] = scores
            top = jnp.maximum(top, jnp.max(scores.reshape(chunk // 8, 8, chunk), axis=0))
        tops.append(jnp.max(top, axis=0, keepdims=True))
    for k, block in enumerate(blocks_here):
        score_ref = scratch[2 * k + 1]
        lanes = slice(k * chunk, (k + 1) * chunk)
        total = jnp.zeros((8, chunk), f32)
        context = jnp.zeros((size, chunk), f32)
        for d in range(chunks):
            c = turned(block, d)
            expo = jnp.exp(score_ref[d * chunk : (d + 1) * chunk, :] - tops[k])
            total = total + jnp.sum(expo.reshape(chunk // 8, 8, chunk), axis=0)
            low = expo.astype(bf16)
            expo_ref[pl.ds(pl.multiple_of(c * chunk, chunk), chunk), lanes] = low
            context = context + jnp.dot(
                tile_rows(taken_ref, c, 2 * size, 3 * size), low, preferred_element_type=f32
            )
        scale = 1.0 / jnp.sum(total, axis=0, keepdims=True)
        context = context * scale
        context_ref[:, lanes] = context
        scale_ref[:, lanes] = scale
        sent_ref[2 * k] = context[:, :tok].astype(bf16)
        sent_ref[2 * k + 1] = context[:, tok:].astype(bf16)


def attend(taken, lengths, head, table, band, buckets, first, stop, given, *after):
    blocks, size, tok = taken.shape
    size = size // 3
    length = blocks * tok
    smem = pl.BlockSpec(memory_space=pltpu.SMEM)
    return pl.pallas_call(
        functools.partial(attend_kernel, size, blocks, lengths.shape[0], buckets, first),
        grid=((stop or blocks // 2 // subs) - first,),
        in_specs=[
            smem,
            smem,
            smem,
            pl.BlockSpec((blocks, 3 * size, tok), lambda q: (0, 0, 0)),
            pl.BlockSpec((3, chunk, chunk), lambda q: (0, 0, 0)),
        ]
        + [pl.BlockSpec(memory_space=pl.ANY)] * (len(given) + len(after)),
        out_specs=[
            pl.BlockSpec((2 * subs, size, tok), lambda q: (first + q, 0, 0)),
            pl.BlockSpec((size, subs * chunk), lambda q: (0, first + q)),
            pl.BlockSpec((length, subs * chunk), lambda q: (0, first + q)),
            pl.BlockSpec((1, subs * chunk), lambda q: (0, first + q)),
        ],
        out_shape=[
            jax.ShapeDtypeStruct((blocks, size, tok), bf16),
            jax.ShapeDtypeStruct((size, length), f32),
            jax.ShapeDtypeStruct((length, length), bf16),
            jax.ShapeDtypeStruct((1, length), f32),
        ],
        scratch_shapes=[
            pltpu.VMEM((length, 2 * size), bf16),
        ]
        + [
            pltpu.VMEM((2 * size, chunk), bf16),
            pltpu.VMEM((length, chunk), f32),
        ]
        * subs,
        compiler_params=pltpu.CompilerParams(vmem_limit_bytes=vmem_bytes),
        input_output_aliases={5 + k: k for k in range(len(given))},
        cost_estimate=cost(6),
        name="attend",
    )(lengths, head, table, taken, band, *given, *after)


def attend_back_kernel(
    size, blocks, buckets, last, after, taken_ref, grad_ref, context_ref, expo_ref, scale_ref,
    *refs,
):
    before_ref, *refs = refs
    (
        sent_ref, found_ref, band_ref, far_ref, sums_ref,
        queries_ref, wide_ref, delta_ref, grad_queries_ref, grad_scores_ref,
    ) = refs[after:]
    step = pl.program_id(0)
    chunks = blocks // 2
    tok = chunk // 2

    @pl.when(step == 0)
    def _():
        for s in range(blocks):
            spot = slice(s * tok, (s + 1) * tok)
            scaled = grad_ref[s].astype(f32) * scale_ref[:, spot]
            wide_ref[:, spot] = scaled.astype(bf16)
            delta_ref[:, spot] = jnp.sum(scaled * context_ref[:, spot], axis=0, keepdims=True)
            queries_ref[:, spot] = taken_ref[s, :size, :]
        grad_queries_ref[...] = jnp.zeros_like(grad_queries_ref)
        band_ref[...] = jnp.zeros_like(band_ref)
        far_ref[...] = jnp.zeros_like(far_ref)
        for k in range(subs):
            grad_scores_ref[k, :, :chunk] = jnp.zeros((chunk, chunk), bf16)
            grad_scores_ref[k, :, (chunks + 1) * chunk :] = jnp.zeros((chunk, chunk), bf16)

    keys = []
    for k in range(subs):
        c = step * subs + k
        rows = slice(k * chunk, (k + 1) * chunk)
        values = tile_rows(taken_ref, c, 2 * size, 3 * size).astype(f32).T.astype(bf16)
        for q in range(chunks):
            spot = slice(q * chunk, (q + 1) * chunk)
            grad_weights = jnp.dot(values, wide_ref[:, spot], preferred_element_type=f32)
            weights = expo_ref[rows, spot].astype(f32)
            grad_scores = (weights * (grad_weights - delta_ref[:, spot])).astype(bf16)
            grad_scores_ref[k, :, (q + 1) * chunk : (q + 2) * chunk] = grad_scores
        grad_values = dot_on(wide_ref[...], expo_ref[rows, :], 1, 1).astype(bf16)
        grad_keys = dot_on(
            queries_ref[...], grad_scores_ref[k, :, chunk : (chunks + 1) * chunk], 1, 1
        ).astype(bf16)
        for t in range(2):
            sent_ref[2 * c + t, size : 2 * size, :] = grad_keys[:, t * tok : (t + 1) * tok]
            sent_ref[2 * c + t, 2 * size : 3 * size, :] = grad_values[:, t * tok : (t + 1) * tok]
        keys.append(
            jnp.concatenate(
                [tile_rows(taken_ref, c, size, 2 * size), jnp.ones((16, chunk), bf16)], axis=0
            )
        )
    for q in range(chunks):
        spot = slice(q * chunk, (q + 1) * chunk)
        total = grad_queries_ref[:, spot]
        for k in range(subs):
            c = step * subs + k
            part = jnp.dot(
                keys[k],
                grad_scores_ref[k, :, (q + 1) * chunk : (q + 2) * chunk],
                preferred_element_type=f32,
            )
            total = total + part[:size]
            sums = part[size : size + 8]
            far_ref[0, :, spot] = far_ref[0, :, spot] + jnp.where(c <= q - 2, sums, 0.0)
            far_ref[1, :, spot] = far_ref[1, :, spot] + jnp.where(c >= q + 2, sums, 0.0)
        grad_queries_ref[:, spot] = total
    for k in range(subs):
        c = step * subs + k
        for j in (-1, 0, 1):
            spot = pl.ds(pl.multiple_of((c - j + 1) * chunk, chunk), chunk)
            band_ref[j + 1] = band_ref[j + 1] + grad_scores_ref[k, :, spot].astype(f32)

    @pl.when(step == chunks // subs - 1)
    def _():
        for s in range(blocks):
            sent_ref[s, :size, :] = grad_queries_ref[:, s * tok : (s + 1) * tok].astype(bf16)
        found = before_ref[...] + table_sums(buckets, band_ref, far_ref, sums_ref)
        found_ref[...] = found
        if last:
            pieces = table_pieces(found)
            for s in range(blocks):
                sent_ref[s, 3 * size :, :] = pieces


def attend_back(taken, grads, context, expo, scale, buckets, m, last, before, *after):
    blocks, size, _ = grads.shape
    tok = taken.shape[2]
    length = expo.shape[0]
    height = 3 * size + 16 if last else 3 * size
    return pl.pallas_call(
        functools.partial(attend_back_kernel, size, blocks, buckets, last, len(after)),
        grid=(blocks // 2 // subs,),
        in_specs=[
            pl.BlockSpec((blocks, 3 * size, tok), lambda c: (0, 0, 0)),
            pl.BlockSpec((blocks, size, tok), lambda c: (0, 0, m)),
            pl.BlockSpec((size, length), lambda c: (0, 0)),
            pl.BlockSpec((subs * chunk, length), lambda c: (c, 0)),
            pl.BlockSpec((1, length), lambda c: (0, 0)),
            pl.BlockSpec((1, chunk // 2), lambda c: (0, 0)),
        ]
        + [pl.BlockSpec(memory_space=pl.ANY)] * len(after),
        out_specs=[
            pl.BlockSpec((blocks, height, tok), lambda c: (0, 0, 0)),
            pl.BlockSpec((1, chunk // 2), lambda c: (0, 0)),
        ],
        out_shape=[
            jax.ShapeDtypeStruct((blocks, height, tok), bf16),
            jax.ShapeDtypeStruct((1, chunk // 2), f32),
        ],
        scratch_shapes=[
            pltpu.VMEM((3, chunk, chunk), f32),
            pltpu.VMEM((2, 8, length), f32),
            pltpu.VMEM((buckets, chunk // 2), f32),
            pltpu.VMEM((size, length), bf16),
            pltpu.VMEM((size, length), bf16),
            pltpu.VMEM((1, length), f32),
            pltpu.VMEM((size, length), f32),
            pltpu.VMEM((subs, chunk, length + 2 * chunk), bf16),
        ],
        compiler_params=pltpu.CompilerParams(vmem_limit_bytes=vmem_bytes),
        cost_estimate=cost(13),
        name="attend_back",
    )(taken, grads, context, expo, scale, before, *after)


def feed_kernel(
    heads, steps, micro, flipped_ref, matrix_ref, hidden_ref, given_ref, gain_ref, *refs
):
    contexts, refs = refs[:micro], refs[micro:]
    outs, gates, ups, downs = (refs[2 * k : 2 * k + 2] for k in range(4))
    (
        result_ref, grad_mid_ref, grad_context_ref, packet_ref, heard_ref, left_ref, other_left_ref,
        normed_ref, branch_ref, cot_ref, mid_ref, total_ref, grad_ref,
    ) = refs[-13:]
    j = pl.program_id(0)
    size = contexts[0].shape[1]
    sides = side(flipped_ref[0], hidden_ref.shape[1] // 2)

    @pl.when(j == 0)
    def _():
        cot_ref[...] = jnp.dot(
            given_ref[...], matrix_ref[...], preferred_element_type=f32
        ).astype(bf16)
        context = jnp.concatenate(
            [ref[...].reshape(-1, ref.shape[2]).astype(f32).T for ref in contexts], axis=0
        ).astype(bf16)
        heard_ref[...] = context
        context = context[:, : heads * size]
        for lanes, ref in zip(sides, outs):
            mid_ref[:, lanes] = dot_on(context, ref[...], 1, 1)
        mid = hidden_ref[...].astype(f32) + mid_ref[...]
        mid_ref[...] = mid
        total_ref[...] = mid
        normed_ref[...] = rms_norm(mid, gain_ref[...]).astype(bf16)
        grad_ref[...] = jnp.zeros_like(grad_ref)

    def over_width(left_ref, rights):
        own, other = (
            jnp.dot(left_ref[:, lanes], ref[...], preferred_element_type=f32)
            for lanes, ref in zip(sides, rights)
        )
        return own + other

    gate = over_width(normed_ref, gates)
    up = over_width(normed_ref, ups)
    grad_inner = over_width(cot_ref, downs)
    slope = 0.7978845608028654
    square = gate * gate
    bent = jnp.tanh(slope * (gate + 0.044715 * (square * gate)))
    half = 0.5 * (1.0 + bent)
    gelu = gate * half
    gelu_grad = half + (0.5 * gate) * (1.0 - bent * bent) * (
        slope * (1.0 + (3 * 0.044715) * square)
    )
    inner = (gelu * up).astype(bf16)
    grad_gate = (grad_inner * up * gelu_grad).astype(bf16)
    grad_up = (grad_inner * gelu).astype(bf16)
    for k, part in enumerate((grad_gate, grad_up, inner)):
        packet_ref[k] = part
    for k, lanes in enumerate(sides):
        total_ref[:, lanes] = total_ref[:, lanes] + dot_on(inner, downs[k][...], 1, 1)
        grad_ref[:, lanes] = (
            grad_ref[:, lanes]
            + dot_on(grad_gate, gates[k][...], 1, 1)
            + dot_on(grad_up, ups[k][...], 1, 1)
        )

    @pl.when(j == steps - 1)
    def _():
        result_ref[...] = dot_on(total_ref[...].astype(bf16), matrix_ref[...], 1, 1).astype(bf16)
        mid = mid_ref[...]
        scale = lax.rsqrt(jnp.mean(mid * mid, axis=-1, keepdims=True) + norm_eps)
        grad_normed = grad_ref[...]
        gained = grad_normed * gain_ref[...]
        inward = jnp.mean(gained * mid, axis=-1, keepdims=True)
        grad_mid = cot_ref[...].astype(f32) + scale * gained - mid * (scale * scale * scale * inward)
        grad_mid_ref[...] = grad_mid
        branch_ref[...] = grad_mid.astype(bf16)
        grad_context = over_width(branch_ref, outs).T.astype(bf16)
        grad_context_ref[...] = jnp.zeros_like(grad_context_ref)
        for h in range(heads):
            grad_context_ref[h] = grad_context[h * size : (h + 1) * size, :]
        own, other = sides
        half = hidden_ref.shape[1] // 2
        for k, ref in enumerate((normed_ref, cot_ref, branch_ref)):
            left_ref[:, k * half : (k + 1) * half] = ref[:, own]
            other_left_ref[:, k * half : (k + 1) * half] = ref[:, other]


def feed(flipped, matrix, hidden, contexts, cot, gain, weights, heads, *after):
    tok, width = hidden.shape
    blocks, size, _ = contexts[0].shape
    micro = len(contexts)
    inner_width = heads * size
    units = (weights[0].shape[1] - inner_width) // 3
    steps = units // feed_chunk
    assert 3 * units % inner_width == 0
    whole = lambda *shape: pl.BlockSpec(shape, lambda j: (0,) * len(shape))
    column = lambda offset: pl.BlockSpec((width // 2, feed_chunk), lambda j: (0, offset + j))
    spot = 3 * units // inner_width
    weight_specs = [pl.BlockSpec((width // 2, inner_width), lambda j: (0, spot))] * 2
    for k in range(3):
        weight_specs += [column(k * steps)] * 2
    return pl.pallas_call(
        functools.partial(feed_kernel, heads, steps, micro),
        grid=(steps,),
        in_specs=[
            pl.BlockSpec(memory_space=pltpu.SMEM),
            whole(width, width),
            whole(tok, width),
            whole(tok, width),
            whole(1, width),
            *[whole(*context.shape) for context in contexts],
            *weight_specs,
        ]
        + [pl.BlockSpec(memory_space=pl.ANY)] * len(after),
        out_specs=[
            whole(tok, width),
            whole(tok, width),
            whole(blocks, size, tok),
            pl.BlockSpec((3, tok, feed_chunk), lambda j: (0, 0, j)),
            whole(tok, blocks * size),
            whole(tok, 3 * (width // 2)),
            whole(tok, 3 * (width // 2)),
        ],
        out_shape=[
            jax.ShapeDtypeStruct((tok, width), bf16),
            jax.ShapeDtypeStruct((tok, width), f32),
            jax.ShapeDtypeStruct((blocks, size, tok), bf16),
            jax.ShapeDtypeStruct((3, tok, units), bf16),
            jax.ShapeDtypeStruct((tok, blocks * size), bf16),
            jax.ShapeDtypeStruct((tok, 3 * (width // 2)), bf16),
            jax.ShapeDtypeStruct((tok, 3 * (width // 2)), bf16),
        ],
        scratch_shapes=[pltpu.VMEM((tok, width), bf16)] * 3 + [pltpu.VMEM((tok, width), f32)] * 3,
        compiler_params=pltpu.CompilerParams(vmem_limit_bytes=vmem_bytes),
        cost_estimate=cost(8),
        name="feed",
    )(flipped, matrix, hidden, cot, gain, *contexts, *weights * 4, *after)


def store_tall(ref, parts):
    for m, part in enumerate(parts):
        tok = part.shape[0]
        ref[:, m * tok : (m + 1) * tok] = part.astype(f32).T.astype(bf16)


def weight_grad_kernel(counts, parts, half, *refs):
    j = pl.program_id(0)
    out_ref, tall_ref = refs[-2:]
    lefts, packets, heard = (refs[k * parts : (k + 1) * parts] for k in range(3))
    start = 0
    for k, count in counts:

        @pl.when(j == start)
        def _(k=k):
            store_tall(tall_ref, [ref[:, k * half : (k + 1) * half] for ref in lefts])

        start += count

    def product(rights):
        right = jnp.concatenate([ref[...] for ref in rights], axis=0)
        out_ref[...] = jnp.dot(tall_ref[...], right, preferred_element_type=f32).astype(bf16)

    @pl.when(j < start - counts[-1][1])
    def _():
        product(packets)

    @pl.when(j >= start - counts[-1][1])
    def _():
        product(heard)


def weight_grads(lefts, packets, heard, inner_width, *after):
    tok, half = lefts[0].shape[0], lefts[0].shape[1] // 3
    block = grad_chunk
    units, wide = packets[0].shape[2], heard[0].shape[1]
    steps, more = units // block, wide // block
    counts = [(0, 2 * steps), (1, steps), (2, more)]
    place = lambda j: jnp.minimum(j, 3 * steps - 1)
    return pl.pallas_call(
        functools.partial(weight_grad_kernel, counts, len(lefts), half),
        grid=(3 * steps + more,),
        in_specs=[pl.BlockSpec((tok, 3 * half), lambda j: (0, 0))] * len(lefts)
        + [
            pl.BlockSpec((None, tok, block), lambda j: (place(j) // steps, 0, place(j) % steps))
        ]
        * len(packets)
        + [pl.BlockSpec((tok, block), lambda j: (0, jnp.clip(j - 3 * steps, 0, more - 1)))]
        * len(heard)
        + [pl.BlockSpec(memory_space=pl.ANY)] * len(after),
        out_specs=pl.BlockSpec((half, block), lambda j: (0, j)),
        out_shape=jax.ShapeDtypeStruct((half, 3 * units + inner_width), bf16),
        scratch_shapes=[pltpu.VMEM((half, len(lefts) * tok), bf16)],
        compiler_params=pltpu.CompilerParams(vmem_limit_bytes=vmem_bytes),
        cost_estimate=cost(10),
        name="weight_grads",
    )(*lefts, *packets, *heard, *after)


def project_kernel(
    heads, flipped_ref, matrix_ref, inputs_ref, own_ref, other_ref, after_ref, *refs
):
    micro, tok, width = inputs_ref.shape
    sent, (tokens_ref, normed_ref, gain_a_ref, gain_f_ref, gains_ref) = refs[:micro], refs[micro:]
    inner_width = (own_ref.shape[1] - 128) // 3
    size = inner_width // heads
    sides = side(flipped_ref[0], width // 2)
    for lanes, ref in zip(sides, (own_ref, other_ref)):
        gains_ref[:, lanes] = ref[:, 3 * inner_width :].astype(f32).T[:8]
    gain_a_ref[...] = gains_ref[:1]
    gain_f_ref[...] = gains_ref[1:2]
    hidden = jnp.dot(
        inputs_ref[...].reshape(micro * tok, width), matrix_ref[...], preferred_element_type=f32
    )
    tokens_ref[...] = hidden.astype(bf16).reshape(micro, tok, width)
    normed_ref[...] = rms_norm(hidden, gains_ref[:1]).astype(bf16)
    for ref in sent:
        ref[heads:] = jnp.zeros((ref.shape[0] - heads,) + ref.shape[1:], bf16)
    for k in range(3):
        for half in range(2):
            start = k * inner_width + half * (inner_width // 2)
            own, other = (
                jnp.dot(
                    normed_ref[:, lanes],
                    ref[:, start : start + inner_width // 2],
                    preferred_element_type=f32,
                )
                for lanes, ref in zip(sides, (own_ref, other_ref))
            )
            part = (own + other).T.astype(bf16)
            for h in range(heads // 2):
                for m, ref in enumerate(sent):
                    ref[half * (heads // 2) + h, k * size : (k + 1) * size, :] = part[
                        h * size : (h + 1) * size, m * tok : (m + 1) * tok
                    ]


def project(flipped, matrix, inputs, weights, heads, blocks, after):
    micro, tok, width = inputs.shape
    size = (weights[0].shape[1] - 128) // 3 // heads
    vmem = pl.BlockSpec(memory_space=pltpu.VMEM)
    outs = pl.pallas_call(
        functools.partial(project_kernel, heads),
        in_specs=[
            pl.BlockSpec(memory_space=pltpu.SMEM),
            vmem,
            vmem,
            vmem,
            vmem,
            pl.BlockSpec(memory_space=pl.ANY),
        ],
        out_shape=[jax.ShapeDtypeStruct((blocks, 3 * size, tok), bf16)] * micro
        + [
            jax.ShapeDtypeStruct((micro, tok, width), bf16),
            jax.ShapeDtypeStruct((micro * tok, width), bf16),
            jax.ShapeDtypeStruct((1, width), f32),
            jax.ShapeDtypeStruct((1, width), f32),
        ],
        scratch_shapes=[pltpu.VMEM((8, width), f32)],
        compiler_params=pltpu.CompilerParams(vmem_limit_bytes=few_bytes),
        cost_estimate=cost(3),
        name="project",
    )(flipped, matrix, inputs, *weights, after)
    return outs[:micro], *outs[micro:]


def lined(refs, heads, size, lined_ref):
    tok = refs[0].shape[2]
    for m, ref in enumerate(refs):
        for k in range(3):
            for h in range(heads):
                start = (k * heads + h) * size
                lined_ref[start : start + size, m * tok : (m + 1) * tok] = ref[
                    h, k * size : (k + 1) * size, :
                ]


def input_grad_kernel(heads, micro, *refs):
    flipped_ref, matrix_ref, inputs_ref, own_weights, other_weights, gains_ref = refs[:6]
    mid_ref, *grads = refs[6 : 7 + micro]
    input_grad_ref, wide_ref, lined_ref = refs[-3:]
    tok, width = inputs_ref.shape[1:]
    inner_width = (own_weights.shape[1] - 128) // 3
    sides = side(flipped_ref[0], width // 2)
    lined(grads, heads, inner_width // heads, lined_ref)
    for ref, rows in zip((own_weights, other_weights), sides):
        wide_ref[rows, :] = jnp.dot(
            ref[:, : 3 * inner_width], lined_ref[...], preferred_element_type=f32
        )
    gain = gains_ref[...]
    for m in range(micro):
        grad = wide_ref[:, m * tok : (m + 1) * tok].T
        hidden = inputs_ref[m].astype(f32)
        scale = lax.rsqrt(jnp.mean(hidden * hidden, axis=-1, keepdims=True) + norm_eps)
        gained = grad * gain
        inward = jnp.mean(gained * hidden, axis=-1, keepdims=True)
        found = mid_ref[m * tok : (m + 1) * tok, :] + scale * gained - hidden * (scale * scale * scale * inward)
        high = found.astype(bf16)
        rest = found - high.astype(f32)
        middle = rest.astype(bf16)
        low = (rest - middle.astype(f32)).astype(bf16)
        input_grad_ref[m] = sum(
            dot_on(part, matrix_ref[...], 1, 1) for part in (low, middle, high)
        )


def input_grads(flipped, matrix, inputs, weights, gains, grads, mid, heads, *after):
    micro, tok, width = inputs.shape
    inner_width = (weights[0].shape[1] - 128) // 3
    vmem = pl.BlockSpec(memory_space=pltpu.VMEM)
    return pl.pallas_call(
        functools.partial(input_grad_kernel, heads, micro),
        in_specs=[pl.BlockSpec(memory_space=pltpu.SMEM)]
        + [vmem] * (6 + micro)
        + [pl.BlockSpec(memory_space=pl.ANY)] * len(after),
        out_shape=jax.ShapeDtypeStruct((micro, tok, width), f32),
        scratch_shapes=[
            pltpu.VMEM((width, micro * tok), f32),
            pltpu.VMEM((3 * inner_width, micro * tok), bf16),
        ],
        compiler_params=pltpu.CompilerParams(vmem_limit_bytes=vmem_bytes),
        cost_estimate=cost(6),
        name="input_grads",
    )(flipped, matrix, inputs, *weights, gains, mid, *grads, *after)


def front_grad_kernel(heads, parts, half, which, *refs):
    flipped_ref = refs[0]
    lefts, grads = refs[1 : 1 + parts], refs[1 + parts : 1 + 2 * parts]
    out_ref, tall_ref, lined_ref = refs[-3:]
    _, size, tok = grads[0].shape

    @pl.when(pl.program_id(0) == 0)
    def _():
        lanes = side(flipped_ref[0], half)[which]
        for p, ref in enumerate(lefts):
            tall = ref[:, lanes].astype(f32).T.astype(bf16)
            tall_ref[:, p * tok : (p + 1) * tok] = tall

    for p, ref in enumerate(grads):
        lined_ref[:, p * tok : (p + 1) * tok] = ref[:heads].reshape(heads * size, tok)
    out_ref[...] = dot_on(tall_ref[...], lined_ref[...], 1, 1).astype(bf16)


def front_grads(flipped, lefts, grads, inner_width, heads, which):
    tok, width = lefts[0].shape
    parts = len(lefts)
    part = pl.BlockSpec((grads[0].shape[0], inner_width // heads, tok), lambda k: (0, k, 0))
    return pl.pallas_call(
        functools.partial(front_grad_kernel, heads, parts, width // 2, which),
        grid=(3,),
        in_specs=[pl.BlockSpec(memory_space=pltpu.SMEM)]
        + [pl.BlockSpec((tok, width), lambda k: (0, 0))] * parts
        + [part] * parts,
        out_specs=pl.BlockSpec((width // 2, inner_width), lambda k: (0, k)),
        out_shape=jax.ShapeDtypeStruct((width // 2, 3 * inner_width), bf16),
        scratch_shapes=[
            pltpu.VMEM((width // 2, parts * tok), bf16),
            pltpu.VMEM((inner_width, parts * tok), bf16),
        ],
        compiler_params=pltpu.CompilerParams(vmem_limit_bytes=few_bytes),
        cost_estimate=cost(5),
        name="front_grads",
    )(flipped, *lefts, *grads)


def row_of(column):
    share = column.shape[0]
    shape = (share, share)
    spread = lax.broadcasted_iota(jnp.int32, shape, 0) == lax.broadcasted_iota(jnp.int32, shape, 1)
    return jnp.sum(jnp.where(spread, column, 0.0), axis=0, keepdims=True)


def gain_grad_of(weights, grads, gain_ref):
    total = sum(
        jnp.sum(weight[...].astype(f32) * grad[...], axis=1, keepdims=True)
        for weight, grad in zip(weights, grads)
    )
    return row_of(total) / gain_ref[...].astype(f32)


def unpack_back_kernel(sums_ref, gate_ref, up_ref, gain_ref, *refs):
    gate_grad_ref, up_grad_ref, down_grad_ref, out_grad_ref, gain_grad_ref = refs
    units = gate_ref.shape[1]
    for k, ref in enumerate((gate_grad_ref, up_grad_ref, down_grad_ref, out_grad_ref)):
        ref[...] = sums_ref[:, k * units : k * units + ref.shape[1]].astype(f32)
    gain_grad_ref[...] = gain_grad_of((gate_ref, up_ref), (gate_grad_ref, up_grad_ref), gain_ref)


def unpack_back(sums, w_gate, w_up, gain, inner_width):
    share, units = w_gate.shape
    shapes = [(share, units)] * 3 + [(share, inner_width), (1, share)]
    gate, up, down, out, gain_grad = pl.pallas_call(
        unpack_back_kernel,
        out_shape=[jax.ShapeDtypeStruct(shape, f32) for shape in shapes],
        compiler_params=pltpu.CompilerParams(vmem_limit_bytes=few_bytes),
        name="unpack_back",
    )(sums, w_gate, w_up, gain[None, :])
    return gate, up, down.T, out.T, gain_grad[0]


def unpack_front_kernel(parts_ref, query_ref, key_ref, value_ref, gain_ref, after_ref, *refs):
    grads, gain_grad_ref = refs[:3], refs[3]
    width = query_ref.shape[1]
    for k, ref in enumerate(grads):
        part = parts_ref[:, :, k * width : (k + 1) * width].astype(f32)
        ref[...] = jnp.sum(part, axis=0)
    gain_grad_ref[...] = gain_grad_of((query_ref, key_ref, value_ref), grads, gain_ref)


def unpack_front(parts, w_query, w_key, w_value, gain, after):
    share, width = w_query.shape
    vmem = pl.BlockSpec(memory_space=pltpu.VMEM)
    shapes = [(share, width)] * 3 + [(1, share)]
    query, key, value, gain_grad = pl.pallas_call(
        unpack_front_kernel,
        in_specs=[vmem] * 5 + [pl.BlockSpec(memory_space=pl.ANY)],
        out_shape=[jax.ShapeDtypeStruct(shape, f32) for shape in shapes],
        compiler_params=pltpu.CompilerParams(vmem_limit_bytes=few_bytes),
        name="unpack_front",
    )(parts, w_query, w_key, w_value, gain[None, :], after)
    return query, key, value, gain_grad[0]


def body(
    inputs, doc_lengths, attn_gain, w_query, w_key, w_value, w_out, ff_gain,
    w_gate, w_up, w_down, rel_table, cotangent,
):
    micro, _, tok, width = inputs.shape
    inner_width = w_query.shape[1]
    hidden_units = w_gate.shape[1]
    buckets, heads = rel_table.shape
    size = inner_width // heads
    blocks = lax.axis_size("blk")
    rows = lax.axis_size("rows")
    me = lax.axis_index("blk")
    share = w_query.shape[0]
    micros = range(micro)

    flipped = lax.axis_index("rows") if staged(rows, blocks, share) else 0
    flipped = jnp.full((1,), flipped, jnp.int32)
    matrix = stage_matrix(rows, blocks, share)
    head = jnp.minimum(me, heads - 1).astype(jnp.int32).reshape(1)
    table = rel_table.astype(f32).reshape(-1)

    with jax.named_scope("weights"):
        front_full = gather_front(w_query, w_key, w_value, attn_gain, ff_gain)
        back_own = gather_back(jnp.concatenate([w_gate, w_up, w_down.T, w_out.T], axis=1), front_full[0])

    band = bias_tiles(head, table, buckets)
    sent, tokens, normed_a, gain_a, gain_f = project(
        flipped, matrix, inputs[:, 0], front_full, heads, blocks, band
    )
    taken = []
    for m in micros:
        with jax.named_scope("project"):
            part = tie(sent[m], taken[-1]) if m else sent[m]
            taken.append(lax.all_to_all(part, "blk", 0, 0, tiled=True))

    kept, contexts, half = [], [], blocks // 4 // subs
    for m in micros:
        given = taken[m], doc_lengths[m, 0], head, table, band, buckets
        outs = [k[0] for k in kept]
        if m:
            outs = attend(*given, 0, half, [], *outs)
            outs = attend(*given, half, None, outs, *contexts)
        else:
            outs = attend(*given, 0, None, [])
        kept.append(outs[1:])
        with jax.named_scope("context"):
            contexts.append(lax.all_to_all(outs[0], "blk", 0, 0, tiled=True))
    with jax.named_scope("weights"):
        back_full = gather_other(back_own, outs[0])

    fits = staged(rows, blocks, share)
    here = micro * tok
    result, grad_mid, grad_context, mine, heard, left, left_other = feed(
        flipped, matrix, tokens.reshape(here, width), contexts,
        cotangent[:, 0].reshape(here, width), gain_f, back_full, heads,
    )
    with jax.named_scope("grad_context"):
        grads = lax.all_to_all(grad_context, "blk", 0, 0, tiled=True)
    if fits:
        with jax.named_scope("packet"):
            packet, near_heard, near_left = (flip(a, "rows", 1) for a in (mine, heard, left_other))

    with jax.named_scope("back_grads"):
        if fits:
            own = weight_grads([left, near_left], [mine, packet], [heard, near_heard], inner_width)
            own = tie(own, grads)
            back_grad = scatter_back(own)
        else:
            own, other = (
                weight_grads([lefts], [mine], [heard], inner_width) for lefts in (left, left_other)
            )
            back_grad = scatter_whole(own, other)
    grad_qkv, found = [], jnp.zeros((1, chunk // 2), f32)
    for m in micros:
        returned, found = attend_back(
            taken[m], grads, *kept[m], buckets, m, m == micro - 1, found, own
        )
        with jax.named_scope("grad_qkv"):
            returned = tie(returned, *grad_qkv) if m else returned
            grad_qkv.append(lax.all_to_all(returned, "blk", 0, 0, tiled=True))

    with jax.named_scope("table"):
        pieces = grad_qkv[-1][:heads, 3 * size : 3 * size + 3, :buckets]
        table_grad = jnp.sum(pieces.astype(f32), axis=1).T
        for bit in bits_of(rows):
            table_grad = table_grad + flip(table_grad, "rows", bit)

    with jax.named_scope("front_grads"):
        normed = [normed_a[m * tok : (m + 1) * tok] for m in micros]
        if fits:
            near_grads = [flip(g, "rows", 1) for g in grad_qkv]
            near_normed = [flip(n, "rows", 1) for n in normed]
            own = front_grads(
                flipped, normed + near_normed, grad_qkv + near_grads, inner_width, heads, 0
            )
            back_grad = scatter_back_end(back_grad, own)
            front_parts = scatter_front(own, share)
        else:
            own, other = (
                front_grads(flipped, normed, grad_qkv, inner_width, heads, which)
                for which in (0, 1)
            )
            front_parts = scatter_whole(own, other)[None]
    input_grad = input_grads(
        flipped, matrix, tokens, front_full, gain_a, grad_qkv, grad_mid, heads, own
    )
    if fits:
        with jax.named_scope("front_grads"):
            front_parts = scatter_front_end(front_parts, share, input_grad)
    gate_grad, up_grad, down_grad, out_grad, ff_gain_grad = unpack_back(
        back_grad, w_gate, w_up, ff_gain, inner_width
    )
    query_grad, key_grad, value_grad, attn_gain_grad = unpack_front(
        front_parts, w_query, w_key, w_value, attn_gain, gate_grad
    )

    return (
        result.reshape(micro, 1, tok, width),
        input_grad[:, None],
        attn_gain_grad,
        query_grad,
        key_grad,
        value_grad,
        out_grad,
        ff_gain_grad,
        gate_grad,
        up_grad,
        down_grad,
        table_grad,
    )


def solution(mesh):
    weight_rows = P(both, None)
    weight_columns = P(None, both)
    tokens = P(None, "rows", "blk", None)
    in_specs = (
        tokens, P(None, "rows", None), P(both), weight_rows, weight_rows, weight_rows,
        weight_columns, P(both), weight_rows, weight_rows, weight_columns, P(), tokens,
    )
    out_specs = (
        tokens, tokens, P(both), weight_rows, weight_rows, weight_rows,
        weight_columns, P(both), weight_rows, weight_rows, weight_columns, P(),
    )
    return jax.shard_map(body, mesh=mesh, in_specs=in_specs, out_specs=out_specs, check_vma=False)
```

```python
import functools

import jax
import jax.numpy as jnp
import numpy as np
from jax import lax
from jax.experimental import pallas as pl
from jax.experimental.pallas import tpu as pltpu
from jax.sharding import PartitionSpec as P

bucket_edges = (12, 16, 23, 32, 46, 64, 91)
norm_eps = 1e-06
masked_score = -1e30
f32 = jnp.float32
bf16 = jnp.bfloat16
both = ("rows", "blk")
chunk = 256
feed_chunk = 512
grad_chunk = 1024
subs = 2
vmem_bytes = 56 * 1024 * 1024
few_bytes = 24 * 1024 * 1024


def bucket_of(relative, total_buckets):
    half = total_buckets // 2
    exact = half // 2
    distance = jnp.abs(relative)
    far_bucket = exact + sum(((distance >= edge).astype(jnp.int32) for edge in bucket_edges))
    return jnp.where(relative > 0, half, 0) + jnp.where(distance < exact, distance, far_bucket)


def rms_norm(hidden, gain):
    return hidden * lax.rsqrt(jnp.mean(hidden * hidden, axis=-1, keepdims=True) + norm_eps) * gain


def gated(gate, up):
    return jax.nn.gelu(gate, approximate=True) * up


def dot_on(left, right, left_dim, right_dim):
    return lax.dot_general(
        left, right, (((left_dim,), (right_dim,)), ((), ())), preferred_element_type=f32
    )


def flip(array, axis, bit):
    count = lax.axis_size(axis)
    return lax.ppermute(array, axis, [(i, i ^ bit) for i in range(count)])


def bits_of(count):
    return [1 << k for k in range(count.bit_length() - 1)]


def segments_at(bounds, positions):
    total = jnp.zeros(positions.shape, jnp.int32)
    for bound in bounds:
        total = total + (positions >= bound).astype(jnp.int32)
    return total


def groups_of(blocks):
    near = 4
    far = blocks // near
    across = [[f * near + n for f in range(far)] for n in range(near)]
    within = [[f * near + n for n in range(near)] for f in range(far)]
    return far, near, across, within


def staged(rows, blocks, share):
    return rows == 2 and blocks % 4 == 0 and share % 8 == 0


def stage_matrix(rows, blocks, share):
    place = np.arange(rows * blocks * share)
    taken = place
    if staged(rows, blocks, share):
        far, near, _, _ = groups_of(blocks)
        slab = place // share
        half, inner = slab // blocks, slab % blocks
        taken = (half * blocks + inner % far * near + inner // far) * share + place % share
    return jnp.asarray((place[:, None] == taken[None, :]).astype(np.float32), bf16)


def tie_kernel(*refs):
    pass


def tie(value, *after):
    space = pl.BlockSpec(memory_space=pl.ANY)
    return pl.pallas_call(
        tie_kernel,
        in_specs=[space] * (1 + len(after)),
        out_specs=space,
        out_shape=jax.ShapeDtypeStruct(value.shape, value.dtype),
        input_output_aliases={0: 0},
        name="tie",
    )(value, *after)


def exchange(array, groups):
    return lax.all_to_all(array, "blk", 0, 0, tiled=True, axis_index_groups=groups)


def halves_of_whole(whole):
    half = whole.shape[0] // 2
    return whole[:half], whole[half:]


def pack_kernel(query_ref, key_ref, value_ref, gain_a_ref, gain_f_ref, out_ref):
    share = query_ref.shape[0]
    spread = lax.broadcasted_iota(jnp.int32, (share, share), 0) == lax.broadcasted_iota(
        jnp.int32, (share, share), 1
    )
    lane = lax.broadcasted_iota(jnp.int32, (share, 128), 1)
    gains = jnp.zeros((share, 128), f32)
    for k, ref in enumerate((gain_a_ref, gain_f_ref)):
        column = jnp.where(spread, ref[...].astype(f32), 0.0)
        gains = jnp.where(lane == k, jnp.sum(column, axis=1, keepdims=True), gains)
    parts = [query_ref[...], key_ref[...], value_ref[...], gains.astype(bf16)]
    packed = jnp.concatenate(parts, axis=1)
    for copy in range(out_ref.shape[0]):
        out_ref[copy] = packed


def pack(query, key, value, gain_a, gain_f, copies):
    shape = (copies, query.shape[0], 3 * query.shape[1] + 128)
    return pl.pallas_call(
        pack_kernel,
        out_shape=jax.ShapeDtypeStruct(shape, bf16),
        compiler_params=pltpu.CompilerParams(vmem_limit_bytes=vmem_bytes),
        name="pack",
    )(query, key, value, gain_a[None, :], gain_f[None, :])


def gather_front(*parts):
    blocks, rows = lax.axis_size("blk"), lax.axis_size("rows")
    if not staged(rows, blocks, parts[0].shape[0]):
        shard = pack(*parts, 1)[0]
        return halves_of_whole(lax.all_gather(shard, both, axis=0, tiled=True))
    far, near, across, within = groups_of(blocks)
    packed = pack(*parts, far)
    first = exchange(packed.reshape(-1, packed.shape[2]), across)
    own = exchange(jnp.tile(first, (near, 1)), within)
    return own, flip(own, "rows", 1)


def gather_back(shard, after):
    blocks, rows = lax.axis_size("blk"), lax.axis_size("rows")
    if not staged(rows, blocks, shard.shape[0]):
        return lax.all_gather(shard, both, axis=0, tiled=True)
    far, near, across, within = groups_of(blocks)
    own = lax.all_gather(shard, "blk", axis=0, tiled=True, axis_index_groups=across)
    own = tie(own, after)
    return lax.all_gather(own, "blk", axis=0, tiled=True, axis_index_groups=within)


def gather_other(own, after):
    blocks, rows = lax.axis_size("blk"), lax.axis_size("rows")
    if not staged(rows, blocks, own.shape[0] // blocks):
        return halves_of_whole(own)
    own = tie(own, after)
    return own, flip(own, "rows", 1)


def scatter_front(own, share):
    far, near, _, within = groups_of(lax.axis_size("blk"))
    held = exchange(own, within).reshape(near, far * share, own.shape[1])
    return jnp.sum(held.astype(f32), axis=0).astype(bf16)


def scatter_front_end(held, share, *after):
    far, _, across, _ = groups_of(lax.axis_size("blk"))
    return exchange(tie(held, *after), across).reshape(far, share, held.shape[1])


def scatter_back(own):
    _, _, _, within = groups_of(lax.axis_size("blk"))
    return lax.psum_scatter(
        own, "blk", scatter_dimension=0, axis_index_groups=within, tiled=True
    )


def scatter_back_end(part, after):
    _, _, across, _ = groups_of(lax.axis_size("blk"))
    return lax.psum_scatter(
        tie(part, after), "blk", scatter_dimension=0, axis_index_groups=across, tiled=True
    )


def scatter_whole(own, other):
    whole = jnp.concatenate([own, other], axis=0)
    return lax.psum_scatter(whole, both, scatter_dimension=0, tiled=True)


def side(flipped, half):
    return (
        pl.ds(pl.multiple_of(flipped * half, half), half),
        pl.ds(pl.multiple_of((1 - flipped) * half, half), half),
    )


def cost(micros):
    return pl.CostEstimate(flops=int(micros * 1e9), bytes_accessed=0, transcendentals=0)


def tile_rows(ref, index, start, stop):
    return jnp.concatenate(
        [ref[2 * index, start:stop, :], ref[2 * index + 1, start:stop, :]], axis=1
    )


def steps_of(buckets):
    half = buckets // 2
    exact = half // 2
    lows = list(range(1, exact)) + [exact] + list(bucket_edges)
    places = [(1 - low, k) for k, low in reversed(list(enumerate(lows)))]
    return half - 1, places + [(low, half + 1 + k) for k, low in enumerate(lows)]


def relative_tile(j):
    shape = (chunk, chunk)
    return (
        lax.broadcasted_iota(jnp.int32, shape, 0)
        - lax.broadcasted_iota(jnp.int32, shape, 1)
        + j * chunk
    )


def bias_kernel(buckets, heads, head_ref, table_ref, band_ref):
    first, places = steps_of(buckets)
    value = lambda bucket: table_ref[bucket * heads + head_ref[0]]
    for j in (-1, 0, 1):
        relative = relative_tile(j)
        tile = jnp.full((chunk, chunk), value(first), f32)
        for place, bucket in places:
            tile = jnp.where(relative >= place, value(bucket), tile)
        band_ref[j + 1] = tile


def bias_tiles(head, table, buckets):
    smem = pl.BlockSpec(memory_space=pltpu.SMEM)
    return pl.pallas_call(
        functools.partial(bias_kernel, buckets, table.shape[0] // buckets),
        in_specs=[smem, smem],
        out_shape=jax.ShapeDtypeStruct((3, chunk, chunk), f32),
        compiler_params=pltpu.CompilerParams(vmem_limit_bytes=vmem_bytes),
        cost_estimate=cost(2),
        name="bias_tiles",
    )(head, table)


def table_sums(buckets, band_ref, far_ref, sums_ref):
    first, places = steps_of(buckets)
    edge = chunk // 2
    reach = -(-bucket_edges[-1] // 8) * 8
    sums_ref[...] = jnp.zeros_like(sums_ref)
    relative = [relative_tile(j) for j in (-1, 0, 1)]

    def fold(tile):
        return jnp.sum(tile.reshape(-1, 8, tile.shape[1]), axis=0)

    above = fold(band_ref[0]) + fold(band_ref[1]) + fold(band_ref[2])
    for q in range(far_ref.shape[2] // chunk):
        spot = slice(q * chunk, (q + 1) * chunk)
        above = above + far_ref[0, :, spot] * 0.125 + far_ref[1, :, spot] * 0.125
    right = fold(band_ref[2])
    for q in range(far_ref.shape[2] // chunk):
        right = right + far_ref[1, :, q * chunk : (q + 1) * chunk] * 0.125
    corner = band_ref[2, :reach, edge:]
    corner_relative = relative[2][:reach, edge:]
    left_corner = band_ref[0, chunk - reach :, :edge]
    left_relative = relative[0][chunk - reach :, :edge]
    bucket = first
    for place, following in places:
        if place > 0:
            after = right[:, :edge] + right[:, edge:]
            after = after - fold(jnp.where(corner_relative < place, corner, 0.0))
        else:
            after = right[:, :edge] + right[:, edge:]
            after = after + fold(jnp.where(left_relative >= place, left_corner, 0.0))
        part = fold(jnp.where(relative[1] >= place, band_ref[1], 0.0))
        after = after + part[:, :edge] + part[:, edge:]
        if above.shape[1] == chunk:
            above = above[:, :edge] + above[:, edge:]
        sums_ref[bucket : bucket + 1, :] = jnp.sum(above - after, axis=0, keepdims=True)
        above, bucket = after, following
    sums_ref[bucket : bucket + 1, :] = jnp.sum(above, axis=0, keepdims=True)
    found = jnp.sum(sums_ref[...], axis=1, keepdims=True)
    shape = (buckets, edge)
    spread = lax.broadcasted_iota(jnp.int32, shape, 0) == lax.broadcasted_iota(jnp.int32, shape, 1)
    return jnp.sum(jnp.where(spread, found, 0.0), axis=0, keepdims=True)


def table_pieces(found):
    high = found.astype(bf16).astype(f32)
    middle = (found - high).astype(bf16).astype(f32)
    pieces = [high, middle, found - high - middle, jnp.zeros((13, found.shape[1]), f32)]
    return jnp.concatenate(pieces, axis=0).astype(bf16)


def attend_kernel(
    size, blocks, docs, buckets, first, bounds_ref, head_ref, table_ref, taken_ref, band_ref, *refs
):
    sent_ref, context_ref, expo_ref, scale_ref, keys_ref, *scratch = refs[-5 - 2 * subs :]
    step = pl.program_id(0) + first
    chunks = blocks // 2
    tok = chunk // 2
    bounds = [bounds_ref[0]]
    for d in range(1, docs):
        bounds.append(bounds[-1] + bounds_ref[d])
    heads = table_ref.shape[0] // buckets
    entry = lambda bucket: table_ref[bucket * heads + head_ref[0]]

    @pl.when(step == first)
    def _():
        for s in range(blocks):
            position = s * tok + lax.broadcasted_iota(jnp.int32, (1, tok), 1)
            segment = segments_at(bounds, position)
            row = lax.broadcasted_iota(jnp.int32, (16, tok), 0)
            own = jnp.where(row == segment, 1.0, 0.0)
            part = jnp.where(row == s // 2, 1.0, 0.0)
            tall = jnp.concatenate(
                [
                    taken_ref[s, size : 2 * size, :].astype(f32),
                    own,
                    part,
                    jnp.zeros((size - 32, tok), f32),
                ],
                axis=0,
            )
            keys_ref[s * tok : (s + 1) * tok, :] = tall.T.astype(bf16)
        for query_ref in scratch[::2]:
            query_ref[size:, :] = jnp.zeros((size, chunk), bf16)

    def turned(block, d):
        c = block + d
        return jnp.where(c >= chunks, c - chunks, c)

    blocks_here = [step * subs + k for k in range(subs)]
    tops = []
    for k, block in enumerate(blocks_here):
        query_ref, score_ref = scratch[2 * k : 2 * k + 2]
        position = block * chunk + lax.broadcasted_iota(jnp.int32, (1, chunk), 1)
        segment = segments_at(bounds, position)
        row = lax.broadcasted_iota(jnp.int32, (16, chunk), 0)
        query_ref[:size, :] = tile_rows(taken_ref, block, 0, size)
        query_ref[size : size + 16, :] = jnp.where(row == segment, 0.0, masked_score).astype(bf16)
        far = jnp.where(
            row <= block - 2,
            entry(buckets // 2 - 1),
            jnp.where(row >= block + 2, entry(buckets - 1), 0.0),
        )
        query_ref[size + 16 : size + 32, :] = far.astype(bf16)
        query = query_ref[...]
        top = jnp.full((8, chunk), masked_score, f32)
        for d in range(chunks):
            spot = pl.ds(pl.multiple_of(turned(block, d) * chunk, chunk), chunk)
            scores = jnp.dot(keys_ref[spot, :], query, preferred_element_type=f32)
            if d == 0:
                scores = scores + band_ref[1]
            elif d == 1:
                scores = scores + jnp.where(block + 1 < chunks, 1.0, 0.0) * band_ref[2]
            elif d == chunks - 1:
                scores = scores + jnp.where(block >= 1, 1.0, 0.0) * band_ref[0]
            score_ref[d * chunk : (d + 1) * chunk, :] = scores
            top = jnp.maximum(top, jnp.max(scores.reshape(chunk // 8, 8, chunk), axis=0))
        tops.append(jnp.max(top, axis=0, keepdims=True))
    for k, block in enumerate(blocks_here):
        score_ref = scratch[2 * k + 1]
        lanes = slice(k * chunk, (k + 1) * chunk)
        total = jnp.zeros((8, chunk), f32)
        context = jnp.zeros((size, chunk), f32)
        for d in range(chunks):
            c = turned(block, d)
            expo = jnp.exp(score_ref[d * chunk : (d + 1) * chunk, :] - tops[k])
            total = total + jnp.sum(expo.reshape(chunk // 8, 8, chunk), axis=0)
            low = expo.astype(bf16)
            expo_ref[pl.ds(pl.multiple_of(c * chunk, chunk), chunk), lanes] = low
            context = context + jnp.dot(
                tile_rows(taken_ref, c, 2 * size, 3 * size), low, preferred_element_type=f32
            )
        scale = 1.0 / jnp.sum(total, axis=0, keepdims=True)
        context = context * scale
        context_ref[:, lanes] = context
        scale_ref[:, lanes] = scale
        sent_ref[2 * k] = context[:, :tok].astype(bf16)
        sent_ref[2 * k + 1] = context[:, tok:].astype(bf16)


def attend(taken, lengths, head, table, band, buckets, first, stop, given, *after):
    blocks, size, tok = taken.shape
    size = size // 3
    length = blocks * tok
    smem = pl.BlockSpec(memory_space=pltpu.SMEM)
    return pl.pallas_call(
        functools.partial(attend_kernel, size, blocks, lengths.shape[0], buckets, first),
        grid=((stop or blocks // 2 // subs) - first,),
        in_specs=[
            smem,
            smem,
            smem,
            pl.BlockSpec((blocks, 3 * size, tok), lambda q: (0, 0, 0)),
            pl.BlockSpec((3, chunk, chunk), lambda q: (0, 0, 0)),
        ]
        + [pl.BlockSpec(memory_space=pl.ANY)] * (len(given) + len(after)),
        out_specs=[
            pl.BlockSpec((2 * subs, size, tok), lambda q: (first + q, 0, 0)),
            pl.BlockSpec((size, subs * chunk), lambda q: (0, first + q)),
            pl.BlockSpec((length, subs * chunk), lambda q: (0, first + q)),
            pl.BlockSpec((1, subs * chunk), lambda q: (0, first + q)),
        ],
        out_shape=[
            jax.ShapeDtypeStruct((blocks, size, tok), bf16),
            jax.ShapeDtypeStruct((size, length), f32),
            jax.ShapeDtypeStruct((length, length), bf16),
            jax.ShapeDtypeStruct((1, length), f32),
        ],
        scratch_shapes=[
            pltpu.VMEM((length, 2 * size), bf16),
        ]
        + [
            pltpu.VMEM((2 * size, chunk), bf16),
            pltpu.VMEM((length, chunk), f32),
        ]
        * subs,
        compiler_params=pltpu.CompilerParams(vmem_limit_bytes=vmem_bytes),
        input_output_aliases={5 + k: k for k in range(len(given))},
        cost_estimate=cost(6),
        name="attend",
    )(lengths, head, table, taken, band, *given, *after)


def attend_back_kernel(
    size, blocks, buckets, last, after, taken_ref, grad_ref, context_ref, expo_ref, scale_ref,
    *refs,
):
    before_ref, *refs = refs
    (
        sent_ref, found_ref, band_ref, far_ref, sums_ref,
        queries_ref, wide_ref, delta_ref, grad_queries_ref, grad_scores_ref,
    ) = refs[after:]
    step = pl.program_id(0)
    chunks = blocks // 2
    tok = chunk // 2

    @pl.when(step == 0)
    def _():
        for s in range(blocks):
            spot = slice(s * tok, (s + 1) * tok)
            scaled = grad_ref[s].astype(f32) * scale_ref[:, spot]
            wide_ref[:, spot] = scaled.astype(bf16)
            delta_ref[:, spot] = jnp.sum(scaled * context_ref[:, spot], axis=0, keepdims=True)
            queries_ref[:, spot] = taken_ref[s, :size, :]
        grad_queries_ref[...] = jnp.zeros_like(grad_queries_ref)
        band_ref[...] = jnp.zeros_like(band_ref)
        far_ref[...] = jnp.zeros_like(far_ref)
        for k in range(subs):
            grad_scores_ref[k, :, :chunk] = jnp.zeros((chunk, chunk), bf16)
            grad_scores_ref[k, :, (chunks + 1) * chunk :] = jnp.zeros((chunk, chunk), bf16)

    keys = []
    for k in range(subs):
        c = step * subs + k
        rows = slice(k * chunk, (k + 1) * chunk)
        values = tile_rows(taken_ref, c, 2 * size, 3 * size).astype(f32).T.astype(bf16)
        for q in range(chunks):
            spot = slice(q * chunk, (q + 1) * chunk)
            grad_weights = jnp.dot(values, wide_ref[:, spot], preferred_element_type=f32)
            weights = expo_ref[rows, spot].astype(f32)
            grad_scores = (weights * (grad_weights - delta_ref[:, spot])).astype(bf16)
            grad_scores_ref[k, :, (q + 1) * chunk : (q + 2) * chunk] = grad_scores
        grad_values = dot_on(wide_ref[...], expo_ref[rows, :], 1, 1).astype(bf16)
        grad_keys = dot_on(
            queries_ref[...], grad_scores_ref[k, :, chunk : (chunks + 1) * chunk], 1, 1
        ).astype(bf16)
        for t in range(2):
            sent_ref[2 * c + t, size : 2 * size, :] = grad_keys[:, t * tok : (t + 1) * tok]
            sent_ref[2 * c + t, 2 * size : 3 * size, :] = grad_values[:, t * tok : (t + 1) * tok]
        keys.append(
            jnp.concatenate(
                [tile_rows(taken_ref, c, size, 2 * size), jnp.ones((16, chunk), bf16)], axis=0
            )
        )
    for q in range(chunks):
        spot = slice(q * chunk, (q + 1) * chunk)
        total = grad_queries_ref[:, spot]
        for k in range(subs):
            c = step * subs + k
            part = jnp.dot(
                keys[k],
                grad_scores_ref[k, :, (q + 1) * chunk : (q + 2) * chunk],
                preferred_element_type=f32,
            )
            total = total + part[:size]
            sums = part[size : size + 8]
            far_ref[0, :, spot] = far_ref[0, :, spot] + jnp.where(c <= q - 2, sums, 0.0)
            far_ref[1, :, spot] = far_ref[1, :, spot] + jnp.where(c >= q + 2, sums, 0.0)
        grad_queries_ref[:, spot] = total
    for k in range(subs):
        c = step * subs + k
        for j in (-1, 0, 1):
            spot = pl.ds(pl.multiple_of((c - j + 1) * chunk, chunk), chunk)
            band_ref[j + 1] = band_ref[j + 1] + grad_scores_ref[k, :, spot].astype(f32)

    @pl.when(step == chunks // subs - 1)
    def _():
        for s in range(blocks):
            sent_ref[s, :size, :] = grad_queries_ref[:, s * tok : (s + 1) * tok].astype(bf16)
        found = before_ref[...] + table_sums(buckets, band_ref, far_ref, sums_ref)
        found_ref[...] = found
        if last:
            pieces = table_pieces(found)
            for s in range(blocks):
                sent_ref[s, 3 * size :, :] = pieces


def attend_back(taken, grads, context, expo, scale, buckets, m, last, before, *after):
    blocks, size, _ = grads.shape
    tok = taken.shape[2]
    length = expo.shape[0]
    height = 3 * size + 16 if last else 3 * size
    return pl.pallas_call(
        functools.partial(attend_back_kernel, size, blocks, buckets, last, len(after)),
        grid=(blocks // 2 // subs,),
        in_specs=[
            pl.BlockSpec((blocks, 3 * size, tok), lambda c: (0, 0, 0)),
            pl.BlockSpec((blocks, size, tok), lambda c: (0, 0, m)),
            pl.BlockSpec((size, length), lambda c: (0, 0)),
            pl.BlockSpec((subs * chunk, length), lambda c: (c, 0)),
            pl.BlockSpec((1, length), lambda c: (0, 0)),
            pl.BlockSpec((1, chunk // 2), lambda c: (0, 0)),
        ]
        + [pl.BlockSpec(memory_space=pl.ANY)] * len(after),
        out_specs=[
            pl.BlockSpec((blocks, height, tok), lambda c: (0, 0, 0)),
            pl.BlockSpec((1, chunk // 2), lambda c: (0, 0)),
        ],
        out_shape=[
            jax.ShapeDtypeStruct((blocks, height, tok), bf16),
            jax.ShapeDtypeStruct((1, chunk // 2), f32),
        ],
        scratch_shapes=[
            pltpu.VMEM((3, chunk, chunk), f32),
            pltpu.VMEM((2, 8, length), f32),
            pltpu.VMEM((buckets, chunk // 2), f32),
            pltpu.VMEM((size, length), bf16),
            pltpu.VMEM((size, length), bf16),
            pltpu.VMEM((1, length), f32),
            pltpu.VMEM((size, length), f32),
            pltpu.VMEM((subs, chunk, length + 2 * chunk), bf16),
        ],
        compiler_params=pltpu.CompilerParams(vmem_limit_bytes=vmem_bytes),
        cost_estimate=cost(13),
        name="attend_back",
    )(taken, grads, context, expo, scale, before, *after)


def reorder_kernel(array_ref, matrix_ref, out_ref):
    out_ref[...] = jnp.dot(
        array_ref[...], matrix_ref[...], preferred_element_type=f32
    ).astype(bf16)


def reorder(array, matrix):
    return pl.pallas_call(
        reorder_kernel,
        out_shape=jax.ShapeDtypeStruct(array.shape, bf16),
        compiler_params=pltpu.CompilerParams(vmem_limit_bytes=vmem_bytes),
        cost_estimate=cost(2),
        name="reorder",
    )(array, matrix)


def feed_kernel(
    heads, steps, micro, flipped_ref, hidden_ref, cot_ref, gain_ref, *refs
):
    contexts, refs = refs[:micro], refs[micro:]
    outs, gates, ups, downs = (refs[2 * k : 2 * k + 2] for k in range(4))
    (
        result_ref, grad_mid_ref, grad_context_ref, packet_ref, heard_ref, left_ref, other_left_ref,
        normed_ref, branch_ref, mid_ref, total_ref, grad_ref,
    ) = refs[-12:]
    j = pl.program_id(0)
    size = contexts[0].shape[1]
    sides = side(flipped_ref[0], hidden_ref.shape[1] // 2)

    @pl.when(j == 0)
    def _():
        context = jnp.concatenate(
            [ref[...].reshape(-1, ref.shape[2]).astype(f32).T for ref in contexts], axis=0
        ).astype(bf16)
        heard_ref[...] = context
        context = context[:, : heads * size]
        for lanes, ref in zip(sides, outs):
            mid_ref[:, lanes] = dot_on(context, ref[...], 1, 1)
        mid = hidden_ref[...].astype(f32) + mid_ref[...]
        mid_ref[...] = mid
        total_ref[...] = mid
        normed_ref[...] = rms_norm(mid, gain_ref[...]).astype(bf16)
        grad_ref[...] = jnp.zeros_like(grad_ref)

    def over_width(left_ref, rights):
        own, other = (
            jnp.dot(left_ref[:, lanes], ref[...], preferred_element_type=f32)
            for lanes, ref in zip(sides, rights)
        )
        return own + other

    gate = over_width(normed_ref, gates)
    up = over_width(normed_ref, ups)
    grad_inner = over_width(cot_ref, downs)
    slope = 0.7978845608028654
    square = gate * gate
    bent = jnp.tanh(slope * (gate + 0.044715 * (square * gate)))
    half = 0.5 * (1.0 + bent)
    gelu = gate * half
    gelu_grad = half + (0.5 * gate) * (1.0 - bent * bent) * (
        slope * (1.0 + (3 * 0.044715) * square)
    )
    inner = (gelu * up).astype(bf16)
    grad_gate = (grad_inner * up * gelu_grad).astype(bf16)
    grad_up = (grad_inner * gelu).astype(bf16)
    for k, part in enumerate((grad_gate, grad_up, inner)):
        packet_ref[k] = part
    for k, lanes in enumerate(sides):
        total_ref[:, lanes] = total_ref[:, lanes] + dot_on(inner, downs[k][...], 1, 1)
        grad_ref[:, lanes] = (
            grad_ref[:, lanes]
            + dot_on(grad_gate, gates[k][...], 1, 1)
            + dot_on(grad_up, ups[k][...], 1, 1)
        )

    @pl.when(j == steps - 1)
    def _():
        result_ref[...] = total_ref[...].astype(bf16)
        mid = mid_ref[...]
        scale = lax.rsqrt(jnp.mean(mid * mid, axis=-1, keepdims=True) + norm_eps)
        grad_normed = grad_ref[...]
        gained = grad_normed * gain_ref[...]
        inward = jnp.mean(gained * mid, axis=-1, keepdims=True)
        grad_mid = cot_ref[...].astype(f32) + scale * gained - mid * (scale * scale * scale * inward)
        grad_mid_ref[...] = grad_mid
        branch_ref[...] = grad_mid.astype(bf16)
        grad_context = over_width(branch_ref, outs).T.astype(bf16)
        grad_context_ref[...] = jnp.zeros_like(grad_context_ref)
        for h in range(heads):
            grad_context_ref[h] = grad_context[h * size : (h + 1) * size, :]
        own, other = sides
        half = hidden_ref.shape[1] // 2
        for k, ref in enumerate((normed_ref, cot_ref, branch_ref)):
            left_ref[:, k * half : (k + 1) * half] = ref[:, own]
            other_left_ref[:, k * half : (k + 1) * half] = ref[:, other]


def feed(flipped, hidden, contexts, cot, gain, weights, heads, *after):
    tok, width = hidden.shape
    blocks, size, _ = contexts[0].shape
    micro = len(contexts)
    inner_width = heads * size
    units = (weights[0].shape[1] - inner_width) // 3
    steps = units // feed_chunk
    assert 3 * units % inner_width == 0
    whole = lambda *shape: pl.BlockSpec(shape, lambda j: (0,) * len(shape))
    column = lambda offset: pl.BlockSpec((width // 2, feed_chunk), lambda j: (0, offset + j))
    spot = 3 * units // inner_width
    weight_specs = [pl.BlockSpec((width // 2, inner_width), lambda j: (0, spot))] * 2
    for k in range(3):
        weight_specs += [column(k * steps)] * 2
    return pl.pallas_call(
        functools.partial(feed_kernel, heads, steps, micro),
        grid=(steps,),
        in_specs=[
            pl.BlockSpec(memory_space=pltpu.SMEM),
            whole(tok, width),
            whole(tok, width),
            whole(1, width),
            *[whole(*context.shape) for context in contexts],
            *weight_specs,
        ]
        + [pl.BlockSpec(memory_space=pl.ANY)] * len(after),
        out_specs=[
            whole(tok, width),
            whole(tok, width),
            whole(blocks, size, tok),
            pl.BlockSpec((3, tok, feed_chunk), lambda j: (0, 0, j)),
            whole(tok, blocks * size),
            whole(tok, 3 * (width // 2)),
            whole(tok, 3 * (width // 2)),
        ],
        out_shape=[
            jax.ShapeDtypeStruct((tok, width), bf16),
            jax.ShapeDtypeStruct((tok, width), f32),
            jax.ShapeDtypeStruct((blocks, size, tok), bf16),
            jax.ShapeDtypeStruct((3, tok, units), bf16),
            jax.ShapeDtypeStruct((tok, blocks * size), bf16),
            jax.ShapeDtypeStruct((tok, 3 * (width // 2)), bf16),
            jax.ShapeDtypeStruct((tok, 3 * (width // 2)), bf16),
        ],
        scratch_shapes=[pltpu.VMEM((tok, width), bf16)] * 2 + [pltpu.VMEM((tok, width), f32)] * 3,
        compiler_params=pltpu.CompilerParams(vmem_limit_bytes=vmem_bytes),
        cost_estimate=cost(8),
        name="feed",
    )(flipped, hidden, cot, gain, *contexts, *weights * 4, *after)


def store_tall(ref, parts):
    for m, part in enumerate(parts):
        tok = part.shape[0]
        ref[:, m * tok : (m + 1) * tok] = part.astype(f32).T.astype(bf16)


def weight_grad_kernel(counts, parts, half, *refs):
    j = pl.program_id(0)
    out_ref, tall_ref = refs[-2:]
    lefts, packets, heard = (refs[k * parts : (k + 1) * parts] for k in range(3))
    start = 0
    for k, count in counts:

        @pl.when(j == start)
        def _(k=k):
            store_tall(tall_ref, [ref[:, k * half : (k + 1) * half] for ref in lefts])

        start += count

    def product(rights):
        right = jnp.concatenate([ref[...] for ref in rights], axis=0)
        out_ref[...] = jnp.dot(tall_ref[...], right, preferred_element_type=f32).astype(bf16)

    @pl.when(j < start - counts[-1][1])
    def _():
        product(packets)

    @pl.when(j >= start - counts[-1][1])
    def _():
        product(heard)


def weight_grads(lefts, packets, heard, inner_width, *after):
    tok, half = lefts[0].shape[0], lefts[0].shape[1] // 3
    block = grad_chunk
    units, wide = packets[0].shape[2], heard[0].shape[1]
    steps, more = units // block, wide // block
    counts = [(0, 2 * steps), (1, steps), (2, more)]
    place = lambda j: jnp.minimum(j, 3 * steps - 1)
    return pl.pallas_call(
        functools.partial(weight_grad_kernel, counts, len(lefts), half),
        grid=(3 * steps + more,),
        in_specs=[pl.BlockSpec((tok, 3 * half), lambda j: (0, 0))] * len(lefts)
        + [
            pl.BlockSpec((None, tok, block), lambda j: (place(j) // steps, 0, place(j) % steps))
        ]
        * len(packets)
        + [pl.BlockSpec((tok, block), lambda j: (0, jnp.clip(j - 3 * steps, 0, more - 1)))]
        * len(heard)
        + [pl.BlockSpec(memory_space=pl.ANY)] * len(after),
        out_specs=pl.BlockSpec((half, block), lambda j: (0, j)),
        out_shape=jax.ShapeDtypeStruct((half, 3 * units + inner_width), bf16),
        scratch_shapes=[pltpu.VMEM((half, len(lefts) * tok), bf16)],
        compiler_params=pltpu.CompilerParams(vmem_limit_bytes=vmem_bytes),
        cost_estimate=cost(10),
        name="weight_grads",
    )(*lefts, *packets, *heard, *after)


def project_kernel(
    heads, flipped_ref, matrix_ref, inputs_ref, own_ref, other_ref, after_ref, *refs
):
    micro, tok, width = inputs_ref.shape
    sent, (tokens_ref, normed_ref, gain_a_ref, gain_f_ref, gains_ref) = refs[:micro], refs[micro:]
    inner_width = (own_ref.shape[1] - 128) // 3
    size = inner_width // heads
    sides = side(flipped_ref[0], width // 2)
    for lanes, ref in zip(sides, (own_ref, other_ref)):
        gains_ref[:, lanes] = ref[:, 3 * inner_width :].astype(f32).T[:8]
    gain_a_ref[...] = gains_ref[:1]
    gain_f_ref[...] = gains_ref[1:2]
    hidden = jnp.dot(
        inputs_ref[...].reshape(micro * tok, width), matrix_ref[...], preferred_element_type=f32
    )
    tokens_ref[...] = hidden.astype(bf16).reshape(micro, tok, width)
    normed_ref[...] = rms_norm(hidden, gains_ref[:1]).astype(bf16)
    for ref in sent:
        ref[heads:] = jnp.zeros((ref.shape[0] - heads,) + ref.shape[1:], bf16)
    for k in range(3):
        for half in range(2):
            start = k * inner_width + half * (inner_width // 2)
            own, other = (
                jnp.dot(
                    normed_ref[:, lanes],
                    ref[:, start : start + inner_width // 2],
                    preferred_element_type=f32,
                )
                for lanes, ref in zip(sides, (own_ref, other_ref))
            )
            part = (own + other).T.astype(bf16)
            for h in range(heads // 2):
                for m, ref in enumerate(sent):
                    ref[half * (heads // 2) + h, k * size : (k + 1) * size, :] = part[
                        h * size : (h + 1) * size, m * tok : (m + 1) * tok
                    ]


def project(flipped, matrix, inputs, weights, heads, blocks, after):
    micro, tok, width = inputs.shape
    size = (weights[0].shape[1] - 128) // 3 // heads
    vmem = pl.BlockSpec(memory_space=pltpu.VMEM)
    outs = pl.pallas_call(
        functools.partial(project_kernel, heads),
        in_specs=[
            pl.BlockSpec(memory_space=pltpu.SMEM),
            vmem,
            vmem,
            vmem,
            vmem,
            pl.BlockSpec(memory_space=pl.ANY),
        ],
        out_shape=[jax.ShapeDtypeStruct((blocks, 3 * size, tok), bf16)] * micro
        + [
            jax.ShapeDtypeStruct((micro, tok, width), bf16),
            jax.ShapeDtypeStruct((micro * tok, width), bf16),
            jax.ShapeDtypeStruct((1, width), f32),
            jax.ShapeDtypeStruct((1, width), f32),
        ],
        scratch_shapes=[pltpu.VMEM((8, width), f32)],
        compiler_params=pltpu.CompilerParams(vmem_limit_bytes=few_bytes),
        cost_estimate=cost(3),
        name="project",
    )(flipped, matrix, inputs, *weights, after)
    return outs[:micro], *outs[micro:]


def lined(refs, heads, size, lined_ref):
    tok = refs[0].shape[2]
    for m, ref in enumerate(refs):
        for k in range(3):
            for h in range(heads):
                start = (k * heads + h) * size
                lined_ref[start : start + size, m * tok : (m + 1) * tok] = ref[
                    h, k * size : (k + 1) * size, :
                ]


def input_grad_kernel(heads, micro, *refs):
    flipped_ref, matrix_ref, inputs_ref, own_weights, other_weights, gains_ref = refs[:6]
    mid_ref, *grads = refs[6 : 7 + micro]
    result_ref, input_grad_ref, placed_ref, wide_ref, lined_ref = refs[6 + 1 + micro], *refs[-4:]
    tok, width = inputs_ref.shape[1:]
    inner_width = (own_weights.shape[1] - 128) // 3
    sides = side(flipped_ref[0], width // 2)
    lined(grads, heads, inner_width // heads, lined_ref)
    for ref, rows in zip((own_weights, other_weights), sides):
        wide_ref[rows, :] = jnp.dot(
            ref[:, : 3 * inner_width], lined_ref[...], preferred_element_type=f32
        )
    placed_ref[...] = dot_on(result_ref[...], matrix_ref[...], 1, 1).astype(bf16)
    gain = gains_ref[...]
    for m in range(micro):
        grad = wide_ref[:, m * tok : (m + 1) * tok].T
        hidden = inputs_ref[m].astype(f32)
        scale = lax.rsqrt(jnp.mean(hidden * hidden, axis=-1, keepdims=True) + norm_eps)
        gained = grad * gain
        inward = jnp.mean(gained * hidden, axis=-1, keepdims=True)
        found = mid_ref[m * tok : (m + 1) * tok, :] + scale * gained - hidden * (scale * scale * scale * inward)
        high = found.astype(bf16)
        rest = found - high.astype(f32)
        middle = rest.astype(bf16)
        low = (rest - middle.astype(f32)).astype(bf16)
        input_grad_ref[m] = sum(
            dot_on(part, matrix_ref[...], 1, 1) for part in (low, middle, high)
        )


def input_grads(flipped, matrix, inputs, weights, gains, grads, mid, result, heads, *after):
    micro, tok, width = inputs.shape
    inner_width = (weights[0].shape[1] - 128) // 3
    vmem = pl.BlockSpec(memory_space=pltpu.VMEM)
    return pl.pallas_call(
        functools.partial(input_grad_kernel, heads, micro),
        in_specs=[pl.BlockSpec(memory_space=pltpu.SMEM)]
        + [vmem] * (7 + micro)
        + [pl.BlockSpec(memory_space=pl.ANY)] * len(after),
        out_shape=[
            jax.ShapeDtypeStruct((micro, tok, width), f32),
            jax.ShapeDtypeStruct(result.shape, bf16),
        ],
        scratch_shapes=[
            pltpu.VMEM((width, micro * tok), f32),
            pltpu.VMEM((3 * inner_width, micro * tok), bf16),
        ],
        compiler_params=pltpu.CompilerParams(vmem_limit_bytes=vmem_bytes),
        cost_estimate=cost(6),
        name="input_grads",
    )(flipped, matrix, inputs, *weights, gains, mid, *grads, result, *after)


def front_grad_kernel(heads, parts, half, which, *refs):
    flipped_ref = refs[0]
    lefts, grads = refs[1 : 1 + parts], refs[1 + parts : 1 + 2 * parts]
    out_ref, tall_ref, lined_ref = refs[-3:]
    _, size, tok = grads[0].shape

    @pl.when(pl.program_id(0) == 0)
    def _():
        lanes = side(flipped_ref[0], half)[which]
        for p, ref in enumerate(lefts):
            tall = ref[:, lanes].astype(f32).T.astype(bf16)
            tall_ref[:, p * tok : (p + 1) * tok] = tall

    for p, ref in enumerate(grads):
        lined_ref[:, p * tok : (p + 1) * tok] = ref[:heads].reshape(heads * size, tok)
    out_ref[...] = dot_on(tall_ref[...], lined_ref[...], 1, 1).astype(bf16)


def front_grads(flipped, lefts, grads, inner_width, heads, which):
    tok, width = lefts[0].shape
    parts = len(lefts)
    part = pl.BlockSpec((grads[0].shape[0], inner_width // heads, tok), lambda k: (0, k, 0))
    return pl.pallas_call(
        functools.partial(front_grad_kernel, heads, parts, width // 2, which),
        grid=(3,),
        in_specs=[pl.BlockSpec(memory_space=pltpu.SMEM)]
        + [pl.BlockSpec((tok, width), lambda k: (0, 0))] * parts
        + [part] * parts,
        out_specs=pl.BlockSpec((width // 2, inner_width), lambda k: (0, k)),
        out_shape=jax.ShapeDtypeStruct((width // 2, 3 * inner_width), bf16),
        scratch_shapes=[
            pltpu.VMEM((width // 2, parts * tok), bf16),
            pltpu.VMEM((inner_width, parts * tok), bf16),
        ],
        compiler_params=pltpu.CompilerParams(vmem_limit_bytes=few_bytes),
        cost_estimate=cost(5),
        name="front_grads",
    )(flipped, *lefts, *grads)


def row_of(column):
    share = column.shape[0]
    shape = (share, share)
    spread = lax.broadcasted_iota(jnp.int32, shape, 0) == lax.broadcasted_iota(jnp.int32, shape, 1)
    return jnp.sum(jnp.where(spread, column, 0.0), axis=0, keepdims=True)


def gain_grad_of(weights, grads, gain_ref):
    total = sum(
        jnp.sum(weight[...].astype(f32) * grad[...], axis=1, keepdims=True)
        for weight, grad in zip(weights, grads)
    )
    return row_of(total) / gain_ref[...].astype(f32)


def unpack_back_kernel(sums_ref, gate_ref, up_ref, gain_ref, *refs):
    gate_grad_ref, up_grad_ref, down_grad_ref, out_grad_ref, gain_grad_ref = refs
    units = gate_ref.shape[1]
    for k, ref in enumerate((gate_grad_ref, up_grad_ref, down_grad_ref, out_grad_ref)):
        ref[...] = sums_ref[:, k * units : k * units + ref.shape[1]].astype(f32)
    gain_grad_ref[...] = gain_grad_of((gate_ref, up_ref), (gate_grad_ref, up_grad_ref), gain_ref)


def unpack_back(sums, w_gate, w_up, gain, inner_width):
    share, units = w_gate.shape
    shapes = [(share, units)] * 3 + [(share, inner_width), (1, share)]
    gate, up, down, out, gain_grad = pl.pallas_call(
        unpack_back_kernel,
        out_shape=[jax.ShapeDtypeStruct(shape, f32) for shape in shapes],
        compiler_params=pltpu.CompilerParams(vmem_limit_bytes=few_bytes),
        name="unpack_back",
    )(sums, w_gate, w_up, gain[None, :])
    return gate, up, down.T, out.T, gain_grad[0]


def unpack_front_kernel(parts_ref, query_ref, key_ref, value_ref, gain_ref, after_ref, *refs):
    grads, gain_grad_ref = refs[:3], refs[3]
    width = query_ref.shape[1]
    for k, ref in enumerate(grads):
        part = parts_ref[:, :, k * width : (k + 1) * width].astype(f32)
        ref[...] = jnp.sum(part, axis=0)
    gain_grad_ref[...] = gain_grad_of((query_ref, key_ref, value_ref), grads, gain_ref)


def unpack_front(parts, w_query, w_key, w_value, gain, after):
    share, width = w_query.shape
    vmem = pl.BlockSpec(memory_space=pltpu.VMEM)
    shapes = [(share, width)] * 3 + [(1, share)]
    query, key, value, gain_grad = pl.pallas_call(
        unpack_front_kernel,
        in_specs=[vmem] * 5 + [pl.BlockSpec(memory_space=pl.ANY)],
        out_shape=[jax.ShapeDtypeStruct(shape, f32) for shape in shapes],
        compiler_params=pltpu.CompilerParams(vmem_limit_bytes=few_bytes),
        name="unpack_front",
    )(parts, w_query, w_key, w_value, gain[None, :], after)
    return query, key, value, gain_grad[0]


def body(
    inputs, doc_lengths, attn_gain, w_query, w_key, w_value, w_out, ff_gain,
    w_gate, w_up, w_down, rel_table, cotangent,
):
    micro, _, tok, width = inputs.shape
    inner_width = w_query.shape[1]
    hidden_units = w_gate.shape[1]
    buckets, heads = rel_table.shape
    size = inner_width // heads
    blocks = lax.axis_size("blk")
    rows = lax.axis_size("rows")
    me = lax.axis_index("blk")
    share = w_query.shape[0]
    micros = range(micro)

    flipped = lax.axis_index("rows") if staged(rows, blocks, share) else 0
    flipped = jnp.full((1,), flipped, jnp.int32)
    matrix = stage_matrix(rows, blocks, share)
    head = jnp.minimum(me, heads - 1).astype(jnp.int32).reshape(1)
    table = rel_table.astype(f32).reshape(-1)

    with jax.named_scope("weights"):
        front_full = gather_front(w_query, w_key, w_value, attn_gain, ff_gain)
        back_own = gather_back(jnp.concatenate([w_gate, w_up, w_down.T, w_out.T], axis=1), front_full[0])

    band = bias_tiles(head, table, buckets)
    sent, tokens, normed_a, gain_a, gain_f = project(
        flipped, matrix, inputs[:, 0], front_full, heads, blocks, band
    )
    taken = []
    for m in micros:
        with jax.named_scope("project"):
            part = tie(sent[m], taken[-1]) if m else sent[m]
            taken.append(lax.all_to_all(part, "blk", 0, 0, tiled=True))

    cots = reorder(cotangent[:, 0].reshape(micro * tok, width), matrix)
    kept, contexts, half = [], [], blocks // 4 // subs
    for m in micros:
        given = taken[m], doc_lengths[m, 0], head, table, band, buckets
        outs = [k[0] for k in kept]
        if m:
            outs = attend(*given, 0, half, [], *outs, cots)
            outs = attend(*given, half, None, outs, *contexts)
        else:
            outs = attend(*given, 0, None, [])
        kept.append(outs[1:])
        with jax.named_scope("context"):
            contexts.append(lax.all_to_all(outs[0], "blk", 0, 0, tiled=True))
    with jax.named_scope("weights"):
        back_full = gather_other(back_own, outs[0])

    fits = staged(rows, blocks, share)
    here = micro * tok
    result, grad_mid, grad_context, mine, heard, left, left_other = feed(
        flipped, tokens.reshape(here, width), contexts, cots, gain_f, back_full, heads,
    )
    with jax.named_scope("grad_context"):
        grads = lax.all_to_all(grad_context, "blk", 0, 0, tiled=True)
    if fits:
        with jax.named_scope("packet"):
            packet, near_heard, near_left = (flip(a, "rows", 1) for a in (mine, heard, left_other))

    with jax.named_scope("back_grads"):
        if fits:
            own = weight_grads([left, near_left], [mine, packet], [heard, near_heard], inner_width)
            own = tie(own, grads)
            back_grad = scatter_back(own)
        else:
            own, other = (
                weight_grads([lefts], [mine], [heard], inner_width) for lefts in (left, left_other)
            )
            back_grad = scatter_whole(own, other)
    grad_qkv, found = [], jnp.zeros((1, chunk // 2), f32)
    for m in micros:
        returned, found = attend_back(
            taken[m], grads, *kept[m], buckets, m, m == micro - 1, found, own
        )
        with jax.named_scope("grad_qkv"):
            returned = tie(returned, *grad_qkv) if m else returned
            grad_qkv.append(lax.all_to_all(returned, "blk", 0, 0, tiled=True))

    with jax.named_scope("table"):
        pieces = grad_qkv[-1][:heads, 3 * size : 3 * size + 3, :buckets]
        table_grad = jnp.sum(pieces.astype(f32), axis=1).T
        for bit in bits_of(rows):
            table_grad = table_grad + flip(table_grad, "rows", bit)

    with jax.named_scope("front_grads"):
        normed = [normed_a[m * tok : (m + 1) * tok] for m in micros]
        if fits:
            near_grads = [flip(g, "rows", 1) for g in grad_qkv]
            near_normed = [flip(n, "rows", 1) for n in normed]
            own = front_grads(
                flipped, normed + near_normed, grad_qkv + near_grads, inner_width, heads, 0
            )
            back_grad = scatter_back_end(back_grad, own)
            front_parts = scatter_front(own, share)
        else:
            own, other = (
                front_grads(flipped, normed, grad_qkv, inner_width, heads, which)
                for which in (0, 1)
            )
            front_parts = scatter_whole(own, other)[None]
    input_grad, result = input_grads(
        flipped, matrix, tokens, front_full, gain_a, grad_qkv, grad_mid, result, heads, own
    )
    if fits:
        with jax.named_scope("front_grads"):
            front_parts = scatter_front_end(front_parts, share, input_grad)
    gate_grad, up_grad, down_grad, out_grad, ff_gain_grad = unpack_back(
        back_grad, w_gate, w_up, ff_gain, inner_width
    )
    query_grad, key_grad, value_grad, attn_gain_grad = unpack_front(
        front_parts, w_query, w_key, w_value, attn_gain, gate_grad
    )

    return (
        result.reshape(micro, 1, tok, width),
        input_grad[:, None],
        attn_gain_grad,
        query_grad,
        key_grad,
        value_grad,
        out_grad,
        ff_gain_grad,
        gate_grad,
        up_grad,
        down_grad,
        table_grad,
    )


def solution(mesh):
    weight_rows = P(both, None)
    weight_columns = P(None, both)
    tokens = P(None, "rows", "blk", None)
    in_specs = (
        tokens, P(None, "rows", None), P(both), weight_rows, weight_rows, weight_rows,
        weight_columns, P(both), weight_rows, weight_rows, weight_columns, P(), tokens,
    )
    out_specs = (
        tokens, tokens, P(both), weight_rows, weight_rows, weight_rows,
        weight_columns, P(both), weight_rows, weight_rows, weight_columns, P(),
    )
    return jax.shard_map(body, mesh=mesh, in_specs=in_specs, out_specs=out_specs, check_vma=False)
```

```python
import functools

import jax
import jax.numpy as jnp
import numpy as np
from jax import lax
from jax.experimental import pallas as pl
from jax.experimental.pallas import tpu as pltpu
from jax.sharding import PartitionSpec as P

bucket_edges = (12, 16, 23, 32, 46, 64, 91)
norm_eps = 1e-06
masked_score = -1e30
f32 = jnp.float32
bf16 = jnp.bfloat16
both = ("rows", "blk")
chunk = 256
feed_chunk = 512
grad_chunk = 1024
subs = 2
vmem_bytes = 56 * 1024 * 1024
few_bytes = 40 * 1024 * 1024


def bucket_of(relative, total_buckets):
    half = total_buckets // 2
    exact = half // 2
    distance = jnp.abs(relative)
    far_bucket = exact + sum(((distance >= edge).astype(jnp.int32) for edge in bucket_edges))
    return jnp.where(relative > 0, half, 0) + jnp.where(distance < exact, distance, far_bucket)


def rms_norm(hidden, gain):
    return hidden * lax.rsqrt(jnp.mean(hidden * hidden, axis=-1, keepdims=True) + norm_eps) * gain


def gated(gate, up):
    return jax.nn.gelu(gate, approximate=True) * up


def dot_on(left, right, left_dim, right_dim):
    return lax.dot_general(
        left, right, (((left_dim,), (right_dim,)), ((), ())), preferred_element_type=f32
    )


def flip(array, axis, bit):
    count = lax.axis_size(axis)
    return lax.ppermute(array, axis, [(i, i ^ bit) for i in range(count)])


def bits_of(count):
    return [1 << k for k in range(count.bit_length() - 1)]


def segments_at(bounds, positions):
    total = jnp.zeros(positions.shape, jnp.int32)
    for bound in bounds:
        total = total + (positions >= bound).astype(jnp.int32)
    return total


def groups_of(blocks):
    near = 4
    far = blocks // near
    across = [[f * near + n for f in range(far)] for n in range(near)]
    within = [[f * near + n for n in range(near)] for f in range(far)]
    return far, near, across, within


def staged(rows, blocks, share):
    return rows == 2 and blocks % 4 == 0 and share % 8 == 0


def stage_matrix(rows, blocks, share):
    place = np.arange(rows * blocks * share)
    taken = place
    if staged(rows, blocks, share):
        far, near, _, _ = groups_of(blocks)
        slab = place // share
        half, inner = slab // blocks, slab % blocks
        taken = (half * blocks + inner % far * near + inner // far) * share + place % share
    return jnp.asarray((place[:, None] == taken[None, :]).astype(np.float32), bf16)


def tie_kernel(*refs):
    pass


def tie(value, *after):
    space = pl.BlockSpec(memory_space=pl.ANY)
    return pl.pallas_call(
        tie_kernel,
        in_specs=[space] * (1 + len(after)),
        out_specs=space,
        out_shape=jax.ShapeDtypeStruct(value.shape, value.dtype),
        input_output_aliases={0: 0},
        name="tie",
    )(value, *after)


def exchange(array, groups):
    return lax.all_to_all(array, "blk", 0, 0, tiled=True, axis_index_groups=groups)


def halves_of_whole(whole):
    half = whole.shape[0] // 2
    return whole[:half], whole[half:]


def pack_kernel(query_ref, key_ref, value_ref, gain_a_ref, gain_f_ref, out_ref):
    share = query_ref.shape[0]
    spread = lax.broadcasted_iota(jnp.int32, (share, share), 0) == lax.broadcasted_iota(
        jnp.int32, (share, share), 1
    )
    lane = lax.broadcasted_iota(jnp.int32, (share, 128), 1)
    gains = jnp.zeros((share, 128), f32)
    for k, ref in enumerate((gain_a_ref, gain_f_ref)):
        column = jnp.where(spread, ref[...].astype(f32), 0.0)
        gains = jnp.where(lane == k, jnp.sum(column, axis=1, keepdims=True), gains)
    parts = [query_ref[...], key_ref[...], value_ref[...], gains.astype(bf16)]
    packed = jnp.concatenate(parts, axis=1)
    for copy in range(out_ref.shape[0]):
        out_ref[copy] = packed


def pack(query, key, value, gain_a, gain_f, copies):
    shape = (copies, query.shape[0], 3 * query.shape[1] + 128)
    return pl.pallas_call(
        pack_kernel,
        out_shape=jax.ShapeDtypeStruct(shape, bf16),
        compiler_params=pltpu.CompilerParams(vmem_limit_bytes=vmem_bytes),
        name="pack",
    )(query, key, value, gain_a[None, :], gain_f[None, :])


def gather_front(*parts):
    blocks, rows = lax.axis_size("blk"), lax.axis_size("rows")
    if not staged(rows, blocks, parts[0].shape[0]):
        shard = pack(*parts, 1)[0]
        return halves_of_whole(lax.all_gather(shard, both, axis=0, tiled=True))
    far, near, across, within = groups_of(blocks)
    packed = pack(*parts, far)
    first = exchange(packed.reshape(-1, packed.shape[2]), across)
    own = exchange(jnp.tile(first, (near, 1)), within)
    return own, flip(own, "rows", 1)


def gather_back(shard, after):
    blocks, rows = lax.axis_size("blk"), lax.axis_size("rows")
    if not staged(rows, blocks, shard.shape[0]):
        return lax.all_gather(shard, both, axis=0, tiled=True)
    far, near, across, within = groups_of(blocks)
    own = lax.all_gather(shard, "blk", axis=0, tiled=True, axis_index_groups=across)
    own = tie(own, after)
    return lax.all_gather(own, "blk", axis=0, tiled=True, axis_index_groups=within)


def gather_other(own, after):
    blocks, rows = lax.axis_size("blk"), lax.axis_size("rows")
    if not staged(rows, blocks, own.shape[0] // blocks):
        return halves_of_whole(own)
    own = tie(own, after)
    return own, flip(own, "rows", 1)


def scatter_front(own, share):
    far, near, _, within = groups_of(lax.axis_size("blk"))
    held = exchange(own, within).reshape(near, far * share, own.shape[1])
    return jnp.sum(held.astype(f32), axis=0).astype(bf16)


def scatter_front_end(held, share, *after):
    far, _, across, _ = groups_of(lax.axis_size("blk"))
    return exchange(tie(held, *after), across).reshape(far, share, held.shape[1])


def scatter_back(own):
    _, _, _, within = groups_of(lax.axis_size("blk"))
    return lax.psum_scatter(
        own, "blk", scatter_dimension=0, axis_index_groups=within, tiled=True
    )


def scatter_back_end(part, after):
    _, _, across, _ = groups_of(lax.axis_size("blk"))
    return lax.psum_scatter(
        tie(part, after), "blk", scatter_dimension=0, axis_index_groups=across, tiled=True
    )


def scatter_whole(own, other):
    whole = jnp.concatenate([own, other], axis=0)
    return lax.psum_scatter(whole, both, scatter_dimension=0, tiled=True)


def side(flipped, half):
    return (
        pl.ds(pl.multiple_of(flipped * half, half), half),
        pl.ds(pl.multiple_of((1 - flipped) * half, half), half),
    )


def cost(micros):
    return pl.CostEstimate(flops=int(micros * 1e9), bytes_accessed=0, transcendentals=0)


def tile_rows(ref, index, start, stop):
    return jnp.concatenate(
        [ref[2 * index, start:stop, :], ref[2 * index + 1, start:stop, :]], axis=1
    )


def steps_of(buckets):
    half = buckets // 2
    exact = half // 2
    lows = list(range(1, exact)) + [exact] + list(bucket_edges)
    places = [(1 - low, k) for k, low in reversed(list(enumerate(lows)))]
    return half - 1, places + [(low, half + 1 + k) for k, low in enumerate(lows)]


def relative_tile(j):
    shape = (chunk, chunk)
    return (
        lax.broadcasted_iota(jnp.int32, shape, 0)
        - lax.broadcasted_iota(jnp.int32, shape, 1)
        + j * chunk
    )


def bias_kernel(buckets, heads, head_ref, table_ref, band_ref):
    first, places = steps_of(buckets)
    value = lambda bucket: table_ref[bucket * heads + head_ref[0]]
    for j in (-1, 0, 1):
        relative = relative_tile(j)
        tile = jnp.full((chunk, chunk), value(first), f32)
        for place, bucket in places:
            tile = jnp.where(relative >= place, value(bucket), tile)
        band_ref[j + 1] = tile


def bias_tiles(head, table, buckets):
    smem = pl.BlockSpec(memory_space=pltpu.SMEM)
    return pl.pallas_call(
        functools.partial(bias_kernel, buckets, table.shape[0] // buckets),
        in_specs=[smem, smem],
        out_shape=jax.ShapeDtypeStruct((3, chunk, chunk), f32),
        compiler_params=pltpu.CompilerParams(vmem_limit_bytes=vmem_bytes),
        cost_estimate=cost(2),
        name="bias_tiles",
    )(head, table)


def table_sums(buckets, band_ref, far_ref, sums_ref):
    first, places = steps_of(buckets)
    edge = chunk // 2
    reach = -(-bucket_edges[-1] // 8) * 8
    sums_ref[...] = jnp.zeros_like(sums_ref)
    relative = [relative_tile(j) for j in (-1, 0, 1)]

    def fold(tile):
        return jnp.sum(tile.reshape(-1, 8, tile.shape[1]), axis=0)

    above = fold(band_ref[0]) + fold(band_ref[1]) + fold(band_ref[2])
    for q in range(far_ref.shape[2] // chunk):
        spot = slice(q * chunk, (q + 1) * chunk)
        above = above + far_ref[0, :, spot] * 0.125 + far_ref[1, :, spot] * 0.125
    right = fold(band_ref[2])
    for q in range(far_ref.shape[2] // chunk):
        right = right + far_ref[1, :, q * chunk : (q + 1) * chunk] * 0.125
    corner = band_ref[2, :reach, edge:]
    corner_relative = relative[2][:reach, edge:]
    left_corner = band_ref[0, chunk - reach :, :edge]
    left_relative = relative[0][chunk - reach :, :edge]
    bucket = first
    for place, following in places:
        if place > 0:
            after = right[:, :edge] + right[:, edge:]
            after = after - fold(jnp.where(corner_relative < place, corner, 0.0))
        else:
            after = right[:, :edge] + right[:, edge:]
            after = after + fold(jnp.where(left_relative >= place, left_corner, 0.0))
        part = fold(jnp.where(relative[1] >= place, band_ref[1], 0.0))
        after = after + part[:, :edge] + part[:, edge:]
        if above.shape[1] == chunk:
            above = above[:, :edge] + above[:, edge:]
        sums_ref[bucket : bucket + 1, :] = jnp.sum(above - after, axis=0, keepdims=True)
        above, bucket = after, following
    sums_ref[bucket : bucket + 1, :] = jnp.sum(above, axis=0, keepdims=True)
    found = jnp.sum(sums_ref[...], axis=1, keepdims=True)
    shape = (buckets, edge)
    spread = lax.broadcasted_iota(jnp.int32, shape, 0) == lax.broadcasted_iota(jnp.int32, shape, 1)
    return jnp.sum(jnp.where(spread, found, 0.0), axis=0, keepdims=True)


def table_pieces(found):
    high = found.astype(bf16).astype(f32)
    middle = (found - high).astype(bf16).astype(f32)
    pieces = [high, middle, found - high - middle, jnp.zeros((13, found.shape[1]), f32)]
    return jnp.concatenate(pieces, axis=0).astype(bf16)


def attend_kernel(
    size, blocks, docs, buckets, first, bounds_ref, head_ref, table_ref, taken_ref, band_ref, *refs
):
    sent_ref, context_ref, expo_ref, scale_ref, keys_ref, *scratch = refs[-5 - 2 * subs :]
    step = pl.program_id(0) + first
    chunks = blocks // 2
    tok = chunk // 2
    bounds = [bounds_ref[0]]
    for d in range(1, docs):
        bounds.append(bounds[-1] + bounds_ref[d])
    heads = table_ref.shape[0] // buckets
    entry = lambda bucket: table_ref[bucket * heads + head_ref[0]]

    @pl.when(step == first)
    def _():
        for s in range(blocks):
            position = s * tok + lax.broadcasted_iota(jnp.int32, (1, tok), 1)
            segment = segments_at(bounds, position)
            row = lax.broadcasted_iota(jnp.int32, (16, tok), 0)
            own = jnp.where(row == segment, 1.0, 0.0)
            part = jnp.where(row == s // 2, 1.0, 0.0)
            tall = jnp.concatenate(
                [
                    taken_ref[s, size : 2 * size, :].astype(f32),
                    own,
                    part,
                    jnp.zeros((size - 32, tok), f32),
                ],
                axis=0,
            )
            keys_ref[s * tok : (s + 1) * tok, :] = tall.T.astype(bf16)
        for query_ref in scratch[::2]:
            query_ref[size:, :] = jnp.zeros((size, chunk), bf16)

    def turned(block, d):
        c = block + d
        return jnp.where(c >= chunks, c - chunks, c)

    blocks_here = [step * subs + k for k in range(subs)]
    tops = []
    for k, block in enumerate(blocks_here):
        query_ref, score_ref = scratch[2 * k : 2 * k + 2]
        position = block * chunk + lax.broadcasted_iota(jnp.int32, (1, chunk), 1)
        segment = segments_at(bounds, position)
        row = lax.broadcasted_iota(jnp.int32, (16, chunk), 0)
        query_ref[:size, :] = tile_rows(taken_ref, block, 0, size)
        query_ref[size : size + 16, :] = jnp.where(row == segment, 0.0, masked_score).astype(bf16)
        far = jnp.where(
            row <= block - 2,
            entry(buckets // 2 - 1),
            jnp.where(row >= block + 2, entry(buckets - 1), 0.0),
        )
        query_ref[size + 16 : size + 32, :] = far.astype(bf16)
        query = query_ref[...]
        top = jnp.full((8, chunk), masked_score, f32)
        for d in range(chunks):
            spot = pl.ds(pl.multiple_of(turned(block, d) * chunk, chunk), chunk)
            scores = jnp.dot(keys_ref[spot, :], query, preferred_element_type=f32)
            if d == 0:
                scores = scores + band_ref[1]
            elif d == 1:
                scores = scores + jnp.where(block + 1 < chunks, 1.0, 0.0) * band_ref[2]
            elif d == chunks - 1:
                scores = scores + jnp.where(block >= 1, 1.0, 0.0) * band_ref[0]
            score_ref[d * chunk : (d + 1) * chunk, :] = scores
            top = jnp.maximum(top, jnp.max(scores.reshape(chunk // 8, 8, chunk), axis=0))
        tops.append(jnp.max(top, axis=0, keepdims=True))
    for k, block in enumerate(blocks_here):
        score_ref = scratch[2 * k + 1]
        lanes = slice(k * chunk, (k + 1) * chunk)
        total = jnp.zeros((8, chunk), f32)
        context = jnp.zeros((size, chunk), f32)
        for d in range(chunks):
            c = turned(block, d)
            expo = jnp.exp(score_ref[d * chunk : (d + 1) * chunk, :] - tops[k])
            total = total + jnp.sum(expo.reshape(chunk // 8, 8, chunk), axis=0)
            low = expo.astype(bf16)
            expo_ref[pl.ds(pl.multiple_of(c * chunk, chunk), chunk), lanes] = low
            context = context + jnp.dot(
                tile_rows(taken_ref, c, 2 * size, 3 * size), low, preferred_element_type=f32
            )
        scale = 1.0 / jnp.sum(total, axis=0, keepdims=True)
        context = context * scale
        context_ref[:, lanes] = context
        scale_ref[:, lanes] = scale
        sent_ref[2 * k] = context[:, :tok].astype(bf16)
        sent_ref[2 * k + 1] = context[:, tok:].astype(bf16)


def attend(taken, lengths, head, table, band, buckets, first, stop, given, *after):
    blocks, size, tok = taken.shape
    size = size // 3
    length = blocks * tok
    smem = pl.BlockSpec(memory_space=pltpu.SMEM)
    return pl.pallas_call(
        functools.partial(attend_kernel, size, blocks, lengths.shape[0], buckets, first),
        grid=((stop or blocks // 2 // subs) - first,),
        in_specs=[
            smem,
            smem,
            smem,
            pl.BlockSpec((blocks, 3 * size, tok), lambda q: (0, 0, 0)),
            pl.BlockSpec((3, chunk, chunk), lambda q: (0, 0, 0)),
        ]
        + [pl.BlockSpec(memory_space=pl.ANY)] * (len(given) + len(after)),
        out_specs=[
            pl.BlockSpec((2 * subs, size, tok), lambda q: (first + q, 0, 0)),
            pl.BlockSpec((size, subs * chunk), lambda q: (0, first + q)),
            pl.BlockSpec((length, subs * chunk), lambda q: (0, first + q)),
            pl.BlockSpec((1, subs * chunk), lambda q: (0, first + q)),
        ],
        out_shape=[
            jax.ShapeDtypeStruct((blocks, size, tok), bf16),
            jax.ShapeDtypeStruct((size, length), f32),
            jax.ShapeDtypeStruct((length, length), bf16),
            jax.ShapeDtypeStruct((1, length), f32),
        ],
        scratch_shapes=[
            pltpu.VMEM((length, 2 * size), bf16),
        ]
        + [
            pltpu.VMEM((2 * size, chunk), bf16),
            pltpu.VMEM((length, chunk), f32),
        ]
        * subs,
        compiler_params=pltpu.CompilerParams(vmem_limit_bytes=vmem_bytes),
        input_output_aliases={5 + k: k for k in range(len(given))},
        cost_estimate=cost(6),
        name="attend",
    )(lengths, head, table, taken, band, *given, *after)


def attend_back_kernel(
    size, blocks, buckets, last, after, taken_ref, grad_ref, context_ref, expo_ref, scale_ref,
    *refs,
):
    before_ref, *refs = refs
    (
        sent_ref, found_ref, band_ref, far_ref, sums_ref,
        queries_ref, wide_ref, delta_ref, grad_queries_ref, grad_scores_ref,
    ) = refs[after:]
    step = pl.program_id(0)
    chunks = blocks // 2
    tok = chunk // 2

    @pl.when(step == 0)
    def _():
        for s in range(blocks):
            spot = slice(s * tok, (s + 1) * tok)
            scaled = grad_ref[s].astype(f32) * scale_ref[:, spot]
            wide_ref[:, spot] = scaled.astype(bf16)
            delta_ref[:, spot] = jnp.sum(scaled * context_ref[:, spot], axis=0, keepdims=True)
            queries_ref[:, spot] = taken_ref[s, :size, :]
        grad_queries_ref[...] = jnp.zeros_like(grad_queries_ref)
        band_ref[...] = jnp.zeros_like(band_ref)
        far_ref[...] = jnp.zeros_like(far_ref)
        for k in range(subs):
            grad_scores_ref[k, :, :chunk] = jnp.zeros((chunk, chunk), bf16)
            grad_scores_ref[k, :, (chunks + 1) * chunk :] = jnp.zeros((chunk, chunk), bf16)

    keys = []
    for k in range(subs):
        c = step * subs + k
        rows = slice(k * chunk, (k + 1) * chunk)
        values = tile_rows(taken_ref, c, 2 * size, 3 * size).astype(f32).T.astype(bf16)
        for q in range(chunks):
            spot = slice(q * chunk, (q + 1) * chunk)
            grad_weights = jnp.dot(values, wide_ref[:, spot], preferred_element_type=f32)
            weights = expo_ref[rows, spot].astype(f32)
            grad_scores = (weights * (grad_weights - delta_ref[:, spot])).astype(bf16)
            grad_scores_ref[k, :, (q + 1) * chunk : (q + 2) * chunk] = grad_scores
        grad_values = dot_on(wide_ref[...], expo_ref[rows, :], 1, 1).astype(bf16)
        grad_keys = dot_on(
            queries_ref[...], grad_scores_ref[k, :, chunk : (chunks + 1) * chunk], 1, 1
        ).astype(bf16)
        for t in range(2):
            sent_ref[2 * c + t, size : 2 * size, :] = grad_keys[:, t * tok : (t + 1) * tok]
            sent_ref[2 * c + t, 2 * size : 3 * size, :] = grad_values[:, t * tok : (t + 1) * tok]
        keys.append(
            jnp.concatenate(
                [tile_rows(taken_ref, c, size, 2 * size), jnp.ones((16, chunk), bf16)], axis=0
            )
        )
    for q in range(chunks):
        spot = slice(q * chunk, (q + 1) * chunk)
        total = grad_queries_ref[:, spot]
        for k in range(subs):
            c = step * subs + k
            part = jnp.dot(
                keys[k],
                grad_scores_ref[k, :, (q + 1) * chunk : (q + 2) * chunk],
                preferred_element_type=f32,
            )
            total = total + part[:size]
            sums = part[size : size + 8]
            far_ref[0, :, spot] = far_ref[0, :, spot] + jnp.where(c <= q - 2, sums, 0.0)
            far_ref[1, :, spot] = far_ref[1, :, spot] + jnp.where(c >= q + 2, sums, 0.0)
        grad_queries_ref[:, spot] = total
    for k in range(subs):
        c = step * subs + k
        for j in (-1, 0, 1):
            spot = pl.ds(pl.multiple_of((c - j + 1) * chunk, chunk), chunk)
            band_ref[j + 1] = band_ref[j + 1] + grad_scores_ref[k, :, spot].astype(f32)

    @pl.when(step == chunks // subs - 1)
    def _():
        for s in range(blocks):
            sent_ref[s, :size, :] = grad_queries_ref[:, s * tok : (s + 1) * tok].astype(bf16)
        found = before_ref[...] + table_sums(buckets, band_ref, far_ref, sums_ref)
        found_ref[...] = found
        if last:
            pieces = table_pieces(found)
            for s in range(blocks):
                sent_ref[s, 3 * size :, :] = pieces


def attend_back(taken, grads, context, expo, scale, buckets, m, last, before, *after):
    blocks, size, _ = grads.shape
    tok = taken.shape[2]
    length = expo.shape[0]
    height = 3 * size + 16 if last else 3 * size
    return pl.pallas_call(
        functools.partial(attend_back_kernel, size, blocks, buckets, last, len(after)),
        grid=(blocks // 2 // subs,),
        in_specs=[
            pl.BlockSpec((blocks, 3 * size, tok), lambda c: (0, 0, 0)),
            pl.BlockSpec((blocks, size, tok), lambda c: (0, 0, m)),
            pl.BlockSpec((size, length), lambda c: (0, 0)),
            pl.BlockSpec((subs * chunk, length), lambda c: (c, 0)),
            pl.BlockSpec((1, length), lambda c: (0, 0)),
            pl.BlockSpec((1, chunk // 2), lambda c: (0, 0)),
        ]
        + [pl.BlockSpec(memory_space=pl.ANY)] * len(after),
        out_specs=[
            pl.BlockSpec((blocks, height, tok), lambda c: (0, 0, 0)),
            pl.BlockSpec((1, chunk // 2), lambda c: (0, 0)),
        ],
        out_shape=[
            jax.ShapeDtypeStruct((blocks, height, tok), bf16),
            jax.ShapeDtypeStruct((1, chunk // 2), f32),
        ],
        scratch_shapes=[
            pltpu.VMEM((3, chunk, chunk), f32),
            pltpu.VMEM((2, 8, length), f32),
            pltpu.VMEM((buckets, chunk // 2), f32),
            pltpu.VMEM((size, length), bf16),
            pltpu.VMEM((size, length), bf16),
            pltpu.VMEM((1, length), f32),
            pltpu.VMEM((size, length), f32),
            pltpu.VMEM((subs, chunk, length + 2 * chunk), bf16),
        ],
        compiler_params=pltpu.CompilerParams(vmem_limit_bytes=vmem_bytes),
        cost_estimate=cost(13),
        name="attend_back",
    )(taken, grads, context, expo, scale, before, *after)


def reorder_kernel(array_ref, matrix_ref, out_ref):
    out_ref[...] = jnp.dot(
        array_ref[...], matrix_ref[...], preferred_element_type=f32
    ).astype(bf16)


def reorder(array, matrix):
    return pl.pallas_call(
        reorder_kernel,
        out_shape=jax.ShapeDtypeStruct(array.shape, bf16),
        compiler_params=pltpu.CompilerParams(vmem_limit_bytes=vmem_bytes),
        cost_estimate=cost(2),
        name="reorder",
    )(array, matrix)


def feed_kernel(
    heads, steps, micro, flipped_ref, hidden_ref, cot_ref, gain_ref, *refs
):
    contexts, refs = refs[:micro], refs[micro:]
    outs, gates, ups, downs = (refs[2 * k : 2 * k + 2] for k in range(4))
    (
        result_ref, grad_mid_ref, grad_context_ref, packet_ref, heard_ref, left_ref, other_left_ref,
        normed_ref, branch_ref, mid_ref, total_ref, grad_ref,
    ) = refs[-12:]
    j = pl.program_id(0)
    size = contexts[0].shape[1]
    sides = side(flipped_ref[0], hidden_ref.shape[1] // 2)

    @pl.when(j == 0)
    def _():
        context = jnp.concatenate(
            [ref[...].reshape(-1, ref.shape[2]).astype(f32).T for ref in contexts], axis=0
        ).astype(bf16)
        heard_ref[...] = context
        context = context[:, : heads * size]
        for lanes, ref in zip(sides, outs):
            mid_ref[:, lanes] = dot_on(context, ref[...], 1, 1)
        mid = hidden_ref[...].astype(f32) + mid_ref[...]
        mid_ref[...] = mid
        total_ref[...] = mid
        normed_ref[...] = rms_norm(mid, gain_ref[...]).astype(bf16)
        grad_ref[...] = jnp.zeros_like(grad_ref)

    def over_width(left_ref, rights):
        own, other = (
            jnp.dot(left_ref[:, lanes], ref[...], preferred_element_type=f32)
            for lanes, ref in zip(sides, rights)
        )
        return own + other

    gate = over_width(normed_ref, gates)
    up = over_width(normed_ref, ups)
    grad_inner = over_width(cot_ref, downs)
    slope = 0.7978845608028654
    square = gate * gate
    bent = jnp.tanh(slope * (gate + 0.044715 * (square * gate)))
    half = 0.5 * (1.0 + bent)
    gelu = gate * half
    gelu_grad = half + (0.5 * gate) * (1.0 - bent * bent) * (
        slope * (1.0 + (3 * 0.044715) * square)
    )
    inner = (gelu * up).astype(bf16)
    grad_gate = (grad_inner * up * gelu_grad).astype(bf16)
    grad_up = (grad_inner * gelu).astype(bf16)
    for k, part in enumerate((grad_gate, grad_up, inner)):
        packet_ref[k] = part
    for k, lanes in enumerate(sides):
        total_ref[:, lanes] = total_ref[:, lanes] + dot_on(inner, downs[k][...], 1, 1)
        grad_ref[:, lanes] = (
            grad_ref[:, lanes]
            + dot_on(grad_gate, gates[k][...], 1, 1)
            + dot_on(grad_up, ups[k][...], 1, 1)
        )

    @pl.when(j == steps - 1)
    def _():
        result_ref[...] = total_ref[...].astype(bf16)
        mid = mid_ref[...]
        scale = lax.rsqrt(jnp.mean(mid * mid, axis=-1, keepdims=True) + norm_eps)
        grad_normed = grad_ref[...]
        gained = grad_normed * gain_ref[...]
        inward = jnp.mean(gained * mid, axis=-1, keepdims=True)
        grad_mid = cot_ref[...].astype(f32) + scale * gained - mid * (scale * scale * scale * inward)
        grad_mid_ref[...] = grad_mid
        branch_ref[...] = grad_mid.astype(bf16)
        grad_context = over_width(branch_ref, outs).T.astype(bf16)
        grad_context_ref[...] = jnp.zeros_like(grad_context_ref)
        for h in range(heads):
            grad_context_ref[h] = grad_context[h * size : (h + 1) * size, :]
        own, other = sides
        half = hidden_ref.shape[1] // 2
        for k, ref in enumerate((normed_ref, cot_ref, branch_ref)):
            left_ref[:, k * half : (k + 1) * half] = ref[:, own]
            other_left_ref[:, k * half : (k + 1) * half] = ref[:, other]


def feed(flipped, hidden, contexts, cot, gain, weights, heads, *after):
    tok, width = hidden.shape
    blocks, size, _ = contexts[0].shape
    micro = len(contexts)
    inner_width = heads * size
    units = (weights[0].shape[1] - inner_width) // 3
    steps = units // feed_chunk
    assert 3 * units % inner_width == 0
    whole = lambda *shape: pl.BlockSpec(shape, lambda j: (0,) * len(shape))
    column = lambda offset: pl.BlockSpec((width // 2, feed_chunk), lambda j: (0, offset + j))
    spot = 3 * units // inner_width
    weight_specs = [pl.BlockSpec((width // 2, inner_width), lambda j: (0, spot))] * 2
    for k in range(3):
        weight_specs += [column(k * steps)] * 2
    return pl.pallas_call(
        functools.partial(feed_kernel, heads, steps, micro),
        grid=(steps,),
        in_specs=[
            pl.BlockSpec(memory_space=pltpu.SMEM),
            whole(tok, width),
            whole(tok, width),
            whole(1, width),
            *[whole(*context.shape) for context in contexts],
            *weight_specs,
        ]
        + [pl.BlockSpec(memory_space=pl.ANY)] * len(after),
        out_specs=[
            whole(tok, width),
            whole(tok, width),
            whole(blocks, size, tok),
            pl.BlockSpec((3, tok, feed_chunk), lambda j: (0, 0, j)),
            whole(tok, blocks * size),
            whole(tok, 3 * (width // 2)),
            whole(tok, 3 * (width // 2)),
        ],
        out_shape=[
            jax.ShapeDtypeStruct((tok, width), bf16),
            jax.ShapeDtypeStruct((tok, width), f32),
            jax.ShapeDtypeStruct((blocks, size, tok), bf16),
            jax.ShapeDtypeStruct((3, tok, units), bf16),
            jax.ShapeDtypeStruct((tok, blocks * size), bf16),
            jax.ShapeDtypeStruct((tok, 3 * (width // 2)), bf16),
            jax.ShapeDtypeStruct((tok, 3 * (width // 2)), bf16),
        ],
        scratch_shapes=[pltpu.VMEM((tok, width), bf16)] * 2 + [pltpu.VMEM((tok, width), f32)] * 3,
        compiler_params=pltpu.CompilerParams(vmem_limit_bytes=vmem_bytes),
        cost_estimate=cost(8),
        name="feed",
    )(flipped, hidden, cot, gain, *contexts, *weights * 4, *after)


def store_tall(ref, parts):
    for m, part in enumerate(parts):
        tok = part.shape[0]
        ref[:, m * tok : (m + 1) * tok] = part.astype(f32).T.astype(bf16)


def weight_grad_kernel(counts, parts, half, *refs):
    j = pl.program_id(0)
    out_ref, tall_ref = refs[-2:]
    lefts, packets, heard = (refs[k * parts : (k + 1) * parts] for k in range(3))
    start = 0
    for k, count in counts:

        @pl.when(j == start)
        def _(k=k):
            store_tall(tall_ref, [ref[:, k * half : (k + 1) * half] for ref in lefts])

        start += count

    def product(rights):
        right = jnp.concatenate([ref[...] for ref in rights], axis=0)
        out_ref[...] = jnp.dot(tall_ref[...], right, preferred_element_type=f32).astype(bf16)

    @pl.when(j < start - counts[-1][1])
    def _():
        product(packets)

    @pl.when(j >= start - counts[-1][1])
    def _():
        product(heard)


def weight_grads(lefts, packets, heard, inner_width, *after):
    tok, half = lefts[0].shape[0], lefts[0].shape[1] // 3
    block = grad_chunk
    units, wide = packets[0].shape[2], heard[0].shape[1]
    steps, more = units // block, wide // block
    counts = [(0, 2 * steps), (1, steps), (2, more)]
    place = lambda j: jnp.minimum(j, 3 * steps - 1)
    return pl.pallas_call(
        functools.partial(weight_grad_kernel, counts, len(lefts), half),
        grid=(3 * steps + more,),
        in_specs=[pl.BlockSpec((tok, 3 * half), lambda j: (0, 0))] * len(lefts)
        + [
            pl.BlockSpec((None, tok, block), lambda j: (place(j) // steps, 0, place(j) % steps))
        ]
        * len(packets)
        + [pl.BlockSpec((tok, block), lambda j: (0, jnp.clip(j - 3 * steps, 0, more - 1)))]
        * len(heard)
        + [pl.BlockSpec(memory_space=pl.ANY)] * len(after),
        out_specs=pl.BlockSpec((half, block), lambda j: (0, j)),
        out_shape=jax.ShapeDtypeStruct((half, 3 * units + inner_width), bf16),
        scratch_shapes=[pltpu.VMEM((half, len(lefts) * tok), bf16)],
        compiler_params=pltpu.CompilerParams(vmem_limit_bytes=vmem_bytes),
        cost_estimate=cost(10),
        name="weight_grads",
    )(*lefts, *packets, *heard, *after)


def project_kernel(
    heads, flipped_ref, matrix_ref, inputs_ref, own_ref, other_ref, after_ref, *refs
):
    micro, tok, width = inputs_ref.shape
    sent, (tokens_ref, normed_ref, gain_a_ref, gain_f_ref, gains_ref) = refs[:micro], refs[micro:]
    inner_width = (own_ref.shape[1] - 128) // 3
    size = inner_width // heads
    sides = side(flipped_ref[0], width // 2)
    for lanes, ref in zip(sides, (own_ref, other_ref)):
        gains_ref[:, lanes] = ref[:, 3 * inner_width :].astype(f32).T[:8]
    gain_a_ref[...] = gains_ref[:1]
    gain_f_ref[...] = gains_ref[1:2]
    hidden = jnp.dot(
        inputs_ref[...].reshape(micro * tok, width), matrix_ref[...], preferred_element_type=f32
    )
    tokens_ref[...] = hidden.astype(bf16).reshape(micro, tok, width)
    normed_ref[...] = rms_norm(hidden, gains_ref[:1]).astype(bf16)
    for ref in sent:
        ref[heads:] = jnp.zeros((ref.shape[0] - heads,) + ref.shape[1:], bf16)
    for k in range(3):
        for half in range(2):
            start = k * inner_width + half * (inner_width // 2)
            own, other = (
                jnp.dot(
                    normed_ref[:, lanes],
                    ref[:, start : start + inner_width // 2],
                    preferred_element_type=f32,
                )
                for lanes, ref in zip(sides, (own_ref, other_ref))
            )
            part = (own + other).T.astype(bf16)
            for h in range(heads // 2):
                for m, ref in enumerate(sent):
                    ref[half * (heads // 2) + h, k * size : (k + 1) * size, :] = part[
                        h * size : (h + 1) * size, m * tok : (m + 1) * tok
                    ]


def project(flipped, matrix, inputs, weights, heads, blocks, after):
    micro, tok, width = inputs.shape
    size = (weights[0].shape[1] - 128) // 3 // heads
    vmem = pl.BlockSpec(memory_space=pltpu.VMEM)
    outs = pl.pallas_call(
        functools.partial(project_kernel, heads),
        in_specs=[
            pl.BlockSpec(memory_space=pltpu.SMEM),
            vmem,
            vmem,
            vmem,
            vmem,
            pl.BlockSpec(memory_space=pl.ANY),
        ],
        out_shape=[jax.ShapeDtypeStruct((blocks, 3 * size, tok), bf16)] * micro
        + [
            jax.ShapeDtypeStruct((micro, tok, width), bf16),
            jax.ShapeDtypeStruct((micro * tok, width), bf16),
            jax.ShapeDtypeStruct((1, width), f32),
            jax.ShapeDtypeStruct((1, width), f32),
        ],
        scratch_shapes=[pltpu.VMEM((8, width), f32)],
        compiler_params=pltpu.CompilerParams(vmem_limit_bytes=few_bytes),
        cost_estimate=cost(3),
        name="project",
    )(flipped, matrix, inputs, *weights, after)
    return outs[:micro], *outs[micro:]


def lined(refs, heads, size, lined_ref):
    tok = refs[0].shape[2]
    for m, ref in enumerate(refs):
        for k in range(3):
            for h in range(heads):
                start = (k * heads + h) * size
                lined_ref[start : start + size, m * tok : (m + 1) * tok] = ref[
                    h, k * size : (k + 1) * size, :
                ]


def input_grad_kernel(heads, micro, *refs):
    flipped_ref, matrix_ref, inputs_ref, own_weights, other_weights, gains_ref = refs[:6]
    mid_ref, *grads = refs[6 : 7 + micro]
    result_ref, input_grad_ref, placed_ref, wide_ref, lined_ref = refs[6 + 1 + micro], *refs[-4:]
    tok, width = inputs_ref.shape[1:]
    inner_width = (own_weights.shape[1] - 128) // 3
    sides = side(flipped_ref[0], width // 2)
    lined(grads, heads, inner_width // heads, lined_ref)
    for ref, rows in zip((own_weights, other_weights), sides):
        wide_ref[rows, :] = jnp.dot(
            ref[:, : 3 * inner_width], lined_ref[...], preferred_element_type=f32
        )
    placed_ref[...] = dot_on(result_ref[...], matrix_ref[...], 1, 1).astype(bf16)
    gain = gains_ref[...]
    for m in range(micro):
        grad = wide_ref[:, m * tok : (m + 1) * tok].T
        hidden = inputs_ref[m].astype(f32)
        scale = lax.rsqrt(jnp.mean(hidden * hidden, axis=-1, keepdims=True) + norm_eps)
        gained = grad * gain
        inward = jnp.mean(gained * hidden, axis=-1, keepdims=True)
        found = mid_ref[m * tok : (m + 1) * tok, :] + scale * gained - hidden * (scale * scale * scale * inward)
        high = found.astype(bf16)
        rest = found - high.astype(f32)
        middle = rest.astype(bf16)
        low = (rest - middle.astype(f32)).astype(bf16)
        input_grad_ref[m] = sum(
            dot_on(part, matrix_ref[...], 1, 1) for part in (low, middle, high)
        )


def input_grads(flipped, matrix, inputs, weights, gains, grads, mid, result, heads, *after):
    micro, tok, width = inputs.shape
    inner_width = (weights[0].shape[1] - 128) // 3
    vmem = pl.BlockSpec(memory_space=pltpu.VMEM)
    return pl.pallas_call(
        functools.partial(input_grad_kernel, heads, micro),
        in_specs=[pl.BlockSpec(memory_space=pltpu.SMEM)]
        + [vmem] * (7 + micro)
        + [pl.BlockSpec(memory_space=pl.ANY)] * len(after),
        out_shape=[
            jax.ShapeDtypeStruct((micro, tok, width), f32),
            jax.ShapeDtypeStruct(result.shape, bf16),
        ],
        scratch_shapes=[
            pltpu.VMEM((width, micro * tok), f32),
            pltpu.VMEM((3 * inner_width, micro * tok), bf16),
        ],
        compiler_params=pltpu.CompilerParams(vmem_limit_bytes=vmem_bytes),
        cost_estimate=cost(6),
        name="input_grads",
    )(flipped, matrix, inputs, *weights, gains, mid, *grads, result, *after)


def front_grad_kernel(heads, parts, half, which, *refs):
    flipped_ref = refs[0]
    lefts, grads = refs[1 : 1 + parts], refs[1 + parts : 1 + 2 * parts]
    out_ref, tall_ref, lined_ref = refs[-3:]
    _, size, tok = grads[0].shape

    @pl.when(pl.program_id(0) == 0)
    def _():
        lanes = side(flipped_ref[0], half)[which]
        for p, ref in enumerate(lefts):
            tall = ref[:, lanes].astype(f32).T.astype(bf16)
            tall_ref[:, p * tok : (p + 1) * tok] = tall

    for p, ref in enumerate(grads):
        lined_ref[:, p * tok : (p + 1) * tok] = ref[:heads].reshape(heads * size, tok)
    out_ref[...] = dot_on(tall_ref[...], lined_ref[...], 1, 1).astype(bf16)


def front_grads(flipped, lefts, grads, inner_width, heads, which):
    tok, width = lefts[0].shape
    parts = len(lefts)
    part = pl.BlockSpec((grads[0].shape[0], inner_width // heads, tok), lambda k: (0, k, 0))
    return pl.pallas_call(
        functools.partial(front_grad_kernel, heads, parts, width // 2, which),
        grid=(3,),
        in_specs=[pl.BlockSpec(memory_space=pltpu.SMEM)]
        + [pl.BlockSpec((tok, width), lambda k: (0, 0))] * parts
        + [part] * parts,
        out_specs=pl.BlockSpec((width // 2, inner_width), lambda k: (0, k)),
        out_shape=jax.ShapeDtypeStruct((width // 2, 3 * inner_width), bf16),
        scratch_shapes=[
            pltpu.VMEM((width // 2, parts * tok), bf16),
            pltpu.VMEM((inner_width, parts * tok), bf16),
        ],
        compiler_params=pltpu.CompilerParams(vmem_limit_bytes=few_bytes),
        cost_estimate=cost(5),
        name="front_grads",
    )(flipped, *lefts, *grads)


def row_of(column):
    share = column.shape[0]
    shape = (share, share)
    spread = lax.broadcasted_iota(jnp.int32, shape, 0) == lax.broadcasted_iota(jnp.int32, shape, 1)
    return jnp.sum(jnp.where(spread, column, 0.0), axis=0, keepdims=True)


def gain_grad_of(weights, grads, gain_ref):
    total = sum(
        jnp.sum(weight[...].astype(f32) * grad[...], axis=1, keepdims=True)
        for weight, grad in zip(weights, grads)
    )
    return row_of(total) / gain_ref[...].astype(f32)


def unpack_back_kernel(sums_ref, gate_ref, up_ref, gain_ref, *refs):
    gate_grad_ref, up_grad_ref, down_grad_ref, out_grad_ref, gain_grad_ref = refs
    units = gate_ref.shape[1]
    for k, ref in enumerate((gate_grad_ref, up_grad_ref, down_grad_ref, out_grad_ref)):
        ref[...] = sums_ref[:, k * units : k * units + ref.shape[1]].astype(f32)
    gain_grad_ref[...] = gain_grad_of((gate_ref, up_ref), (gate_grad_ref, up_grad_ref), gain_ref)


def unpack_back(sums, w_gate, w_up, gain, inner_width):
    share, units = w_gate.shape
    shapes = [(share, units)] * 3 + [(share, inner_width), (1, share)]
    gate, up, down, out, gain_grad = pl.pallas_call(
        unpack_back_kernel,
        out_shape=[jax.ShapeDtypeStruct(shape, f32) for shape in shapes],
        compiler_params=pltpu.CompilerParams(vmem_limit_bytes=few_bytes),
        name="unpack_back",
    )(sums, w_gate, w_up, gain[None, :])
    return gate, up, down.T, out.T, gain_grad[0]


def unpack_front_kernel(parts_ref, query_ref, key_ref, value_ref, gain_ref, after_ref, *refs):
    grads, gain_grad_ref = refs[:3], refs[3]
    width = query_ref.shape[1]
    for k, ref in enumerate(grads):
        part = parts_ref[:, :, k * width : (k + 1) * width].astype(f32)
        ref[...] = jnp.sum(part, axis=0)
    gain_grad_ref[...] = gain_grad_of((query_ref, key_ref, value_ref), grads, gain_ref)


def unpack_front(parts, w_query, w_key, w_value, gain, after):
    share, width = w_query.shape
    vmem = pl.BlockSpec(memory_space=pltpu.VMEM)
    shapes = [(share, width)] * 3 + [(1, share)]
    query, key, value, gain_grad = pl.pallas_call(
        unpack_front_kernel,
        in_specs=[vmem] * 5 + [pl.BlockSpec(memory_space=pl.ANY)],
        out_shape=[jax.ShapeDtypeStruct(shape, f32) for shape in shapes],
        compiler_params=pltpu.CompilerParams(vmem_limit_bytes=few_bytes),
        name="unpack_front",
    )(parts, w_query, w_key, w_value, gain[None, :], after)
    return query, key, value, gain_grad[0]


def body(
    inputs, doc_lengths, attn_gain, w_query, w_key, w_value, w_out, ff_gain,
    w_gate, w_up, w_down, rel_table, cotangent,
):
    micro, _, tok, width = inputs.shape
    inner_width = w_query.shape[1]
    hidden_units = w_gate.shape[1]
    buckets, heads = rel_table.shape
    size = inner_width // heads
    blocks = lax.axis_size("blk")
    rows = lax.axis_size("rows")
    me = lax.axis_index("blk")
    share = w_query.shape[0]
    micros = range(micro)

    flipped = lax.axis_index("rows") if staged(rows, blocks, share) else 0
    flipped = jnp.full((1,), flipped, jnp.int32)
    matrix = stage_matrix(rows, blocks, share)
    head = jnp.minimum(me, heads - 1).astype(jnp.int32).reshape(1)
    table = rel_table.astype(f32).reshape(-1)

    with jax.named_scope("weights"):
        front_full = gather_front(w_query, w_key, w_value, attn_gain, ff_gain)
        back_own = gather_back(jnp.concatenate([w_gate, w_up, w_down.T, w_out.T], axis=1), front_full[0])

    band = bias_tiles(head, table, buckets)
    sent, tokens, normed_a, gain_a, gain_f = project(
        flipped, matrix, inputs[:, 0], front_full, heads, blocks, band
    )
    taken = []
    for m in micros:
        with jax.named_scope("project"):
            part = tie(sent[m], taken[-1]) if m else sent[m]
            taken.append(lax.all_to_all(part, "blk", 0, 0, tiled=True))

    cots = reorder(cotangent[:, 0].reshape(micro * tok, width), matrix)
    kept, contexts, half = [], [], blocks // 4 // subs
    for m in micros:
        given = taken[m], doc_lengths[m, 0], head, table, band, buckets
        outs = [k[0] for k in kept]
        if m:
            outs = attend(*given, 0, half, [], *outs, cots)
            outs = attend(*given, half, None, outs, *contexts)
        else:
            outs = attend(*given, 0, None, [])
        kept.append(outs[1:])
        with jax.named_scope("context"):
            contexts.append(lax.all_to_all(outs[0], "blk", 0, 0, tiled=True))
    with jax.named_scope("weights"):
        back_full = gather_other(back_own, outs[0])

    fits = staged(rows, blocks, share)
    here = micro * tok
    result, grad_mid, grad_context, mine, heard, left, left_other = feed(
        flipped, tokens.reshape(here, width), contexts, cots, gain_f, back_full, heads,
    )
    with jax.named_scope("grad_context"):
        grads = lax.all_to_all(grad_context, "blk", 0, 0, tiled=True)
    if fits:
        with jax.named_scope("packet"):
            packet, near_heard, near_left = (flip(a, "rows", 1) for a in (mine, heard, left_other))

    with jax.named_scope("back_grads"):
        if fits:
            own = weight_grads([left, near_left], [mine, packet], [heard, near_heard], inner_width)
            own = tie(own, grads)
            back_grad = scatter_back(own)
        else:
            own, other = (
                weight_grads([lefts], [mine], [heard], inner_width) for lefts in (left, left_other)
            )
            back_grad = scatter_whole(own, other)
    grad_qkv, found = [], jnp.zeros((1, chunk // 2), f32)
    for m in micros:
        returned, found = attend_back(
            taken[m], grads, *kept[m], buckets, m, m == micro - 1, found, own
        )
        with jax.named_scope("grad_qkv"):
            returned = tie(returned, *grad_qkv) if m else returned
            grad_qkv.append(lax.all_to_all(returned, "blk", 0, 0, tiled=True))

    with jax.named_scope("table"):
        pieces = grad_qkv[-1][:heads, 3 * size : 3 * size + 3, :buckets]
        table_grad = jnp.sum(pieces.astype(f32), axis=1).T
        for bit in bits_of(rows):
            table_grad = table_grad + flip(table_grad, "rows", bit)

    with jax.named_scope("front_grads"):
        normed = [normed_a[m * tok : (m + 1) * tok] for m in micros]
        if fits:
            near_grads = [flip(g, "rows", 1) for g in grad_qkv]
            near_normed = [flip(n, "rows", 1) for n in normed]
            own = front_grads(
                flipped, normed + near_normed, grad_qkv + near_grads, inner_width, heads, 0
            )
            back_grad = scatter_back_end(back_grad, own)
            front_parts = scatter_front(own, share)
        else:
            own, other = (
                front_grads(flipped, normed, grad_qkv, inner_width, heads, which)
                for which in (0, 1)
            )
            front_parts = scatter_whole(own, other)[None]
    input_grad, result = input_grads(
        flipped, matrix, tokens, front_full, gain_a, grad_qkv, grad_mid, result, heads, own
    )
    if fits:
        with jax.named_scope("front_grads"):
            front_parts = scatter_front_end(front_parts, share, input_grad)
    gate_grad, up_grad, down_grad, out_grad, ff_gain_grad = unpack_back(
        back_grad, w_gate, w_up, ff_gain, inner_width
    )
    query_grad, key_grad, value_grad, attn_gain_grad = unpack_front(
        front_parts, w_query, w_key, w_value, attn_gain, gate_grad
    )

    return (
        result.reshape(micro, 1, tok, width),
        input_grad[:, None],
        attn_gain_grad,
        query_grad,
        key_grad,
        value_grad,
        out_grad,
        ff_gain_grad,
        gate_grad,
        up_grad,
        down_grad,
        table_grad,
    )


def solution(mesh):
    weight_rows = P(both, None)
    weight_columns = P(None, both)
    tokens = P(None, "rows", "blk", None)
    in_specs = (
        tokens, P(None, "rows", None), P(both), weight_rows, weight_rows, weight_rows,
        weight_columns, P(both), weight_rows, weight_rows, weight_columns, P(), tokens,
    )
    out_specs = (
        tokens, tokens, P(both), weight_rows, weight_rows, weight_rows,
        weight_columns, P(both), weight_rows, weight_rows, weight_columns, P(),
    )
    return jax.shard_map(body, mesh=mesh, in_specs=in_specs, out_specs=out_specs, check_vma=False)
```
